32 devices in a mesh: head: 4 (over y, core), seq: 8 (over z, x).
Axes of the slice: x: 2, y: 2, z: 4, core: 2. Of those that a mesh axis runs over, the one named last changes fastest.
Arguments:
- query_rows: bfloat16 [1024, 768], P(('seq', 'head')), may hold values from -6 to 6
- key_rows: bfloat16 [1024, 768], P(('seq', 'head')), may hold values from -6 to 6
- value_rows: bfloat16 [1024, 768], P(('seq', 'head')), may hold values from -6 to 6
- gate_rows: bfloat16 [1024, 768], P(('seq', 'head')), may hold values from -1 to 1
- step_rates: float32 [1024, 12], P('seq', 'head'), may hold values from 5e-05 to 0.0005
- first_weight: float32 [12, 64, 256], P('head'), may hold values from -0.75 to 0.75
- first_bias: float32 [12, 256], P('head'), may hold values from -3 to 3
- second_weight: float32 [12, 256, 64], P('head'), may hold values from -0.375 to 0.375
- second_bias: float32 [12, 64], P('head'), may hold values from -3 to 3
- norm_gain: float32 [12, 64], P('head'), may hold values from 0.5 to 1.5
- norm_shift: float32 [12, 64], P('head'), may hold values from -3 to 3
Outputs:
- layer_output: bfloat16 [1024, 768], P(('seq', 'head'))
The draws below stay inside these ranges and needn't reach their ends.
All inputs are finite; a program needn't handle non-finite values.
Results may differ from the reference program's by a relative error of at most 0.0049.
Values may be sent and summed in bfloat16 or wider, within the bound.
No kernel may reach another device: no remote copies, remote signals or barrier semaphores. Data moves between devices by JAX's collectives and lax.ppermute only.
A program may use at most 64 MiB of HBM per device.

```python
import math
import jax
import jax.numpy as jnp
from jax import lax

D_HEAD = 64
INNER = 256
MINI = 64
TOKENS = 1024
HEADS = 12


def block_scale(rng, dims, split, least, largest):
    loudness = 1.0
    for axis_at, shards_of in split:
        steps = jax.random.uniform(jax.random.fold_in(jax.random.fold_in(rng, 6), axis_at), (shards_of,), jnp.float32, least / len(split), largest / len(split))
        loudness = loudness * jnp.repeat(jnp.exp(steps), dims[axis_at] // shards_of).reshape((-1,) + (1,) * (len(dims) - 1 - axis_at))
    return loudness


def bell_draw(own_key, extent, width, bound, pieces=(), held_as=jnp.bfloat16):
    values = width * jax.random.normal(own_key, extent, jnp.float32)
    if pieces:
        values = values * block_scale(own_key, extent, pieces, -0.22, 0.18)
    return jnp.clip(values, -bound, bound).astype(held_as)


def setup_inputs(seed: int = 0) -> dict:
    arg_keys = jax.random.split(jax.random.key(seed), 12)
    return {
        "query_rows": bell_draw(arg_keys[0], (TOKENS, HEADS * D_HEAD), 1.0, 6.0, ((0, 32),)),
        "key_rows": bell_draw(arg_keys[1], (TOKENS, HEADS * D_HEAD), 1.0, 6.0, ((0, 32),)),
        "value_rows": bell_draw(arg_keys[2], (TOKENS, HEADS * D_HEAD), 1.0, 6.0, ((0, 32),)),
        "gate_rows": jnp.clip(jax.random.uniform(arg_keys[3], (TOKENS, HEADS * D_HEAD), jnp.float32, -1.0, 1.0) * block_scale(arg_keys[3], (TOKENS, HEADS * D_HEAD), ((0, 32),), -0.4, 0.0), -1.0, 1.0).astype(jnp.bfloat16),
        "step_rates": jnp.clip(jnp.exp(math.log(0.0005) - 2.3025852 * jax.random.uniform(arg_keys[4], (TOKENS, HEADS), jnp.float32) ** block_scale(arg_keys[4], (TOKENS, HEADS), ((0, 8), (1, 4)), -0.2, 0.2)), 4.999999873689376e-05, 0.0005),
        "first_weight": bell_draw(arg_keys[5], (HEADS, D_HEAD, INNER), D_HEAD ** -0.5, 0.75, ((0, 4),), jnp.float32),
        "first_bias": bell_draw(arg_keys[6], (HEADS, INNER), 0.5, 3.0, ((0, 4),), jnp.float32),
        "second_weight": bell_draw(arg_keys[7], (HEADS, INNER, D_HEAD), INNER ** -0.5, 0.375, ((0, 4),), jnp.float32),
        "second_bias": bell_draw(arg_keys[8], (HEADS, D_HEAD), 0.5, 3.0, ((0, 4),), jnp.float32),
        "norm_gain": jnp.clip(0.5 + 1.0 * jax.random.uniform(arg_keys[9], (HEADS, D_HEAD), jnp.float32) ** block_scale(arg_keys[9], (HEADS, D_HEAD), ((0, 4),), -0.2, 0.2), 0.5, 1.5),
        "norm_shift": bell_draw(arg_keys[10], (HEADS, D_HEAD), 0.5, 3.0, ((0, 4),), jnp.float32),
    }


highest = lax.Precision.HIGHEST
eps_norm = 1e-06
root_factor = 0.7978845608028654
cube_factor = 0.044715

def gelu_tanh(values):
    tanh_term = jnp.tanh(root_factor * (values + cube_factor * values * values * values))
    return 0.5 * values * (1.0 + tanh_term)

def gelu_slope(values):
    tanh_term = jnp.tanh(root_factor * (values + cube_factor * values * values * values))
    return 0.5 * (1.0 + tanh_term) + 0.5 * values * (1.0 - tanh_term * tanh_term) * root_factor * (1.0 + 3.0 * cube_factor * values * values)

def layer_norm(values, gain_row, shift_row):
    centred = values - lax.optimization_barrier(jnp.mean(values, axis=-1, keepdims=True))
    spread = jnp.sqrt(lax.optimization_barrier(jnp.mean(centred * centred, axis=-1, keepdims=True)) + eps_norm)
    normed = centred / spread
    return (normed, spread, gain_row * normed + shift_row)

def mini_step(fast_state, block_data, gain_row, shift_row):
    first_weight, bias_one, second_weight, bias_two = fast_state
    query_block = block_data[0].astype(jnp.float32)
    key_block = block_data[1].astype(jnp.float32)
    value_block = block_data[2].astype(jnp.float32)
    rate_row = block_data[3]
    pre_one = jnp.dot(key_block, first_weight, precision=highest) + bias_one
    act_one = gelu_tanh(pre_one)
    pre_two = jnp.dot(act_one, second_weight, precision=highest) + bias_two
    normed, spread, fitted = layer_norm(pre_two, gain_row, shift_row)
    scaled = gain_row * (fitted - (value_block - key_block))
    grad_two = (scaled - lax.optimization_barrier(jnp.mean(scaled, axis=-1, keepdims=True)) - normed * lax.optimization_barrier(jnp.mean(scaled * normed, axis=-1, keepdims=True))) / spread
    grad_one = jnp.dot(grad_two, second_weight.T, precision=highest) * gelu_slope(pre_one)
    lower_mask = jnp.arange(MINI)[:, None] >= jnp.arange(MINI)[None, :]
    step_matrix = jnp.where(lower_mask, rate_row[None, :], 0.0)
    attend_one = (jnp.dot(query_block, key_block.T, precision=highest) + 1.0) * step_matrix
    dual_one = jnp.dot(query_block, first_weight, precision=highest) + bias_one - jnp.dot(attend_one, grad_one, precision=highest)
    dual_act = gelu_tanh(dual_one)
    attend_two = (jnp.dot(dual_act, act_one.T, precision=highest) + 1.0) * step_matrix
    dual_two = jnp.dot(dual_act, second_weight, precision=highest) + bias_two - jnp.dot(attend_two, grad_two, precision=highest)
    result = layer_norm(dual_two, gain_row, shift_row)[2]
    weighted_one = rate_row[:, None] * grad_one
    weighted_two = rate_row[:, None] * grad_two
    updated = (first_weight - jnp.dot(key_block.T, weighted_one, precision=highest), bias_one - lax.optimization_barrier(jnp.sum(weighted_one, axis=0)), second_weight - jnp.dot(act_one.T, weighted_two, precision=highest), bias_two - lax.optimization_barrier(jnp.sum(weighted_two, axis=0)))
    return (updated, result)

def run_direction(queries, keys_all, values_all, rates_all, first_weight, first_bias, second_weight, second_bias, norm_gain, norm_shift):
    block_count = TOKENS // MINI

    def to_blocks(array_in):
        return array_in.reshape((block_count, MINI) + array_in.shape[1:])

    def one_head(query_head, key_head, value_head, rate_head, weight_one, bias_one, weight_two, bias_two, gain_row, shift_row):

        def advance(fast_state, block_data):
            return mini_step(fast_state, block_data, gain_row, shift_row)
        finished, emitted = lax.scan(advance, (weight_one, bias_one, weight_two, bias_two), (query_head, key_head, value_head, rate_head))
        return emitted
    mapped = jax.vmap(one_head, in_axes=(2, 2, 2, 2, 0, 0, 0, 0, 0, 0), out_axes=2)
    emitted = mapped(to_blocks(queries), to_blocks(keys_all), to_blocks(values_all), to_blocks(rates_all), first_weight, first_bias, second_weight, second_bias, norm_gain, norm_shift)
    return emitted.reshape(TOKENS, HEADS, D_HEAD)

def reference(query_rows, key_rows, value_rows, gate_rows, step_rates, first_weight, first_bias, second_weight, second_bias, norm_gain, norm_shift):

    def by_heads(array_in):
        return array_in.reshape(TOKENS, HEADS, D_HEAD)
    queries = by_heads(query_rows)
    keys_all = by_heads(key_rows)
    values_all = by_heads(value_rows)
    forward = run_direction(queries, keys_all, values_all, step_rates, first_weight, first_bias, second_weight, second_bias, norm_gain, norm_shift)
    backward = run_direction(jnp.flip(queries, 0), jnp.flip(keys_all, 0), jnp.flip(values_all, 0), jnp.flip(step_rates, 0), first_weight, first_bias, second_weight, second_bias, norm_gain, norm_shift)
    backward = jnp.flip(backward, 0)
    summed = (forward + backward).reshape(TOKENS, HEADS * D_HEAD).astype(jnp.bfloat16)
    summed = lax.optimization_barrier(summed)
    return (gate_rows.astype(jnp.float32) * summed.astype(jnp.float32)).astype(jnp.bfloat16)
```

```python
import functools

import jax
import jax.numpy as jnp
from jax import lax
from jax.experimental import pallas as pl
from jax.experimental.pallas import tpu as pltpu
from jax.sharding import PartitionSpec as P

D_HEAD = 64
INNER = 256
MINI = 64
CHUNK = 8

eps_norm = 1e-06
root_factor = 0.7978845608028654
cube_factor = 0.044715
f32 = jnp.float32
bf16 = jnp.bfloat16


def mm(left, right):
    return lax.dot_general(left, right, (((1,), (0,)), ((), ())), preferred_element_type=f32)


def mm_turned(left, right):
    return lax.dot_general(left, right, (((1,), (1,)), ((), ())), preferred_element_type=f32)


def gelu_and_slope(values):
    square = values * values
    tanh_term = jnp.tanh(values * (root_factor + root_factor * cube_factor * square))
    half = 0.5 + 0.5 * tanh_term
    act = values * half
    inner = root_factor + 3.0 * root_factor * cube_factor * square
    return act, half + act * (1.0 - tanh_term) * inner


def gelu(values):
    tanh_term = jnp.tanh(values * (root_factor + root_factor * cube_factor * (values * values)))
    return values * (0.5 + 0.5 * tanh_term)


def row_mean(values):
    return jnp.mean(values, axis=1, keepdims=True)


def run_chunk(first_step, steps, total, backward, qk_ref, v_ref, r_ref, state, gain, shift, emit):
    weight_one, bias_one, second_turned, bias_two = state
    rows = lax.broadcasted_iota(jnp.int32, (MINI, MINI), 0)
    columns = lax.broadcasted_iota(jnp.int32, (MINI, MINI), 1)
    ahead = rows - columns
    seen = jnp.where(backward == 0, ahead, -ahead) >= 0
    gain_square = gain * gain

    def place(step):
        return jnp.where(backward == 0, step, total - 1 - step)

    def load_qk(step):
        return qk_ref[pl.ds(pl.multiple_of(place(step) * MINI, MINI), MINI), :]

    pre_one = None
    qk = load_qk(first_step)
    for local_step in range(steps):
        step = first_step + local_step
        spot = place(step)
        value = v_ref[pl.ds(pl.multiple_of(spot * MINI, MINI), MINI), :].astype(f32)
        rate = r_ref[spot]
        query, key = qk[:, :D_HEAD], qk[:, D_HEAD:]
        if local_step + 1 < steps:
            qk = load_qk(step + 1)
            next_key = qk[:, D_HEAD:]
        else:
            next_key = key
        first_high = weight_one.astype(bf16)
        first_low = (weight_one - first_high.astype(f32)).astype(bf16)
        second_high = second_turned.astype(bf16)
        probes = jnp.concatenate([next_key, query], axis=0)
        plain = mm(
            jnp.concatenate([probes, probes], axis=1),
            jnp.concatenate([first_high, first_low], axis=0),
        ) + bias_one
        if pre_one is None:
            pre_one = mm(key, first_high) + mm(key, first_low) + bias_one
        attend = (mm_turned(probes, key) + 1.0) * rate
        mixer = jnp.concatenate(
            [
                attend[:MINI],
                jnp.where(seen, attend[MINI:], 0.0),
                key.astype(f32).T * rate,
                jnp.broadcast_to(rate, (16, MINI)),
            ],
            axis=0,
        ).astype(bf16)
        act, slope = gelu_and_slope(pre_one)
        act_high = act.astype(bf16)
        centred = mm_turned(act_high, second_high) + bias_two
        pull = gain * (shift - value + key.astype(f32))
        scaled = gain_square * centred
        inverse = lax.rsqrt(row_mean(centred * centred) + eps_norm)
        mean_a = inverse * row_mean(scaled) + row_mean(pull)
        mean_an = inverse * (inverse * row_mean(scaled * centred) + row_mean(pull * centred))
        grad_two = inverse * ((gain_square - mean_an) * (inverse * centred) + (pull - mean_a))
        grad_two_high = grad_two.astype(bf16)
        grad_one = (mm(grad_two_high, second_high) * slope).astype(bf16)
        mixed = mm(mixer, grad_one)
        pre_one = plain[:MINI] - mixed[:MINI]
        dual_act = gelu(plain[MINI:] - mixed[MINI : 2 * MINI])
        dual_high = dual_act.astype(bf16)
        dual_low = (dual_act - dual_high.astype(f32)).astype(bf16)
        attend_two = jnp.where(seen, (mm_turned(dual_high, act_high) + 1.0) * rate, 0.0)
        pulled = mm(
            jnp.concatenate([attend_two, jnp.broadcast_to(rate, (16, MINI))], axis=0).astype(bf16),
            grad_two_high,
        )
        dual_two = (
            mm_turned(dual_high, second_high) + mm_turned(dual_low, second_high) + bias_two - pulled[:MINI]
        )
        spread = lax.rsqrt(row_mean(dual_two * dual_two) + eps_norm)
        emit(spot, gain * (dual_two * spread) + shift)
        weight_one = weight_one - mixed[2 * MINI : 3 * MINI]
        bias_one = bias_one - mixed[3 * MINI : 3 * MINI + 1]
        second_turned = second_turned - mm((grad_two.T * rate).astype(bf16), act_high)
        bias_two = bias_two - pulled[MINI : MINI + 1]
    return weight_one, bias_one, second_turned, bias_two


def run_phase(total, backward, qk_ref, v_ref, r_ref, state_refs, gain, shift, emit):
    def chunk(first_step, steps):
        state = tuple(ref[...] for ref in state_refs)
        state = run_chunk(
            first_step, steps, total, backward, qk_ref, v_ref, r_ref, state, gain, shift, emit
        )
        for ref, part in zip(state_refs, state):
            ref[...] = part

    if total <= CHUNK:
        chunk(0, total)
    else:
        assert total % CHUNK == 0

        def body(index, carry):
            chunk(index * CHUNK, CHUNK)
            return carry

        lax.fori_loop(0, total // CHUNK, body, 0)


def centre_start(w1_ref, c1_ref, w2t_ref, c2_ref):
    second_turned = w2t_ref[...]
    second_turned = second_turned - jnp.mean(second_turned, axis=0, keepdims=True)
    bias_two = c2_ref[...] - row_mean(c2_ref[...])
    return w1_ref[...], c1_ref[...], second_turned, bias_two


def first_phase(total, dir_ref, qk_ref, v_ref, r_ref, w1_ref, c1_ref, w2t_ref, c2_ref, gain_ref, shift_ref,
                y_ref, delta_ref, *state_refs):
    start = centre_start(w1_ref, c1_ref, w2t_ref, c2_ref)
    for ref, part in zip(state_refs, start):
        ref[...] = part

    def emit(spot, rows):
        y_ref[pl.ds(pl.multiple_of(spot * MINI, MINI), MINI), :] = rows

    run_phase(total, dir_ref[0], qk_ref, v_ref, r_ref, state_refs, gain_ref[...], shift_ref[...], emit)
    start = centre_start(w1_ref, c1_ref, w2t_ref, c2_ref)
    ends = [ref[...] - part for ref, part in zip(state_refs, start)]
    delta_ref[0:D_HEAD, :] = ends[0].astype(bf16)
    delta_ref[D_HEAD : 2 * D_HEAD, :] = ends[2].astype(bf16)
    wide = jnp.concatenate([ends[3], jnp.zeros((1, INNER - D_HEAD), f32)], axis=1)
    delta_ref[2 * D_HEAD : 2 * D_HEAD + 16, :] = jnp.concatenate(
        [jnp.broadcast_to(ends[1], (8, INNER)), jnp.broadcast_to(wide, (8, INNER))], axis=0
    ).astype(bf16)


def second_phase(total, dir_ref, qk_ref, v_ref, r_ref, w1_ref, c1_ref, w2t_ref, c2_ref, gain_ref, shift_ref,
                 y_ref, delta_ref, out_ref, *state_refs):
    start = centre_start(w1_ref, c1_ref, w2t_ref, c2_ref)
    biases = delta_ref[2 * D_HEAD : 2 * D_HEAD + 16, :].astype(f32)
    deltas = (
        delta_ref[0:D_HEAD, :].astype(f32),
        biases[0:1],
        delta_ref[D_HEAD : 2 * D_HEAD, :].astype(f32),
        biases[8:9, :D_HEAD],
    )
    for ref, part, delta in zip(state_refs, start, deltas):
        ref[...] = part + delta

    def emit(spot, rows):
        spots = pl.ds(pl.multiple_of(spot * MINI, MINI), MINI)
        out_ref[spots, :] = (y_ref[spots, :] + rows).astype(bf16)

    run_phase(total, dir_ref[0], qk_ref, v_ref, r_ref, state_refs, gain_ref[...], shift_ref[...], emit)


def call_phase(kernel, total, outs, *operands):
    in_vmem = pl.BlockSpec(memory_space=pltpu.VMEM)
    return pl.pallas_call(
        functools.partial(kernel, total),
        out_shape=outs,
        in_specs=[pl.BlockSpec(memory_space=pltpu.SMEM)] + [in_vmem] * (len(operands) - 1),
        out_specs=[in_vmem] * len(outs),
        scratch_shapes=[
            pltpu.VMEM((D_HEAD, INNER), f32),
            pltpu.VMEM((1, INNER), f32),
            pltpu.VMEM((D_HEAD, INNER), f32),
            pltpu.VMEM((1, D_HEAD), f32),
        ],
        compiler_params=pltpu.CompilerParams(vmem_limit_bytes=24 * 2**20),
    )(*operands)


def local(head_size, seq_size, query_rows, key_rows, value_rows, gate_rows, step_rates, first_weight,
          first_bias, second_weight, second_bias, norm_gain, norm_shift):
    rows_here = query_rows.shape[0]
    heads_local = step_rates.shape[1]
    token_block = step_rates.shape[0]
    half_seq = seq_size // 2
    group = half_seq * head_size
    half_tokens = group * rows_here
    total = half_tokens // MINI
    spare = half_seq - heads_local
    seq_at = lax.axis_index("seq")
    half = seq_at // half_seq
    slot = jnp.minimum(seq_at % half_seq, heads_local - 1)
    group_at = lax.axis_index("head")
    halves = [
        [s * head_size + h for s in range(k * half_seq, (k + 1) * half_seq) for h in range(head_size)]
        for k in range(2)
    ]

    def exchange(blocks):
        return lax.all_to_all(blocks, ("seq", "head"), 0, 0, axis_index_groups=halves)

    def by_slot(rows):
        return rows.reshape(rows_here, head_size, heads_local, D_HEAD).transpose(2, 1, 0, 3)

    query, key, value = by_slot(query_rows), by_slot(key_rows), by_slot(value_rows)
    pairs = jnp.concatenate([query, key], axis=3)
    folded = jnp.concatenate([value[:, :, : rows_here // 2], value[:, :, rows_here // 2 :]], axis=3)
    rates = step_rates.T
    high = rates.astype(bf16)
    rest = rates - high.astype(f32)
    middle = rest.astype(bf16)
    low = (rest - middle.astype(f32)).astype(bf16)
    rate_rows = jnp.stack([high, middle, low], axis=1)
    rate_rows = jnp.concatenate([rate_rows, jnp.zeros((heads_local, 5, token_block), bf16)], axis=1)
    rate_rows = jnp.broadcast_to(rate_rows[:, None], (heads_local, head_size, 8, token_block))
    blocks = jnp.concatenate([pairs, folded, rate_rows], axis=2)
    blocks = jnp.concatenate([blocks, jnp.zeros((spare,) + blocks.shape[1:], bf16)], axis=0)
    got = exchange(blocks.reshape((group,) + blocks.shape[2:]))

    qk_all = got[:, :rows_here].reshape(half_tokens, 2 * D_HEAD)
    got_value = got[:, rows_here : rows_here + rows_here // 2]
    v_all = jnp.stack([got_value[..., :D_HEAD], got_value[..., D_HEAD:]], axis=1).reshape(half_tokens, D_HEAD)
    got_rate = got[:, rows_here + rows_here // 2 :].reshape(half_seq, head_size, 8, token_block)
    got_rate = lax.dynamic_index_in_dim(got_rate, group_at, 1, keepdims=False).astype(f32)
    r_all = (got_rate[:, 0] + got_rate[:, 1] + got_rate[:, 2]).reshape(total, 1, MINI)

    def pick(array_in):
        return lax.dynamic_index_in_dim(array_in, slot, 0, keepdims=False)

    params = (
        pick(first_weight),
        pick(first_bias)[None],
        pick(second_weight).T,
        pick(second_bias)[None],
        pick(norm_gain)[None],
        pick(norm_shift)[None],
    )
    ahead = half.astype(jnp.int32).reshape(1)
    y_first, delta = call_phase(
        first_phase,
        total,
        [
            jax.ShapeDtypeStruct((half_tokens, D_HEAD), f32),
            jax.ShapeDtypeStruct((2 * D_HEAD + 16, INNER), bf16),
        ],
        ahead, qk_all, v_all, r_all, *params,
    )
    route = [(s, (s + half_seq) % seq_size) for s in range(seq_size)]
    delta = lax.ppermute(delta, "seq", route)
    (summed,) = call_phase(
        second_phase,
        total,
        [jax.ShapeDtypeStruct((half_tokens, D_HEAD), bf16)],
        1 - ahead, qk_all, v_all, r_all, *params, y_first, delta,
    )
    summed = summed.reshape(group, 2, rows_here // 2, D_HEAD)
    back = exchange(jnp.concatenate([summed[:, 0], summed[:, 1]], axis=2))
    back = back.reshape(half_seq, head_size, rows_here // 2, 2, D_HEAD)[:heads_local]
    back = back.transpose(3, 2, 1, 0, 4).reshape(rows_here, head_size * heads_local * D_HEAD)
    return (gate_rows.astype(f32) * back.astype(f32)).astype(bf16)


def solution(mesh):
    tokens = P(("seq", "head"), None)
    in_specs = (
        tokens,
        tokens,
        tokens,
        tokens,
        P("seq", "head"),
        P("head", None, None),
        P("head", None),
        P("head", None, None),
        P("head", None),
        P("head", None),
        P("head", None),
    )
    body = functools.partial(local, mesh.shape["head"], mesh.shape["seq"])
    return jax.shard_map(body, mesh=mesh, in_specs=in_specs, out_specs=tokens, check_vma=False)
```

```python
import functools

import jax
import jax.numpy as jnp
from jax import lax
from jax.experimental import pallas as pl
from jax.experimental.pallas import tpu as pltpu
from jax.sharding import PartitionSpec as P

D_HEAD = 64
INNER = 256
MINI = 64
CHUNK = 8

eps_norm = 1e-06
root_factor = 0.7978845608028654
cube_factor = 0.044715
f32 = jnp.float32
bf16 = jnp.bfloat16


def mm(left, right):
    return lax.dot_general(left, right, (((1,), (0,)), ((), ())), preferred_element_type=f32)


def mm_turned(left, right):
    return lax.dot_general(left, right, (((1,), (1,)), ((), ())), preferred_element_type=f32)


def gelu_and_slope(values):
    square = values * values
    tanh_term = jnp.tanh(values * (root_factor + root_factor * cube_factor * square))
    half = 0.5 + 0.5 * tanh_term
    act = values * half
    inner = root_factor + 3.0 * root_factor * cube_factor * square
    return act, half + act * (1.0 - tanh_term) * inner


def gelu(values):
    tanh_term = jnp.tanh(values * (root_factor + root_factor * cube_factor * (values * values)))
    return values * (0.5 + 0.5 * tanh_term)


def row_mean(values):
    return jnp.mean(values, axis=1, keepdims=True)


def run_chunk(first_step, steps, total, backward, qk_ref, v_ref, r_ref, state, gain, shift, emit):
    weight_one, bias_one, second_turned, bias_two = state
    rows = lax.broadcasted_iota(jnp.int32, (MINI, MINI), 0)
    columns = lax.broadcasted_iota(jnp.int32, (MINI, MINI), 1)
    ahead = rows - columns
    seen = jnp.where(backward == 0, ahead, -ahead) >= 0
    gain_square = gain * gain

    def place(step):
        return jnp.where(backward == 0, step, total - 1 - step)

    places = [place(first_step + step) for step in range(steps)]
    pairs = [qk_ref[pl.ds(pl.multiple_of(spot * MINI, MINI), MINI), :] for spot in places]
    queries = [pair[:, :D_HEAD] for pair in pairs]
    keys = [pair[:, D_HEAD:] for pair in pairs]
    rates = [r_ref[spot] for spot in places]

    def prepare(step):
        key, rate = keys[step], rates[step]
        value = v_ref[pl.ds(pl.multiple_of(places[step] * MINI, MINI), MINI), :].astype(f32)
        probes = jnp.concatenate([keys[min(step + 1, steps - 1)], queries[step]], axis=0)
        attend = (mm_turned(probes, key) + 1.0) * rate
        mixer = jnp.concatenate(
            [
                attend[:MINI],
                jnp.where(seen, attend[MINI:], 0.0),
                key.astype(f32).T * rate,
                jnp.broadcast_to(rate, (16, MINI)),
            ],
            axis=0,
        ).astype(bf16)
        pull = gain * (shift - value + key.astype(f32))
        return probes, mixer, pull, row_mean(pull), jnp.broadcast_to(rate, (MINI, MINI)).T

    def later_weights(waiting):
        _, dual_high, act_high, _, rate = waiting
        return jnp.where(seen, 0.0, (mm_turned(dual_high, act_high) + 1.0) * rate).astype(bf16)

    def finish(waiting, plain_two, bias_now, unseen):
        spot, _, _, grad_two_high, _ = waiting
        dual_two = plain_two + bias_now + mm(unseen, grad_two_high)
        emit(spot, gain * (dual_two * lax.rsqrt(row_mean(dual_two * dual_two) + eps_norm)) + shift)

    ready = prepare(0)
    first_high = weight_one.astype(bf16)
    first_low = (weight_one - first_high.astype(f32)).astype(bf16)
    act, slope = gelu_and_slope(mm(keys[0], first_high) + mm(keys[0], first_low) + bias_one)
    act_high = act.astype(bf16)
    waiting = None
    for step in range(steps):
        probes, mixer, pull, pull_mean, rate_column = ready
        second_high = second_turned.astype(bf16)
        stacked = act_high if waiting is None else jnp.concatenate([act_high, waiting[1]], axis=0)
        passed = mm_turned(stacked, second_high)
        centred = passed[:MINI] + bias_two
        first_high = weight_one.astype(bf16)
        first_low = (weight_one - first_high.astype(f32)).astype(bf16)
        plain = mm(
            jnp.concatenate([probes, probes], axis=1),
            jnp.concatenate([first_high, first_low], axis=0),
        ) + bias_one
        if waiting is not None:
            unseen = later_weights(waiting)
        if step + 1 < steps:
            ready = prepare(step + 1)
        scaled = gain_square * centred
        inverse = lax.rsqrt(row_mean(centred * centred) + eps_norm)
        mean_a = inverse * row_mean(scaled) + pull_mean
        mean_an = inverse * (inverse * row_mean(scaled * centred) + row_mean(pull * centred))
        grad_two = inverse * ((gain_square - mean_an) * (inverse * centred) + (pull - mean_a))
        grad_two_high = grad_two.astype(bf16)
        grad_one = (mm(grad_two_high, second_high) * slope).astype(bf16)
        if waiting is not None:
            finish(waiting, passed[MINI:], bias_two, unseen)
        weighted = grad_two * rate_column
        second_turned = second_turned - mm(weighted.T.astype(bf16), act_high)
        bias_two = bias_two - jnp.sum(weighted, axis=0, keepdims=True)
        mixed = mm(mixer, grad_one)
        dual_high = gelu(plain[MINI:] - mixed[MINI : 2 * MINI]).astype(bf16)
        waiting = (places[step], dual_high, act_high, grad_two_high, rates[step])
        act, slope = gelu_and_slope(plain[:MINI] - mixed[:MINI])
        act_high = act.astype(bf16)
        weight_one = weight_one - mixed[2 * MINI : 3 * MINI]
        bias_one = bias_one - mixed[3 * MINI : 3 * MINI + 1]
    finish(waiting, mm_turned(waiting[1], second_turned.astype(bf16)), bias_two, later_weights(waiting))
    return weight_one, bias_one, second_turned, bias_two


def run_phase(total, backward, qk_ref, v_ref, r_ref, state_refs, gain, shift, emit):
    def chunk(first_step, steps):
        state = tuple(ref[...] for ref in state_refs)
        state = run_chunk(
            first_step, steps, total, backward, qk_ref, v_ref, r_ref, state, gain, shift, emit
        )
        for ref, part in zip(state_refs, state):
            ref[...] = part

    if total <= CHUNK:
        chunk(0, total)
    else:
        assert total % CHUNK == 0

        def body(index, carry):
            chunk(index * CHUNK, CHUNK)
            return carry

        lax.fori_loop(0, total // CHUNK, body, 0)


def centre_start(w1_ref, c1_ref, w2t_ref, c2_ref):
    second_turned = w2t_ref[...]
    second_turned = second_turned - jnp.mean(second_turned, axis=0, keepdims=True)
    bias_two = c2_ref[...] - row_mean(c2_ref[...])
    return w1_ref[...], c1_ref[...], second_turned, bias_two


def first_phase(total, dir_ref, qk_ref, v_ref, r_ref, w1_ref, c1_ref, w2t_ref, c2_ref, gain_ref, shift_ref,
                y_ref, delta_ref, *state_refs):
    start = centre_start(w1_ref, c1_ref, w2t_ref, c2_ref)
    for ref, part in zip(state_refs, start):
        ref[...] = part

    def emit(spot, rows):
        y_ref[pl.ds(pl.multiple_of(spot * MINI, MINI), MINI), :] = rows

    run_phase(total, dir_ref[0], qk_ref, v_ref, r_ref, state_refs, gain_ref[...], shift_ref[...], emit)
    start = centre_start(w1_ref, c1_ref, w2t_ref, c2_ref)
    ends = [ref[...] - part for ref, part in zip(state_refs, start)]
    delta_ref[0:D_HEAD, :] = ends[0].astype(bf16)
    delta_ref[D_HEAD : 2 * D_HEAD, :] = ends[2].astype(bf16)
    wide = jnp.concatenate([ends[3], jnp.zeros((1, INNER - D_HEAD), f32)], axis=1)
    delta_ref[2 * D_HEAD : 2 * D_HEAD + 16, :] = jnp.concatenate(
        [jnp.broadcast_to(ends[1], (8, INNER)), jnp.broadcast_to(wide, (8, INNER))], axis=0
    ).astype(bf16)


def second_phase(total, dir_ref, qk_ref, v_ref, r_ref, w1_ref, c1_ref, w2t_ref, c2_ref, gain_ref, shift_ref,
                 y_ref, delta_ref, out_ref, *state_refs):
    start = centre_start(w1_ref, c1_ref, w2t_ref, c2_ref)
    biases = delta_ref[2 * D_HEAD : 2 * D_HEAD + 16, :].astype(f32)
    deltas = (
        delta_ref[0:D_HEAD, :].astype(f32),
        biases[0:1],
        delta_ref[D_HEAD : 2 * D_HEAD, :].astype(f32),
        biases[8:9, :D_HEAD],
    )
    for ref, part, delta in zip(state_refs, start, deltas):
        ref[...] = part + delta

    def emit(spot, rows):
        spots = pl.ds(pl.multiple_of(spot * MINI, MINI), MINI)
        out_ref[spots, :] = (y_ref[spots, :] + rows).astype(bf16)

    run_phase(total, dir_ref[0], qk_ref, v_ref, r_ref, state_refs, gain_ref[...], shift_ref[...], emit)


def pack_kernel(head_size, heads_local, query_hbm, key_hbm, value_hbm, rate_hbm, out_ref, query_ref, key_ref,
                value_ref, rate_ref, arrived):
    copies = [
        pltpu.make_async_copy(source, target, arrived.at[at])
        for at, (source, target) in enumerate(
            [(rate_hbm, rate_ref), (query_hbm, query_ref), (key_hbm, key_ref), (value_hbm, value_ref)]
        )
    ]
    for copy in copies:
        copy.start()
    for copy in copies:
        copy.wait()
    fold = query_ref.shape[0] // 2
    row_at = lax.broadcasted_iota(jnp.int32, (8, rate_ref.shape[1]), 0)
    for s in range(out_ref.shape[0] // head_size):
        if s >= heads_local:
            for h in range(head_size):
                out_ref[s * head_size + h] = jnp.zeros(out_ref.shape[1:], bf16)
            continue
        rate = rate_ref[s : s + 1, :]
        high = rate.astype(bf16).astype(f32)
        middle = (rate - high).astype(bf16).astype(f32)
        low = rate - high - middle
        rate_rows = jnp.where(row_at == 0, high, jnp.where(row_at == 1, middle, jnp.where(row_at == 2, low, 0.0)))
        for h in range(head_size):
            at = (h * heads_local + s) * D_HEAD
            value = value_ref[:, at : at + D_HEAD]
            pair = jnp.concatenate([query_ref[:, at : at + D_HEAD], key_ref[:, at : at + D_HEAD]], axis=1)
            folded = jnp.concatenate([value[:fold], value[fold:]], axis=1)
            out_ref[s * head_size + h] = jnp.concatenate([pair, folded, rate_rows.astype(bf16)], axis=0)


def join_kernel(head_size, heads_local, back_ref, gate_ref, out_ref):
    fold = back_ref.shape[1]
    for pair_at in range(head_size * heads_local // 2):
        blocks = []
        for head in (2 * pair_at, 2 * pair_at + 1):
            blocks.append(back_ref[(head % heads_local) * head_size + head // heads_local])
        columns = slice(pair_at * 2 * D_HEAD, (pair_at + 1) * 2 * D_HEAD)
        for part in range(2):
            lanes = slice(part * D_HEAD, (part + 1) * D_HEAD)
            ttt = jnp.concatenate([blocks[0][:, lanes], blocks[1][:, lanes]], axis=1)
            spots = slice(part * fold, (part + 1) * fold)
            gated = gate_ref[spots, columns].astype(f32) * ttt.astype(f32)
            out_ref[spots, columns] = gated.astype(bf16)


def call_phase(kernel, total, outs, *operands):
    in_vmem = pl.BlockSpec(memory_space=pltpu.VMEM)
    return pl.pallas_call(
        functools.partial(kernel, total),
        out_shape=outs,
        in_specs=[pl.BlockSpec(memory_space=pltpu.SMEM)] + [in_vmem] * (len(operands) - 1),
        out_specs=[in_vmem] * len(outs),
        scratch_shapes=[
            pltpu.VMEM((D_HEAD, INNER), f32),
            pltpu.VMEM((1, INNER), f32),
            pltpu.VMEM((D_HEAD, INNER), f32),
            pltpu.VMEM((1, D_HEAD), f32),
        ],
        compiler_params=pltpu.CompilerParams(vmem_limit_bytes=24 * 2**20),
    )(*operands)


def pack_plain(head_size, half_seq, query_rows, key_rows, value_rows, step_rates):
    rows_here = query_rows.shape[0]
    token_block, heads_local = step_rates.shape

    def by_slot(rows):
        return rows.reshape(rows_here, head_size, heads_local, D_HEAD).transpose(2, 1, 0, 3)

    query, key, value = by_slot(query_rows), by_slot(key_rows), by_slot(value_rows)
    pairs = jnp.concatenate([query, key], axis=3)
    folded = jnp.concatenate([value[:, :, : rows_here // 2], value[:, :, rows_here // 2 :]], axis=3)
    rates = step_rates.T
    high = rates.astype(bf16)
    rest = rates - high.astype(f32)
    middle = rest.astype(bf16)
    low = (rest - middle.astype(f32)).astype(bf16)
    rate_rows = jnp.stack([high, middle, low], axis=1)
    rate_rows = jnp.concatenate([rate_rows, jnp.zeros((heads_local, 5, token_block), bf16)], axis=1)
    rate_rows = jnp.broadcast_to(rate_rows[:, None], (heads_local, head_size, 8, token_block))
    blocks = jnp.concatenate([pairs, folded, rate_rows], axis=2)
    spare = jnp.zeros((half_seq - heads_local,) + blocks.shape[1:], bf16)
    blocks = jnp.concatenate([blocks, spare], axis=0)
    return blocks.reshape((half_seq * head_size,) + blocks.shape[2:])


def local(head_size, seq_size, query_rows, key_rows, value_rows, gate_rows, step_rates, first_weight,
          first_bias, second_weight, second_bias, norm_gain, norm_shift):
    rows_here = query_rows.shape[0]
    heads_local = step_rates.shape[1]
    token_block = step_rates.shape[0]
    half_seq = seq_size // 2
    group = half_seq * head_size
    half_tokens = group * rows_here
    total = half_tokens // MINI
    seq_at = lax.axis_index("seq")
    half = seq_at // half_seq
    slot = jnp.minimum(seq_at % half_seq, heads_local - 1)
    group_at = lax.axis_index("head")
    halves = [
        [s * head_size + h for s in range(k * half_seq, (k + 1) * half_seq) for h in range(head_size)]
        for k in range(2)
    ]

    def exchange(blocks):
        return lax.all_to_all(blocks, ("seq", "head"), 0, 0, axis_index_groups=halves)

    block_rows = rows_here + rows_here // 2 + 8
    kernels_fit = rows_here % 32 == 0 and token_block == 2 * D_HEAD and head_size * heads_local % 2 == 0
    if kernels_fit:
        blocks = pl.pallas_call(
            functools.partial(pack_kernel, head_size, heads_local),
            out_shape=jax.ShapeDtypeStruct((group, block_rows, 2 * D_HEAD), bf16),
            in_specs=[pl.BlockSpec(memory_space=pltpu.HBM)] * 4,
            scratch_shapes=[
                pltpu.VMEM(query_rows.shape, bf16),
                pltpu.VMEM(key_rows.shape, bf16),
                pltpu.VMEM(value_rows.shape, bf16),
                pltpu.VMEM((heads_local, token_block), f32),
                pltpu.SemaphoreType.DMA((4,)),
            ],
            compiler_params=pltpu.CompilerParams(vmem_limit_bytes=60 * 2**20),
        )(query_rows, key_rows, value_rows, step_rates.T)
    else:
        blocks = pack_plain(head_size, half_seq, query_rows, key_rows, value_rows, step_rates)
    got = exchange(blocks)

    qk_all = got[:, :rows_here].reshape(half_tokens, 2 * D_HEAD)
    got_value = got[:, rows_here : rows_here + rows_here // 2]
    v_all = jnp.stack([got_value[..., :D_HEAD], got_value[..., D_HEAD:]], axis=1).reshape(half_tokens, D_HEAD)
    got_rate = got[:, rows_here + rows_here // 2 :].reshape(half_seq, head_size, 8, token_block)
    got_rate = lax.dynamic_index_in_dim(got_rate, group_at, 1, keepdims=False).astype(f32)
    r_all = (got_rate[:, 0] + got_rate[:, 1] + got_rate[:, 2]).reshape(total, 1, MINI)

    def pick(array_in):
        return lax.dynamic_index_in_dim(array_in, slot, 0, keepdims=False)

    params = (
        pick(first_weight),
        pick(first_bias)[None],
        pick(second_weight).T,
        pick(second_bias)[None],
        pick(norm_gain)[None],
        pick(norm_shift)[None],
    )
    ahead = half.astype(jnp.int32).reshape(1)
    y_first, delta = call_phase(
        first_phase,
        total,
        [
            jax.ShapeDtypeStruct((half_tokens, D_HEAD), f32),
            jax.ShapeDtypeStruct((2 * D_HEAD + 16, INNER), bf16),
        ],
        ahead, qk_all, v_all, r_all, *params,
    )
    route = [(s, (s + half_seq) % seq_size) for s in range(seq_size)]
    delta = lax.ppermute(delta, "seq", route)
    (summed,) = call_phase(
        second_phase,
        total,
        [jax.ShapeDtypeStruct((half_tokens, D_HEAD), bf16)],
        1 - ahead, qk_all, v_all, r_all, *params, y_first, delta,
    )
    summed = summed.reshape(group, 2, rows_here // 2, D_HEAD)
    back = exchange(jnp.concatenate([summed[:, 0], summed[:, 1]], axis=2))
    if kernels_fit:
        return pl.pallas_call(
            functools.partial(join_kernel, head_size, heads_local),
            out_shape=jax.ShapeDtypeStruct(gate_rows.shape, bf16),
            compiler_params=pltpu.CompilerParams(vmem_limit_bytes=8 * 2**20),
        )(back, gate_rows)
    back = back.reshape(half_seq, head_size, rows_here // 2, 2, D_HEAD)[:heads_local]
    back = back.transpose(3, 2, 1, 0, 4).reshape(rows_here, head_size * heads_local * D_HEAD)
    return (gate_rows.astype(f32) * back.astype(f32)).astype(bf16)


def solution(mesh):
    tokens = P(("seq", "head"), None)
    in_specs = (
        tokens,
        tokens,
        tokens,
        tokens,
        P("seq", "head"),
        P("head", None, None),
        P("head", None),
        P("head", None, None),
        P("head", None),
        P("head", None),
        P("head", None),
    )
    body = functools.partial(local, mesh.shape["head"], mesh.shape["seq"])
    return jax.shard_map(body, mesh=mesh, in_specs=in_specs, out_specs=tokens, check_vma=False)
```

```python
import functools

import jax
import jax.numpy as jnp
from jax import lax
from jax.experimental import pallas as pl
from jax.experimental.pallas import tpu as pltpu
from jax.sharding import PartitionSpec as P

D_HEAD = 64
INNER = 256
MINI = 64
CHUNK = 8

eps_norm = 1e-06
root_factor = 0.7978845608028654
cube_factor = 0.044715
f32 = jnp.float32
bf16 = jnp.bfloat16


def mm(left, right):
    return lax.dot_general(left, right, (((1,), (0,)), ((), ())), preferred_element_type=f32)


def mm_turned(left, right):
    return lax.dot_general(left, right, (((1,), (1,)), ((), ())), preferred_element_type=f32)


def gelu_and_slope(values):
    square = values * values
    tanh_term = jnp.tanh(values * (root_factor + root_factor * cube_factor * square))
    half = 0.5 + 0.5 * tanh_term
    act = values * half
    inner = root_factor + 3.0 * root_factor * cube_factor * square
    return act, half + act * (1.0 - tanh_term) * inner


def gelu(values):
    tanh_term = jnp.tanh(values * (root_factor + root_factor * cube_factor * (values * values)))
    return values * (0.5 + 0.5 * tanh_term)


def row_mean(values):
    return jnp.mean(values, axis=1, keepdims=True)


def tokens_of(first_step, steps, total, backward, qk_ref, v_ref, r_ref):
    lower = lax.broadcasted_iota(jnp.int32, (MINI, 2 * D_HEAD), 1) < D_HEAD
    places, pairs, queries, keys, values, rates = [], [], [], [], [], []
    for step in range(first_step, first_step + steps) if isinstance(first_step, int) else range(steps):
        at = step if isinstance(first_step, int) else first_step + step
        spot = jnp.where(backward == 0, at, total - 1 - at)
        spots = pl.ds(pl.multiple_of(spot * MINI, MINI), MINI)
        pair = qk_ref[spots, :]
        turned = jnp.concatenate([pair[:, D_HEAD:], pair[:, :D_HEAD]], axis=1)
        places.append(spot)
        pairs.append(pair)
        queries.append(jnp.where(lower, pair, turned))
        keys.append(jnp.where(lower, turned, pair))
        values.append(v_ref[spots, :])
        rates.append(r_ref[spot])
    return places, pairs, queries, keys, values, rates


def columns_of(gain, shift):
    both = jnp.concatenate([jnp.broadcast_to(gain, (MINI, D_HEAD)), jnp.broadcast_to(shift, (MINI, D_HEAD))], axis=1).T
    return both[:D_HEAD], both[D_HEAD:]


def order_of(backward, shape):
    ahead = lax.broadcasted_iota(jnp.int32, shape, 0) - lax.broadcasted_iota(jnp.int32, shape, 1)
    return jnp.where(backward == 0, ahead, -ahead)


def prepare(one, backward, tokens, gain, shift, columns):
    _, _, queries, keys, values, rates = tokens
    gain_column, shift_column = columns
    steps = len(keys)
    two = min(one + 1, steps - 1)
    lower = lax.broadcasted_iota(jnp.int32, (MINI, 2 * D_HEAD), 1) < D_HEAD
    none = jnp.zeros((MINI, 2 * D_HEAD), bf16)
    seen = order_of(backward, (MINI, MINI)) >= 0
    nexts = [keys[min(step + 1, steps - 1)] for step in (one, two)]
    probes = jnp.concatenate(
        [jnp.where(lower, nexts[0], nexts[1]), jnp.where(lower, queries[one], queries[two])], axis=0
    )
    met = jnp.concatenate([jnp.where(lower, keys[one], none), none, jnp.where(lower, none, keys[two]), none], axis=0)
    attend = mm_turned(probes, met) + 1.0
    made = []
    for at, step in enumerate((one, two)):
        rate = rates[step]
        here = attend[:, 2 * at * MINI : (2 * at + 1) * MINI] * rate
        value, key = values[step].astype(f32), keys[step].astype(f32)
        both = jnp.where(lower, jnp.concatenate([value, value], axis=1), key).T
        value_turned, key_turned = both[:D_HEAD], both[D_HEAD:]
        mixer = jnp.concatenate(
            [
                (-here[:MINI]).astype(bf16),
                jnp.where(seen, -here[MINI:], 0.0).astype(bf16),
                (key_turned * -rate).astype(bf16),
                jnp.broadcast_to(-rate, (16, MINI)).astype(bf16),
            ],
            axis=0,
        )
        plain = jnp.concatenate([nexts[at], queries[step], none, none[:16]], axis=0)
        pull = gain * (shift - value + key[:, :D_HEAD])
        pull_turned = gain_column * (shift_column - value_turned + key_turned)
        pull_row = jnp.mean(pull_turned, axis=0, keepdims=True)
        made.append((plain, mixer, pull, pull_turned, pull_row))
    return made


def finish(waiting, backward, gain, shift, emit):
    count = len(waiting)
    shape = (count * MINI, count * MINI)
    rows, columns = (lax.broadcasted_iota(jnp.int32, shape, dim) // MINI for dim in range(2))
    unseen = jnp.logical_and(rows == columns, order_of(backward, shape) < 0)
    dual, acts, weighted = (jnp.concatenate([one[at] for one in waiting], axis=0) for at in (1, 2, 3))
    hidden = mm(jnp.where(unseen, mm_turned(dual, acts) + 1.0, 0.0).astype(bf16), weighted)
    for at, one in enumerate(waiting):
        dual_two = one[4] + hidden[at * MINI : (at + 1) * MINI]
        spread = lax.rsqrt(row_mean(dual_two * dual_two) + eps_norm)
        emit(one[0], gain * (dual_two * spread) + shift)


def run_chunk(backward, tokens, state, gain, shift, emit, ready=None, keep_last=False):
    weight_one, bias_one, second_turned, bias_two = state
    places, pairs, queries, keys, values, rates = tokens
    steps = len(places)
    gain_square = gain * gain
    columns = columns_of(gain, shift)
    square_column = columns[0] * columns[0]
    blank = jnp.zeros((D_HEAD, INNER), bf16)
    first_high = weight_one.astype(bf16)
    first_low = (weight_one - first_high.astype(f32)).astype(bf16)
    act, slope = gelu_and_slope(
        mm(
            jnp.concatenate([pairs[0], pairs[0]], axis=1),
            jnp.concatenate([blank, first_high, blank, first_low], axis=0),
        )
        + bias_one
    )
    act_high = act.astype(bf16)
    bias_column = jnp.broadcast_to(bias_two, (MINI, D_HEAD)).T
    made = [] if ready is not None else prepare(0, backward, tokens, gain, shift, columns)
    waiting = []
    dual_high = None
    for step in range(steps):
        plain, mixer, pull, pull_turned, pull_row = made[step] if ready is None else ready(step)
        rate = rates[step]
        second_high = second_turned.astype(bf16)
        stacked = act_high if dual_high is None else jnp.concatenate([act_high, dual_high], axis=0)
        passed = mm_turned(stacked, second_high)
        if dual_high is not None:
            waiting[-1] = waiting[-1] + (passed[MINI:] + bias_two,)
        centred = passed[:MINI] + bias_two
        scaled = gain_square * centred
        back = mm(jnp.concatenate([part.astype(bf16) for part in (pull, centred, scaled)], axis=0), second_high)
        first_high = weight_one.astype(bf16)
        first_low = (weight_one - first_high.astype(f32)).astype(bf16)
        inverse = lax.rsqrt(row_mean(centred * centred) + eps_norm)
        mean_an = inverse * (inverse * row_mean(scaled * centred) + row_mean(pull * centred))
        grad_one = inverse * (inverse * (back[2 * MINI :] - mean_an * back[MINI : 2 * MINI]) + back[:MINI]) * slope
        grad_one = grad_one.astype(bf16)
        turned = mm_turned(second_high, act_high) + bias_column
        scaled_turned = square_column * turned
        inverse_row = lax.rsqrt(jnp.mean(turned * turned, axis=0, keepdims=True) + eps_norm)
        mean_a_row = inverse_row * jnp.mean(scaled_turned, axis=0, keepdims=True) + pull_row
        mean_an_row = inverse_row * (
            inverse_row * jnp.mean(scaled_turned * turned, axis=0, keepdims=True)
            + jnp.mean(pull_turned * turned, axis=0, keepdims=True)
        )
        weighted_turned = (rate * inverse_row) * (
            (square_column - mean_an_row) * (inverse_row * turned) + (pull_turned - mean_a_row)
        )
        second_turned = second_turned - mm(weighted_turned.astype(bf16), act_high)
        mixed = mm(
            jnp.concatenate([plain, mixer], axis=1), jnp.concatenate([first_high, first_low, grad_one], axis=0)
        )
        weighted = weighted_turned.T
        bias_column = bias_column - jnp.sum(weighted_turned, axis=1, keepdims=True)
        bias_two = bias_two - jnp.sum(weighted, axis=0, keepdims=True)
        if len(waiting) == 2:
            finish(waiting, backward, gain, shift, emit)
            waiting = []
        if ready is None and step % 2 == 0 and step + 2 < steps:
            made = made + prepare(step + 2, backward, tokens, gain, shift, columns)
        dual_high = gelu(mixed[MINI : 2 * MINI] + bias_one).astype(bf16)
        waiting.append((places[step], dual_high, act_high, weighted.astype(bf16)))
        act, slope = gelu_and_slope(mixed[:MINI] + bias_one)
        act_high = act.astype(bf16)
        weight_one = weight_one + mixed[2 * MINI : 3 * MINI]
        bias_one = bias_one + mixed[3 * MINI : 3 * MINI + 1]
    if not keep_last:
        waiting[-1] = waiting[-1] + (mm_turned(dual_high, second_turned.astype(bf16)) + bias_two,)
        finish(waiting, backward, gain, shift, emit)
    return (weight_one, bias_one, second_turned, bias_two), waiting


def run_chunks(total, backward, qk_ref, v_ref, r_ref, state_refs, gain, shift, emit):
    assert total % CHUNK == 0

    def body(index, carry):
        tokens = tokens_of(index * CHUNK, CHUNK, total, backward, qk_ref, v_ref, r_ref)
        state, _ = run_chunk(backward, tokens, tuple(ref[...] for ref in state_refs), gain, shift, emit)
        for ref, part in zip(state_refs, state):
            ref[...] = part
        return carry

    lax.fori_loop(0, total // CHUNK, body, 0)
    return tuple(ref[...] for ref in state_refs)


def centre_start(w1_ref, c1_ref, w2t_ref, c2_ref):
    second_turned = w2t_ref[...]
    second_turned = second_turned - jnp.mean(second_turned, axis=0, keepdims=True)
    bias_two = c2_ref[...] - row_mean(c2_ref[...])
    return w1_ref[...], c1_ref[...], second_turned, bias_two


def first_phase(total, dir_ref, qk_ref, v_ref, r_ref, w1_ref, c1_ref, w2t_ref, c2_ref, gain_ref, shift_ref, y_ref,
                delta_ref, *refs):
    backward = dir_ref[0]
    gain, shift = gain_ref[...], shift_ref[...]
    start = centre_start(w1_ref, c1_ref, w2t_ref, c2_ref)

    def emit(spot, rows):
        y_ref[pl.ds(pl.multiple_of(spot * MINI, MINI), MINI), :] = rows

    if total <= CHUNK:
        dual_ref, act_ref, weighted_ref, two_ref, second_ref, bias_ref = refs
        tokens = tokens_of(0, total, total, backward, qk_ref, v_ref, r_ref)
        end, waiting = run_chunk(backward, tokens, start, gain, shift, emit, keep_last=True)
        for at, one in enumerate(waiting):
            spots = slice(at * MINI, (at + 1) * MINI)
            dual_ref[spots, :], act_ref[spots, :], weighted_ref[spots, :] = one[1:4]
        two_ref[...] = waiting[0][4]
        second_ref[...] = end[2].astype(bf16)
        bias_ref[...] = end[3]
    else:
        for ref, part in zip(refs, start):
            ref[...] = part
        end = run_chunks(total, backward, qk_ref, v_ref, r_ref, refs, gain, shift, emit)
    start = centre_start(w1_ref, c1_ref, w2t_ref, c2_ref)
    ends = [part - first for part, first in zip(end, start)]
    delta_ref[0:D_HEAD, :] = ends[0].astype(bf16)
    delta_ref[D_HEAD : 2 * D_HEAD, :] = ends[2].astype(bf16)
    wide = jnp.concatenate([ends[3], jnp.zeros((1, INNER - D_HEAD), f32)], axis=1)
    delta_ref[2 * D_HEAD : 2 * D_HEAD + 16, :] = jnp.concatenate(
        [jnp.broadcast_to(ends[1], (8, INNER)), jnp.broadcast_to(wide, (8, INNER))], axis=0
    ).astype(bf16)


def between_phases(total, dir_ref, qk_ref, v_ref, r_ref, gain_ref, shift_ref, dual_ref, act_ref, weighted_ref, two_ref,
                   second_ref, bias_ref, tail_ref, plain_ref, mixer_ref, pull_ref, turned_ref, row_ref):
    gain, shift = gain_ref[...], shift_ref[...]
    backward = 1 - dir_ref[0]
    tokens = tokens_of(0, total, total, backward, qk_ref, v_ref, r_ref)
    columns = columns_of(gain, shift)
    for one in range(0, total, 2):
        for at, made in enumerate(prepare(one, backward, tokens, gain, shift, columns)):
            for ref, part in zip((plain_ref, mixer_ref, pull_ref, turned_ref, row_ref), made):
                ref[one + at] = part
    last_two = mm_turned(dual_ref[MINI:, :], second_ref[...]) + bias_ref[...]
    waiting = []
    for at, plain_two in enumerate((two_ref[...], last_two)):
        spots = slice(at * MINI, (at + 1) * MINI)
        waiting.append((at, dual_ref[spots, :], act_ref[spots, :], weighted_ref[spots, :], plain_two))

    def emit(at, rows):
        tail_ref[at * MINI : (at + 1) * MINI, :] = rows

    finish(waiting, dir_ref[0], gain, shift, emit)


def second_phase(total, dir_ref, qk_ref, v_ref, r_ref, w1_ref, c1_ref, w2t_ref, c2_ref, gain_ref, shift_ref, y_ref,
                 delta_ref, *refs):
    backward = 1 - dir_ref[0]
    gain, shift = gain_ref[...], shift_ref[...]
    biases = delta_ref[2 * D_HEAD : 2 * D_HEAD + 16, :].astype(f32)
    deltas = (
        delta_ref[0:D_HEAD, :].astype(f32),
        biases[0:1],
        delta_ref[D_HEAD : 2 * D_HEAD, :].astype(f32),
        biases[8:9, :D_HEAD],
    )
    start = centre_start(w1_ref, c1_ref, w2t_ref, c2_ref)
    state = tuple(part + delta for part, delta in zip(start, deltas))
    if total <= CHUNK:
        tail_ref, *ready_refs, out_ref = refs
        tokens = tokens_of(0, total, total, backward, qk_ref, v_ref, r_ref)
        done = []

        def emit(spot, rows):
            spots = pl.ds(pl.multiple_of(spot * MINI, MINI), MINI)
            step = len(done)
            done.append(step)
            if step < 2:
                first = tail_ref[(1 - step) * MINI : (2 - step) * MINI, :]
            else:
                first = y_ref[spots, :]
            out_ref[spots, :] = (first + rows).astype(bf16)

        def ready(step):
            return tuple(ref[step] for ref in ready_refs)

        run_chunk(backward, tokens, state, gain, shift, emit, ready)
    else:
        out_ref, *state_refs = refs
        for ref, part in zip(state_refs, state):
            ref[...] = part

        def emit(spot, rows):
            spots = pl.ds(pl.multiple_of(spot * MINI, MINI), MINI)
            out_ref[spots, :] = (y_ref[spots, :] + rows).astype(bf16)

        run_chunks(total, backward, qk_ref, v_ref, r_ref, state_refs, gain, shift, emit)


def pack_kernel(head_size, heads_local, query_hbm, key_hbm, value_hbm, rate_hbm, out_hbm, query_ref, key_ref,
                value_ref, rate_ref, block_ref, arrived, left):
    copies = [
        pltpu.make_async_copy(source, target, arrived.at[at])
        for at, (source, target) in enumerate(
            [(query_hbm, query_ref), (key_hbm, key_ref), (value_hbm, value_ref), (rate_hbm, rate_ref)]
        )
    ]
    for copy in copies:
        copy.start()
    leaving = []

    def leave(s):
        blocks = pl.ds(s * head_size, head_size)
        leaving.append(pltpu.make_async_copy(block_ref.at[blocks], out_hbm.at[blocks], left.at[s]))
        leaving[-1].start()

    for s in range(heads_local, out_hbm.shape[0] // head_size):
        for h in range(head_size):
            block_ref[s * head_size + h] = jnp.zeros(out_hbm.shape[1:], bf16)
        leave(s)
    for copy in copies:
        copy.wait()
    fold = query_ref.shape[0] // 2
    row_at = lax.broadcasted_iota(jnp.int32, (8, rate_ref.shape[1]), 0)
    for s in range(heads_local):
        rate = rate_ref[s : s + 1, :]
        high = rate.astype(bf16).astype(f32)
        middle = (rate - high).astype(bf16).astype(f32)
        low = rate - high - middle
        rate_rows = jnp.where(row_at == 0, high, jnp.where(row_at == 1, middle, jnp.where(row_at == 2, low, 0.0)))
        for h in range(head_size):
            at = (h * heads_local + s) * D_HEAD
            value = value_ref[:, at : at + D_HEAD]
            pair = jnp.concatenate([query_ref[:, at : at + D_HEAD], key_ref[:, at : at + D_HEAD]], axis=1)
            folded = jnp.concatenate([value[:fold], value[fold:]], axis=1)
            block_ref[s * head_size + h] = jnp.concatenate([pair, folded, rate_rows.astype(bf16)], axis=0)
        leave(s)
    for copy in leaving:
        copy.wait()


def join_kernel(head_size, heads_local, back_ref, gate_ref, out_ref):
    fold = back_ref.shape[1]
    for pair_at in range(head_size * heads_local // 2):
        blocks = []
        for head in (2 * pair_at, 2 * pair_at + 1):
            blocks.append(back_ref[(head % heads_local) * head_size + head // heads_local])
        columns = slice(pair_at * 2 * D_HEAD, (pair_at + 1) * 2 * D_HEAD)
        for part in range(2):
            lanes = slice(part * D_HEAD, (part + 1) * D_HEAD)
            ttt = jnp.concatenate([blocks[0][:, lanes], blocks[1][:, lanes]], axis=1)
            spots = slice(part * fold, (part + 1) * fold)
            gated = gate_ref[spots, columns].astype(f32) * ttt.astype(f32)
            out_ref[spots, columns] = gated.astype(bf16)


def call_phase(kernel, outs, keeps_state, *operands):
    in_vmem = pl.BlockSpec(memory_space=pltpu.VMEM)
    state = [(D_HEAD, INNER), (1, INNER), (D_HEAD, INNER), (1, D_HEAD)] if keeps_state else []
    return pl.pallas_call(
        kernel,
        out_shape=outs,
        in_specs=[pl.BlockSpec(memory_space=pltpu.SMEM)] + [in_vmem] * (len(operands) - 1),
        out_specs=[in_vmem] * len(outs),
        scratch_shapes=[pltpu.VMEM(shape, f32) for shape in state],
        compiler_params=pltpu.CompilerParams(vmem_limit_bytes=24 * 2**20),
        cost_estimate=pl.CostEstimate(flops=10**8, bytes_accessed=10**6, transcendentals=10**5),
    )(*operands)


def pack_plain(head_size, half_seq, query_rows, key_rows, value_rows, step_rates):
    rows_here = query_rows.shape[0]
    token_block, heads_local = step_rates.shape

    def by_slot(rows):
        return rows.reshape(rows_here, head_size, heads_local, D_HEAD).transpose(2, 1, 0, 3)

    query, key, value = by_slot(query_rows), by_slot(key_rows), by_slot(value_rows)
    pairs = jnp.concatenate([query, key], axis=3)
    folded = jnp.concatenate([value[:, :, : rows_here // 2], value[:, :, rows_here // 2 :]], axis=3)
    rates = step_rates.T
    high = rates.astype(bf16)
    rest = rates - high.astype(f32)
    middle = rest.astype(bf16)
    low = (rest - middle.astype(f32)).astype(bf16)
    rate_rows = jnp.stack([high, middle, low], axis=1)
    rate_rows = jnp.concatenate([rate_rows, jnp.zeros((heads_local, 5, token_block), bf16)], axis=1)
    rate_rows = jnp.broadcast_to(rate_rows[:, None], (heads_local, head_size, 8, token_block))
    blocks = jnp.concatenate([pairs, folded, rate_rows], axis=2)
    spare = jnp.zeros((half_seq - heads_local,) + blocks.shape[1:], bf16)
    blocks = jnp.concatenate([blocks, spare], axis=0)
    return blocks.reshape((half_seq * head_size,) + blocks.shape[2:])


def local(head_size, seq_size, query_rows, key_rows, value_rows, gate_rows, step_rates, first_weight,
          first_bias, second_weight, second_bias, norm_gain, norm_shift):
    rows_here = query_rows.shape[0]
    heads_local = step_rates.shape[1]
    token_block = step_rates.shape[0]
    half_seq = seq_size // 2
    group = half_seq * head_size
    half_tokens = group * rows_here
    total = half_tokens // MINI
    seq_at = lax.axis_index("seq")
    half = seq_at // half_seq
    slot = jnp.minimum(seq_at % half_seq, heads_local - 1)
    group_at = lax.axis_index("head")
    halves = [
        [s * head_size + h for s in range(k * half_seq, (k + 1) * half_seq) for h in range(head_size)]
        for k in range(2)
    ]

    def exchange(blocks):
        return lax.all_to_all(blocks, ("seq", "head"), 0, 0, axis_index_groups=halves)

    block_rows = rows_here + rows_here // 2 + 8
    kernels_fit = rows_here % 32 == 0 and token_block == 2 * D_HEAD and head_size * heads_local % 2 == 0
    if kernels_fit:
        blocks = pl.pallas_call(
            functools.partial(pack_kernel, head_size, heads_local),
            out_shape=jax.ShapeDtypeStruct((group, block_rows, 2 * D_HEAD), bf16),
            in_specs=[pl.BlockSpec(memory_space=pltpu.HBM)] * 4,
            out_specs=pl.BlockSpec(memory_space=pltpu.HBM),
            scratch_shapes=[
                pltpu.VMEM(query_rows.shape, bf16),
                pltpu.VMEM(key_rows.shape, bf16),
                pltpu.VMEM(value_rows.shape, bf16),
                pltpu.VMEM((heads_local, token_block), f32),
                pltpu.VMEM((group, block_rows, 2 * D_HEAD), bf16),
                pltpu.SemaphoreType.DMA((4,)),
                pltpu.SemaphoreType.DMA((half_seq,)),
            ],
            compiler_params=pltpu.CompilerParams(vmem_limit_bytes=60 * 2**20),
        )(query_rows, key_rows, value_rows, step_rates.T)
    else:
        blocks = pack_plain(head_size, half_seq, query_rows, key_rows, value_rows, step_rates)
    got = exchange(blocks)

    qk_all = got[:, :rows_here].reshape(half_tokens, 2 * D_HEAD)
    got_value = got[:, rows_here : rows_here + rows_here // 2]
    v_all = jnp.stack([got_value[..., :D_HEAD], got_value[..., D_HEAD:]], axis=1).reshape(half_tokens, D_HEAD)
    got_rate = got[:, rows_here + rows_here // 2 :].reshape(half_seq, head_size, 8, token_block)
    got_rate = lax.dynamic_index_in_dim(got_rate, group_at, 1, keepdims=False).astype(f32)
    r_all = (got_rate[:, 0] + got_rate[:, 1] + got_rate[:, 2]).reshape(total, 1, MINI)

    def pick(array_in):
        return lax.dynamic_index_in_dim(array_in, slot, 0, keepdims=False)

    params = (
        pick(first_weight),
        pick(first_bias)[None],
        pick(second_weight).T,
        pick(second_bias)[None],
        pick(norm_gain)[None],
        pick(norm_shift)[None],
    )
    ahead = half.astype(jnp.int32).reshape(1)
    short = total <= CHUNK
    shape = jax.ShapeDtypeStruct
    outs = [shape((half_tokens, D_HEAD), f32), shape((2 * D_HEAD + 16, INNER), bf16)]
    if short:
        outs += [
            shape((2 * MINI, INNER), bf16),
            shape((2 * MINI, INNER), bf16),
            shape((2 * MINI, D_HEAD), bf16),
            shape((MINI, D_HEAD), f32),
            shape((D_HEAD, INNER), bf16),
            shape((1, D_HEAD), f32),
        ]
    tokens = (ahead, qk_all, v_all, r_all)
    y_first, delta, *left = call_phase(functools.partial(first_phase, total), outs, not short, *tokens, *params)
    route = [(s, (s + half_seq) % seq_size) for s in range(seq_size)]
    delta = lax.ppermute(delta, "seq", route)
    extra = []
    if short:
        outs = [
            shape((2 * MINI, D_HEAD), f32),
            shape((total, 3 * MINI + 16, 2 * D_HEAD), bf16),
            shape((total, 3 * MINI + 16, D_HEAD), bf16),
            shape((total, MINI, D_HEAD), f32),
            shape((total, MINI, D_HEAD), f32),
            shape((total, 1, MINI), f32),
        ]
        extra = call_phase(functools.partial(between_phases, total), outs, False, *tokens, *params[4:], *left)
    (summed,) = call_phase(
        functools.partial(second_phase, total),
        [shape((half_tokens, D_HEAD), bf16)],
        not short, *tokens, *params, y_first, delta, *extra,
    )
    summed = summed.reshape(group, 2, rows_here // 2, D_HEAD)
    back = exchange(jnp.concatenate([summed[:, 0], summed[:, 1]], axis=2))
    if kernels_fit:
        return pl.pallas_call(
            functools.partial(join_kernel, head_size, heads_local),
            out_shape=jax.ShapeDtypeStruct(gate_rows.shape, bf16),
            compiler_params=pltpu.CompilerParams(vmem_limit_bytes=8 * 2**20),
        )(back, gate_rows)
    back = back.reshape(half_seq, head_size, rows_here // 2, 2, D_HEAD)[:heads_local]
    back = back.transpose(3, 2, 1, 0, 4).reshape(rows_here, head_size * heads_local * D_HEAD)
    return (gate_rows.astype(f32) * back.astype(f32)).astype(bf16)


def solution(mesh):
    tokens = P(("seq", "head"), None)
    in_specs = (
        tokens,
        tokens,
        tokens,
        tokens,
        P("seq", "head"),
        P("head", None, None),
        P("head", None),
        P("head", None, None),
        P("head", None),
        P("head", None),
        P("head", None),
    )
    body = functools.partial(local, mesh.shape["head"], mesh.shape["seq"])
    return jax.shard_map(body, mesh=mesh, in_specs=in_specs, out_specs=tokens, check_vma=False)
```

```python
import functools

import jax
import jax.numpy as jnp
from jax import lax
from jax.experimental import pallas as pl
from jax.experimental.pallas import tpu as pltpu
from jax.sharding import PartitionSpec as P

D_HEAD = 64
INNER = 256
MINI = 64
CHUNK = 8

eps_norm = 1e-06
root_factor = 0.7978845608028654
cube_factor = 0.044715
f32 = jnp.float32
bf16 = jnp.bfloat16


def mm(left, right):
    return lax.dot_general(left, right, (((1,), (0,)), ((), ())), preferred_element_type=f32)


def mm_turned(left, right):
    return lax.dot_general(left, right, (((1,), (1,)), ((), ())), preferred_element_type=f32)


def gelu_and_slope(values):
    square = values * values
    tanh_term = jnp.tanh(values * (root_factor + root_factor * cube_factor * square))
    half = 0.5 + 0.5 * tanh_term
    act = values * half
    inner = root_factor + 3.0 * root_factor * cube_factor * square
    return act, half + act * (1.0 - tanh_term) * inner


def gelu(values):
    tanh_term = jnp.tanh(values * (root_factor + root_factor * cube_factor * (values * values)))
    return values * (0.5 + 0.5 * tanh_term)


def row_mean(values):
    return jnp.mean(values, axis=1, keepdims=True)


def tokens_of(first_step, steps, total, backward, qk_ref, v_ref, r_ref):
    lower = lax.broadcasted_iota(jnp.int32, (MINI, 2 * D_HEAD), 1) < D_HEAD
    places, pairs, queries, keys, values, rates = [], [], [], [], [], []
    for step in range(first_step, first_step + steps) if isinstance(first_step, int) else range(steps):
        at = step if isinstance(first_step, int) else first_step + step
        spot = jnp.where(backward == 0, at, total - 1 - at)
        spots = pl.ds(pl.multiple_of(spot * MINI, MINI), MINI)
        pair = qk_ref[spots, :]
        turned = jnp.concatenate([pair[:, D_HEAD:], pair[:, :D_HEAD]], axis=1)
        places.append(spot)
        pairs.append(pair)
        queries.append(jnp.where(lower, pair, turned))
        keys.append(jnp.where(lower, turned, pair))
        values.append(v_ref[spots, :])
        rates.append(r_ref[spot])
    return places, pairs, queries, keys, values, rates


def columns_of(gain, shift):
    both = jnp.concatenate([jnp.broadcast_to(gain, (MINI, D_HEAD)), jnp.broadcast_to(shift, (MINI, D_HEAD))], axis=1).T
    return both[:D_HEAD], both[D_HEAD:]


def order_of(backward, shape):
    ahead = lax.broadcasted_iota(jnp.int32, shape, 0) - lax.broadcasted_iota(jnp.int32, shape, 1)
    return jnp.where(backward == 0, ahead, -ahead)


def prepare(one, backward, tokens, gain, shift, columns):
    _, _, queries, keys, values, rates = tokens
    gain_column, shift_column = columns
    steps = len(keys)
    two = min(one + 1, steps - 1)
    lower = lax.broadcasted_iota(jnp.int32, (MINI, 2 * D_HEAD), 1) < D_HEAD
    none = jnp.zeros((MINI, 2 * D_HEAD), bf16)
    seen = order_of(backward, (MINI, MINI)) >= 0
    nexts = [keys[min(step + 1, steps - 1)] for step in (one, two)]
    probes = jnp.concatenate(
        [jnp.where(lower, nexts[0], nexts[1]), jnp.where(lower, queries[one], queries[two])], axis=0
    )
    met = jnp.concatenate([jnp.where(lower, keys[one], none), none, jnp.where(lower, none, keys[two]), none], axis=0)
    attend = mm_turned(probes, met) + 1.0
    made = []
    for at, step in enumerate((one, two)):
        rate = rates[step]
        here = attend[:, 2 * at * MINI : (2 * at + 1) * MINI] * rate
        value, key = values[step].astype(f32), keys[step].astype(f32)
        both = jnp.where(lower, jnp.concatenate([value, value], axis=1), key).T
        value_turned, key_turned = both[:D_HEAD], both[D_HEAD:]
        mixer = jnp.concatenate(
            [
                (-here[:MINI]).astype(bf16),
                jnp.where(seen, -here[MINI:], 0.0).astype(bf16),
                (key_turned * -rate).astype(bf16),
                jnp.broadcast_to(-rate, (16, MINI)).astype(bf16),
            ],
            axis=0,
        )
        plain = jnp.concatenate([nexts[at], queries[step], none, none[:16]], axis=0)
        pull = gain * (shift - value + key[:, :D_HEAD])
        pull_turned = gain_column * (shift_column - value_turned + key_turned)
        pull_row = jnp.mean(pull_turned, axis=0, keepdims=True)
        made.append((plain, mixer, pull, pull_turned, pull_row))
    return made


def finish(waiting, second_high, bias_two, backward, gain, shift, emit):
    count = len(waiting)
    shape = (count * MINI, count * MINI)
    rows, columns = (lax.broadcasted_iota(jnp.int32, shape, dim) // MINI for dim in range(2))
    later = jnp.logical_and(rows == columns, order_of(backward, shape) < 0)
    unseen = jnp.logical_or(rows < columns, later)
    dual, acts, weighted = (jnp.concatenate([one[at] for one in waiting], axis=0) for at in (1, 2, 3))
    hidden = mm(jnp.where(unseen, mm_turned(dual, acts) + 1.0, 0.0).astype(bf16), weighted)
    dual_two = mm_turned(dual, second_high) + bias_two + hidden
    spread = lax.rsqrt(row_mean(dual_two * dual_two) + eps_norm)
    found = gain * (dual_two * spread) + shift
    for at, one in enumerate(waiting):
        emit(one[0], found[at * MINI : (at + 1) * MINI])


def run_chunk(backward, tokens, state, gain, shift, emit, ready=None, keep_last=False):
    weight_one, bias_one, second_turned, bias_two = state
    places, pairs, queries, keys, values, rates = tokens
    steps = len(places)
    gain_square = gain * gain
    columns = columns_of(gain, shift)
    square_column = columns[0] * columns[0]
    blank = jnp.zeros((D_HEAD, INNER), bf16)
    first_high = weight_one.astype(bf16)
    first_low = (weight_one - first_high.astype(f32)).astype(bf16)
    act, slope = gelu_and_slope(
        mm(
            jnp.concatenate([pairs[0], pairs[0]], axis=1),
            jnp.concatenate([blank, first_high, blank, first_low], axis=0),
        )
        + bias_one
    )
    act_high = act.astype(bf16)
    bias_column = jnp.broadcast_to(bias_two, (MINI, D_HEAD)).T
    made = [] if ready is not None else prepare(0, backward, tokens, gain, shift, columns)
    waiting = []
    for step in range(steps):
        plain, mixer, pull, pull_turned, pull_row = made[step] if ready is None else ready(step)
        rate = rates[step]
        second_high = second_turned.astype(bf16)
        centred = mm_turned(act_high, second_high) + bias_two
        turned = mm_turned(second_high, act_high) + bias_column
        bias_before = bias_two
        scaled = gain_square * centred
        both = [part.astype(bf16) for part in (centred, scaled)]
        woven = [part[at : at + 16] for at in range(0, MINI, 16) for part in both]
        back = mm(jnp.concatenate([pull.astype(bf16)] + woven, axis=0), second_high)
        back_plain = jnp.concatenate([back[MINI + at : MINI + at + 16] for at in range(0, 2 * MINI, 32)], axis=0)
        back_scaled = jnp.concatenate([back[MINI + at : MINI + at + 16] for at in range(16, 2 * MINI, 32)], axis=0)
        first_high = weight_one.astype(bf16)
        first_low = (weight_one - first_high.astype(f32)).astype(bf16)
        inverse = lax.rsqrt(row_mean(centred * centred) + eps_norm)
        mean_an = inverse * (inverse * row_mean(scaled * centred) + row_mean(pull * centred))
        front = inverse * slope
        grad_one = (front * inverse) * (back_scaled - mean_an * back_plain) + front * back[:MINI]
        grad_one = grad_one.astype(bf16)
        scaled_turned = square_column * turned
        inverse_row = lax.rsqrt(jnp.mean(turned * turned, axis=0, keepdims=True) + eps_norm)
        mean_a_row = inverse_row * jnp.mean(scaled_turned, axis=0, keepdims=True) + pull_row
        mean_an_row = inverse_row * (
            inverse_row * jnp.mean(scaled_turned * turned, axis=0, keepdims=True)
            + jnp.mean(pull_turned * turned, axis=0, keepdims=True)
        )
        weighted_turned = (rate * inverse_row) * (
            (square_column - mean_an_row) * (inverse_row * turned) + (pull_turned - mean_a_row)
        )
        second_turned = second_turned - mm(weighted_turned.astype(bf16), act_high)
        mixed = mm(
            jnp.concatenate([plain, mixer], axis=1), jnp.concatenate([first_high, first_low, grad_one], axis=0)
        )
        weighted = weighted_turned.T
        bias_column = bias_column - jnp.sum(weighted_turned, axis=1, keepdims=True)
        bias_two = bias_two - jnp.sum(weighted, axis=0, keepdims=True)
        if len(waiting) == 2:
            finish(waiting, second_high, bias_before, backward, gain, shift, emit)
            waiting = []
        if ready is None and step % 2 == 0 and step + 2 < steps:
            made = made + prepare(step + 2, backward, tokens, gain, shift, columns)
        dual_high = gelu(mixed[MINI : 2 * MINI] + bias_one).astype(bf16)
        waiting.append((places[step], dual_high, act_high, weighted.astype(bf16)))
        act, slope = gelu_and_slope(mixed[:MINI] + bias_one)
        act_high = act.astype(bf16)
        weight_one = weight_one + mixed[2 * MINI : 3 * MINI]
        bias_one = bias_one + mixed[3 * MINI : 3 * MINI + 1]
    if not keep_last:
        finish(waiting, second_turned.astype(bf16), bias_two, backward, gain, shift, emit)
    return (weight_one, bias_one, second_turned, bias_two), waiting


def run_chunks(total, backward, qk_ref, v_ref, r_ref, state_refs, gain, shift, emit):
    assert total % CHUNK == 0

    def body(index, carry):
        tokens = tokens_of(index * CHUNK, CHUNK, total, backward, qk_ref, v_ref, r_ref)
        state, _ = run_chunk(backward, tokens, tuple(ref[...] for ref in state_refs), gain, shift, emit)
        for ref, part in zip(state_refs, state):
            ref[...] = part
        return carry

    lax.fori_loop(0, total // CHUNK, body, 0)
    return tuple(ref[...] for ref in state_refs)


def centre_start(w1_ref, c1_ref, w2t_ref, c2_ref):
    second_turned = w2t_ref[...]
    second_turned = second_turned - jnp.mean(second_turned, axis=0, keepdims=True)
    bias_two = c2_ref[...] - row_mean(c2_ref[...])
    return w1_ref[...], c1_ref[...], second_turned, bias_two


def first_phase(total, dir_ref, qk_ref, v_ref, r_ref, w1_ref, c1_ref, w2t_ref, c2_ref, gain_ref, shift_ref, y_ref,
                delta_ref, *refs):
    backward = dir_ref[0]
    gain, shift = gain_ref[...], shift_ref[...]
    start = centre_start(w1_ref, c1_ref, w2t_ref, c2_ref)

    def emit(spot, rows):
        y_ref[pl.ds(pl.multiple_of(spot * MINI, MINI), MINI), :] = rows

    if total <= CHUNK:
        dual_ref, act_ref, weighted_ref, second_ref, bias_ref = refs
        tokens = tokens_of(0, total, total, backward, qk_ref, v_ref, r_ref)
        end, waiting = run_chunk(backward, tokens, start, gain, shift, emit, keep_last=True)
        for at, one in enumerate(waiting):
            spots = slice(at * MINI, (at + 1) * MINI)
            dual_ref[spots, :], act_ref[spots, :], weighted_ref[spots, :] = one[1:4]
        second_ref[...] = end[2].astype(bf16)
        bias_ref[...] = end[3]
    else:
        for ref, part in zip(refs, start):
            ref[...] = part
        end = run_chunks(total, backward, qk_ref, v_ref, r_ref, refs, gain, shift, emit)
    start = centre_start(w1_ref, c1_ref, w2t_ref, c2_ref)
    ends = [part - first for part, first in zip(end, start)]
    delta_ref[0:D_HEAD, :] = ends[0].astype(bf16)
    delta_ref[D_HEAD : 2 * D_HEAD, :] = ends[2].astype(bf16)
    wide = jnp.concatenate([ends[3], jnp.zeros((1, INNER - D_HEAD), f32)], axis=1)
    delta_ref[2 * D_HEAD : 2 * D_HEAD + 16, :] = jnp.concatenate(
        [jnp.broadcast_to(ends[1], (8, INNER)), jnp.broadcast_to(wide, (8, INNER))], axis=0
    ).astype(bf16)


def between_phases(total, dir_ref, qk_ref, v_ref, r_ref, gain_ref, shift_ref, dual_ref, act_ref, weighted_ref,
                   second_ref, bias_ref, tail_ref, plain_ref, mixer_ref, pull_ref, turned_ref, row_ref):
    gain, shift = gain_ref[...], shift_ref[...]
    backward = 1 - dir_ref[0]
    tokens = tokens_of(0, total, total, backward, qk_ref, v_ref, r_ref)
    columns = columns_of(gain, shift)
    for one in range(0, total, 2):
        for at, made in enumerate(prepare(one, backward, tokens, gain, shift, columns)):
            for ref, part in zip((plain_ref, mixer_ref, pull_ref, turned_ref, row_ref), made):
                ref[one + at] = part
    waiting = []
    for at in range(2):
        spots = slice(at * MINI, (at + 1) * MINI)
        waiting.append((at, dual_ref[spots, :], act_ref[spots, :], weighted_ref[spots, :]))

    def emit(at, rows):
        tail_ref[at * MINI : (at + 1) * MINI, :] = rows

    finish(waiting, second_ref[...], bias_ref[...], dir_ref[0], gain, shift, emit)


def second_phase(total, dir_ref, qk_ref, v_ref, r_ref, w1_ref, c1_ref, w2t_ref, c2_ref, gain_ref, shift_ref, y_ref,
                 delta_ref, *refs):
    backward = 1 - dir_ref[0]
    gain, shift = gain_ref[...], shift_ref[...]
    biases = delta_ref[2 * D_HEAD : 2 * D_HEAD + 16, :].astype(f32)
    deltas = (
        delta_ref[0:D_HEAD, :].astype(f32),
        biases[0:1],
        delta_ref[D_HEAD : 2 * D_HEAD, :].astype(f32),
        biases[8:9, :D_HEAD],
    )
    start = centre_start(w1_ref, c1_ref, w2t_ref, c2_ref)
    state = tuple(part + delta for part, delta in zip(start, deltas))
    if total <= CHUNK:
        tail_ref, *ready_refs, out_ref = refs
        tokens = tokens_of(0, total, total, backward, qk_ref, v_ref, r_ref)
        done = []

        def emit(spot, rows):
            spots = pl.ds(pl.multiple_of(spot * MINI, MINI), MINI)
            step = len(done)
            done.append(step)
            if step < 2:
                first = tail_ref[(1 - step) * MINI : (2 - step) * MINI, :]
            else:
                first = y_ref[spots, :]
            out_ref[spots, :] = (first + rows).astype(bf16)

        def ready(step):
            return tuple(ref[step] for ref in ready_refs)

        run_chunk(backward, tokens, state, gain, shift, emit, ready)
    else:
        out_ref, *state_refs = refs
        for ref, part in zip(state_refs, state):
            ref[...] = part

        def emit(spot, rows):
            spots = pl.ds(pl.multiple_of(spot * MINI, MINI), MINI)
            out_ref[spots, :] = (y_ref[spots, :] + rows).astype(bf16)

        run_chunks(total, backward, qk_ref, v_ref, r_ref, state_refs, gain, shift, emit)


def pack_kernel(head_size, heads_local, query_hbm, key_hbm, value_hbm, rate_hbm, out_hbm, query_ref, key_ref,
                value_ref, rate_ref, block_ref, arrived, left):
    copies = [
        pltpu.make_async_copy(source, target, arrived.at[at])
        for at, (source, target) in enumerate(
            [(query_hbm, query_ref), (key_hbm, key_ref), (value_hbm, value_ref), (rate_hbm, rate_ref)]
        )
    ]
    for copy in copies:
        copy.start()
    leaving = []

    def leave(s):
        blocks = pl.ds(s * head_size, head_size)
        leaving.append(pltpu.make_async_copy(block_ref.at[blocks], out_hbm.at[blocks], left.at[s]))
        leaving[-1].start()

    for s in range(heads_local, out_hbm.shape[0] // head_size):
        for h in range(head_size):
            block_ref[s * head_size + h] = jnp.zeros(out_hbm.shape[1:], bf16)
        leave(s)
    for copy in copies:
        copy.wait()
    fold = query_ref.shape[0] // 2
    row_at = lax.broadcasted_iota(jnp.int32, (8, rate_ref.shape[1]), 0)
    for s in range(heads_local):
        rate = rate_ref[s : s + 1, :]
        high = rate.astype(bf16).astype(f32)
        middle = (rate - high).astype(bf16).astype(f32)
        low = rate - high - middle
        rate_rows = jnp.where(row_at == 0, high, jnp.where(row_at == 1, middle, jnp.where(row_at == 2, low, 0.0)))
        for h in range(head_size):
            at = (h * heads_local + s) * D_HEAD
            value = value_ref[:, at : at + D_HEAD]
            pair = jnp.concatenate([query_ref[:, at : at + D_HEAD], key_ref[:, at : at + D_HEAD]], axis=1)
            folded = jnp.concatenate([value[:fold], value[fold:]], axis=1)
            block_ref[s * head_size + h] = jnp.concatenate([pair, folded, rate_rows.astype(bf16)], axis=0)
        leave(s)
    for copy in leaving:
        copy.wait()


def join_kernel(head_size, heads_local, back_ref, gate_ref, out_ref):
    fold = back_ref.shape[1]
    for pair_at in range(head_size * heads_local // 2):
        blocks = []
        for head in (2 * pair_at, 2 * pair_at + 1):
            blocks.append(back_ref[(head % heads_local) * head_size + head // heads_local])
        columns = slice(pair_at * 2 * D_HEAD, (pair_at + 1) * 2 * D_HEAD)
        for part in range(2):
            lanes = slice(part * D_HEAD, (part + 1) * D_HEAD)
            ttt = jnp.concatenate([blocks[0][:, lanes], blocks[1][:, lanes]], axis=1)
            spots = slice(part * fold, (part + 1) * fold)
            gated = gate_ref[spots, columns].astype(f32) * ttt.astype(f32)
            out_ref[spots, columns] = gated.astype(bf16)


def call_phase(kernel, outs, keeps_state, *operands):
    in_vmem = pl.BlockSpec(memory_space=pltpu.VMEM)
    state = [(D_HEAD, INNER), (1, INNER), (D_HEAD, INNER), (1, D_HEAD)] if keeps_state else []
    return pl.pallas_call(
        kernel,
        out_shape=outs,
        in_specs=[pl.BlockSpec(memory_space=pltpu.SMEM)] + [in_vmem] * (len(operands) - 1),
        out_specs=[in_vmem] * len(outs),
        scratch_shapes=[pltpu.VMEM(shape, f32) for shape in state],
        compiler_params=pltpu.CompilerParams(vmem_limit_bytes=24 * 2**20),
        cost_estimate=pl.CostEstimate(flops=10**8, bytes_accessed=10**6, transcendentals=10**5),
    )(*operands)


def pack_plain(head_size, half_seq, query_rows, key_rows, value_rows, step_rates):
    rows_here = query_rows.shape[0]
    token_block, heads_local = step_rates.shape

    def by_slot(rows):
        return rows.reshape(rows_here, head_size, heads_local, D_HEAD).transpose(2, 1, 0, 3)

    query, key, value = by_slot(query_rows), by_slot(key_rows), by_slot(value_rows)
    pairs = jnp.concatenate([query, key], axis=3)
    folded = jnp.concatenate([value[:, :, : rows_here // 2], value[:, :, rows_here // 2 :]], axis=3)
    rates = step_rates.T
    high = rates.astype(bf16)
    rest = rates - high.astype(f32)
    middle = rest.astype(bf16)
    low = (rest - middle.astype(f32)).astype(bf16)
    rate_rows = jnp.stack([high, middle, low], axis=1)
    rate_rows = jnp.concatenate([rate_rows, jnp.zeros((heads_local, 5, token_block), bf16)], axis=1)
    rate_rows = jnp.broadcast_to(rate_rows[:, None], (heads_local, head_size, 8, token_block))
    blocks = jnp.concatenate([pairs, folded, rate_rows], axis=2)
    spare = jnp.zeros((half_seq - heads_local,) + blocks.shape[1:], bf16)
    blocks = jnp.concatenate([blocks, spare], axis=0)
    return blocks.reshape((half_seq * head_size,) + blocks.shape[2:])


def local(head_size, seq_size, query_rows, key_rows, value_rows, gate_rows, step_rates, first_weight,
          first_bias, second_weight, second_bias, norm_gain, norm_shift):
    rows_here = query_rows.shape[0]
    heads_local = step_rates.shape[1]
    token_block = step_rates.shape[0]
    half_seq = seq_size // 2
    group = half_seq * head_size
    half_tokens = group * rows_here
    total = half_tokens // MINI
    seq_at = lax.axis_index("seq")
    half = seq_at // half_seq
    slot = jnp.minimum(seq_at % half_seq, heads_local - 1)
    group_at = lax.axis_index("head")
    halves = [
        [s * head_size + h for s in range(k * half_seq, (k + 1) * half_seq) for h in range(head_size)]
        for k in range(2)
    ]

    def exchange(blocks):
        return lax.all_to_all(blocks, ("seq", "head"), 0, 0, axis_index_groups=halves)

    block_rows = rows_here + rows_here // 2 + 8
    kernels_fit = rows_here % 32 == 0 and token_block == 2 * D_HEAD and head_size * heads_local % 2 == 0
    if kernels_fit:
        blocks = pl.pallas_call(
            functools.partial(pack_kernel, head_size, heads_local),
            out_shape=jax.ShapeDtypeStruct((group, block_rows, 2 * D_HEAD), bf16),
            in_specs=[pl.BlockSpec(memory_space=pltpu.HBM)] * 4,
            out_specs=pl.BlockSpec(memory_space=pltpu.HBM),
            scratch_shapes=[
                pltpu.VMEM(query_rows.shape, bf16),
                pltpu.VMEM(key_rows.shape, bf16),
                pltpu.VMEM(value_rows.shape, bf16),
                pltpu.VMEM((heads_local, token_block), f32),
                pltpu.VMEM((group, block_rows, 2 * D_HEAD), bf16),
                pltpu.SemaphoreType.DMA((4,)),
                pltpu.SemaphoreType.DMA((half_seq,)),
            ],
            compiler_params=pltpu.CompilerParams(vmem_limit_bytes=60 * 2**20),
        )(query_rows, key_rows, value_rows, step_rates.T)
    else:
        blocks = pack_plain(head_size, half_seq, query_rows, key_rows, value_rows, step_rates)
    got = exchange(blocks)

    qk_all = got[:, :rows_here].reshape(half_tokens, 2 * D_HEAD)
    got_value = got[:, rows_here : rows_here + rows_here // 2]
    v_all = jnp.stack([got_value[..., :D_HEAD], got_value[..., D_HEAD:]], axis=1).reshape(half_tokens, D_HEAD)
    got_rate = got[:, rows_here + rows_here // 2 :].reshape(half_seq, head_size, 8, token_block)
    got_rate = lax.dynamic_index_in_dim(got_rate, group_at, 1, keepdims=False).astype(f32)
    r_all = (got_rate[:, 0] + got_rate[:, 1] + got_rate[:, 2]).reshape(total, 1, MINI)

    def pick(array_in):
        return lax.dynamic_index_in_dim(array_in, slot, 0, keepdims=False)

    params = (
        pick(first_weight),
        pick(first_bias)[None],
        pick(second_weight).T,
        pick(second_bias)[None],
        pick(norm_gain)[None],
        pick(norm_shift)[None],
    )
    ahead = half.astype(jnp.int32).reshape(1)
    short = total <= CHUNK
    shape = jax.ShapeDtypeStruct
    outs = [shape((half_tokens, D_HEAD), f32), shape((2 * D_HEAD + 16, INNER), bf16)]
    if short:
        outs += [
            shape((2 * MINI, INNER), bf16),
            shape((2 * MINI, INNER), bf16),
            shape((2 * MINI, D_HEAD), bf16),
            shape((D_HEAD, INNER), bf16),
            shape((1, D_HEAD), f32),
        ]
    tokens = (ahead, qk_all, v_all, r_all)
    y_first, delta, *left = call_phase(functools.partial(first_phase, total), outs, not short, *tokens, *params)
    route = [(s, (s + half_seq) % seq_size) for s in range(seq_size)]
    delta = lax.ppermute(delta, "seq", route)
    extra = []
    if short:
        outs = [
            shape((2 * MINI, D_HEAD), f32),
            shape((total, 3 * MINI + 16, 2 * D_HEAD), bf16),
            shape((total, 3 * MINI + 16, D_HEAD), bf16),
            shape((total, MINI, D_HEAD), f32),
            shape((total, MINI, D_HEAD), f32),
            shape((total, 1, MINI), f32),
        ]
        extra = call_phase(functools.partial(between_phases, total), outs, False, *tokens, *params[4:], *left)
    (summed,) = call_phase(
        functools.partial(second_phase, total),
        [shape((half_tokens, D_HEAD), bf16)],
        not short, *tokens, *params, y_first, delta, *extra,
    )
    summed = summed.reshape(group, 2, rows_here // 2, D_HEAD)
    back = exchange(jnp.concatenate([summed[:, 0], summed[:, 1]], axis=2))
    if kernels_fit:
        return pl.pallas_call(
            functools.partial(join_kernel, head_size, heads_local),
            out_shape=jax.ShapeDtypeStruct(gate_rows.shape, bf16),
            compiler_params=pltpu.CompilerParams(vmem_limit_bytes=8 * 2**20),
        )(back, gate_rows)
    back = back.reshape(half_seq, head_size, rows_here // 2, 2, D_HEAD)[:heads_local]
    back = back.transpose(3, 2, 1, 0, 4).reshape(rows_here, head_size * heads_local * D_HEAD)
    return (gate_rows.astype(f32) * back.astype(f32)).astype(bf16)


def solution(mesh):
    tokens = P(("seq", "head"), None)
    in_specs = (
        tokens,
        tokens,
        tokens,
        tokens,
        P("seq", "head"),
        P("head", None, None),
        P("head", None),
        P("head", None, None),
        P("head", None),
        P("head", None),
        P("head", None),
    )
    body = functools.partial(local, mesh.shape["head"], mesh.shape["seq"])
    return jax.shard_map(body, mesh=mesh, in_specs=in_specs, out_specs=tokens, check_vma=False)
```

```python
import functools

import jax
import jax.numpy as jnp
from jax import lax
from jax.experimental import pallas as pl
from jax.experimental.pallas import tpu as pltpu
from jax.sharding import PartitionSpec as P

D_HEAD = 64
INNER = 256
MINI = 64
CHUNK = 8

eps_norm = 1e-06
root_factor = 0.7978845608028654
cube_factor = 0.044715
f32 = jnp.float32
bf16 = jnp.bfloat16


def mm(left, right):
    return lax.dot_general(left, right, (((1,), (0,)), ((), ())), preferred_element_type=f32)


def mm_turned(left, right):
    return lax.dot_general(left, right, (((1,), (1,)), ((), ())), preferred_element_type=f32)


def gelu_and_slope(values):
    square = values * values
    tanh_term = jnp.tanh(values * (root_factor + root_factor * cube_factor * square))
    half = 0.5 + 0.5 * tanh_term
    act = values * half
    inner = root_factor + 3.0 * root_factor * cube_factor * square
    return act, half + act * (1.0 - tanh_term) * inner


def gelu(values):
    tanh_term = jnp.tanh(values * (root_factor + root_factor * cube_factor * (values * values)))
    return values * (0.5 + 0.5 * tanh_term)


def row_mean(values):
    return jnp.mean(values, axis=1, keepdims=True)


def tokens_of(first_step, steps, total, backward, qk_ref, v_ref, r_ref):
    lower = lax.broadcasted_iota(jnp.int32, (MINI, 2 * D_HEAD), 1) < D_HEAD
    places, pairs, queries, keys, values, rates = [], [], [], [], [], []
    for step in range(first_step, first_step + steps) if isinstance(first_step, int) else range(steps):
        at = step if isinstance(first_step, int) else first_step + step
        spot = jnp.where(backward == 0, at, total - 1 - at)
        spots = pl.ds(pl.multiple_of(spot * MINI, MINI), MINI)
        pair = qk_ref[spots, :]
        turned = jnp.concatenate([pair[:, D_HEAD:], pair[:, :D_HEAD]], axis=1)
        places.append(spot)
        pairs.append(pair)
        queries.append(jnp.where(lower, pair, turned))
        keys.append(jnp.where(lower, turned, pair))
        rate = r_ref[lax.div(spot, 2)]
        rate_turned = jnp.concatenate([rate[:, MINI:], rate[:, :MINI]], axis=1)
        rates.append(jnp.where(lax.rem(spot, 2) == 0, rate, rate_turned)[:, :MINI])
        if v_ref is None:
            continue
        if len(v_ref.shape) == 2:
            value = v_ref[spots, :]
            values.append(jnp.concatenate([value, value], axis=1))
            continue
        halves = []
        for block in range(MINI // (2 * v_ref.shape[1])):
            folded = v_ref[spot * (MINI // (2 * v_ref.shape[1])) + block]
            halves += [folded, jnp.concatenate([folded[:, D_HEAD:], folded[:, :D_HEAD]], axis=1)]
        values.append(jnp.concatenate(halves, axis=0))
    return places, pairs, queries, keys, values, rates


def columns_of(gain, shift):
    both = jnp.concatenate([jnp.broadcast_to(gain, (MINI, D_HEAD)), jnp.broadcast_to(shift, (MINI, D_HEAD))], axis=1).T
    return both[:D_HEAD], both[D_HEAD:]


def order_of(backward, shape):
    ahead = lax.broadcasted_iota(jnp.int32, shape, 0) - lax.broadcasted_iota(jnp.int32, shape, 1)
    return jnp.where(backward == 0, ahead, -ahead)


def prepare(one, backward, tokens, gain, shift, columns):
    _, _, queries, keys, values, rates = tokens
    gain_column, shift_column = columns
    steps = len(keys)
    two = min(one + 1, steps - 1)
    lower = lax.broadcasted_iota(jnp.int32, (MINI, 2 * D_HEAD), 1) < D_HEAD
    none = jnp.zeros((MINI, 2 * D_HEAD), bf16)
    seen = order_of(backward, (MINI, MINI)) >= 0
    nexts = [keys[min(step + 1, steps - 1)] for step in (one, two)]
    probes = jnp.concatenate(
        [jnp.where(lower, nexts[0], nexts[1]), jnp.where(lower, queries[one], queries[two])], axis=0
    )
    met = jnp.concatenate([jnp.where(lower, keys[one], none), none, jnp.where(lower, none, keys[two]), none], axis=0)
    attend = mm_turned(probes, met) + 1.0
    made = []
    for at, step in enumerate((one, two)):
        rate = rates[step]
        here = attend[:, 2 * at * MINI : (2 * at + 1) * MINI] * rate
        value, key = values[step].astype(f32), keys[step].astype(f32)
        both = jnp.where(lower, value, key).T
        value_turned, key_turned = both[:D_HEAD], both[D_HEAD:]
        mixer = jnp.concatenate(
            [
                (-here[:MINI]).astype(bf16),
                jnp.where(seen, -here[MINI:], 0.0).astype(bf16),
                (key_turned * -rate).astype(bf16),
                jnp.broadcast_to(-rate, (16, MINI)).astype(bf16),
            ],
            axis=0,
        )
        plain = jnp.concatenate([nexts[at], queries[step], none, none[:16]], axis=0)
        pull = gain * (shift - value[:, :D_HEAD] + key[:, :D_HEAD])
        pull_turned = gain_column * (shift_column - value_turned + key_turned)
        pull_row = jnp.mean(pull_turned, axis=0, keepdims=True)
        made.append((plain, mixer, pull, pull_turned, pull_row))
    return made


def finish(waiting, second_turned, bias_two, backward, gain, shift, emit):
    count = len(waiting)
    shape = (count * MINI, count * MINI)
    rows, columns = (lax.broadcasted_iota(jnp.int32, shape, dim) // MINI for dim in range(2))
    later = jnp.logical_and(rows == columns, order_of(backward, shape) < 0)
    unseen = jnp.logical_or(rows < columns, later)
    dual, dual_low, acts, weighted = (jnp.concatenate([one[at] for one in waiting], axis=0) for at in (1, 2, 3, 4))
    second_high = second_turned.astype(bf16)
    hidden = mm(jnp.where(unseen, mm_turned(dual, acts) + 1.0, 0.0).astype(bf16), weighted)
    plain = mm_turned(jnp.concatenate([dual, dual_low], axis=0), second_high)
    dual_two = plain[: count * MINI] + plain[count * MINI :] + bias_two + hidden
    second_low = (second_turned - second_high.astype(f32)).astype(bf16)
    dual_two = dual_two + mm_turned(dual, second_low)
    spread = lax.rsqrt(row_mean(dual_two * dual_two) + eps_norm)
    found = gain * (dual_two * spread) + shift
    for at, one in enumerate(waiting):
        emit(one[0], found[at * MINI : (at + 1) * MINI])


def run_chunk(backward, tokens, state, gain, shift, emit, ready=None, keep_last=False):
    weight_one, bias_one, second_turned, bias_two = state
    places, pairs, queries, keys, values, rates = tokens
    steps = len(places)
    gain_square = gain * gain
    columns = columns_of(gain, shift)
    square_column = columns[0] * columns[0]
    blank = jnp.zeros((D_HEAD, INNER), bf16)
    first_high = weight_one.astype(bf16)
    first_low = (weight_one - first_high.astype(f32)).astype(bf16)
    act, slope = gelu_and_slope(
        mm(
            jnp.concatenate([pairs[0], pairs[0]], axis=1),
            jnp.concatenate([blank, first_high, blank, first_low], axis=0),
        )
        + bias_one
    )
    act_high = act.astype(bf16)
    bias_column = jnp.broadcast_to(bias_two, (MINI, D_HEAD)).T
    made = [] if ready is not None else prepare(0, backward, tokens, gain, shift, columns)
    waiting = []
    for step in range(steps):
        plain, mixer, pull, pull_turned, pull_row = made[step] if ready is None else ready(step)
        rate = rates[step]
        second_high = second_turned.astype(bf16)
        second_low = (second_turned - second_high.astype(f32)).astype(bf16)
        centred = mm_turned(act_high, second_high) + bias_two
        turned = mm_turned(jnp.concatenate([second_high, second_low], axis=0), act_high)
        turned = turned[:D_HEAD] + turned[D_HEAD:] + bias_column
        second_before, bias_before = second_turned, bias_two
        scaled = gain_square * centred
        both = [part.astype(bf16) for part in (centred, scaled)]
        woven = [part[at : at + 16] for at in range(0, MINI, 16) for part in both]
        back = mm(jnp.concatenate([pull.astype(bf16)] + woven, axis=0), second_high)
        back_plain = jnp.concatenate([back[MINI + at : MINI + at + 16] for at in range(0, 2 * MINI, 32)], axis=0)
        back_scaled = jnp.concatenate([back[MINI + at : MINI + at + 16] for at in range(16, 2 * MINI, 32)], axis=0)
        first_high = weight_one.astype(bf16)
        first_low = (weight_one - first_high.astype(f32)).astype(bf16)
        inverse = lax.rsqrt(row_mean(centred * centred) + eps_norm)
        mean_an = inverse * (inverse * row_mean(scaled * centred) + row_mean(pull * centred))
        front = inverse * slope
        grad_one = (front * inverse) * (back_scaled - mean_an * back_plain) + front * back[:MINI]
        grad_one = grad_one.astype(bf16)
        scaled_turned = square_column * turned
        inverse_row = lax.rsqrt(jnp.mean(turned * turned, axis=0, keepdims=True) + eps_norm)
        mean_a_row = inverse_row * jnp.mean(scaled_turned, axis=0, keepdims=True) + pull_row
        mean_an_row = inverse_row * (
            inverse_row * jnp.mean(scaled_turned * turned, axis=0, keepdims=True)
            + jnp.mean(pull_turned * turned, axis=0, keepdims=True)
        )
        weighted_turned = (rate * inverse_row) * (
            (square_column - mean_an_row) * (inverse_row * turned) + (pull_turned - mean_a_row)
        )
        weighted_high = weighted_turned.astype(bf16)
        weighted_low = (weighted_turned - weighted_high.astype(f32)).astype(bf16)
        change = mm(jnp.concatenate([weighted_high, weighted_low], axis=0), act_high)
        second_turned = second_turned - (change[:D_HEAD] + change[D_HEAD:])
        mixed = mm(
            jnp.concatenate([plain, mixer], axis=1), jnp.concatenate([first_high, first_low, grad_one], axis=0)
        )
        weighted = weighted_turned.T
        bias_column = bias_column - jnp.sum(weighted_turned, axis=1, keepdims=True)
        bias_two = bias_two - jnp.sum(weighted, axis=0, keepdims=True)
        if len(waiting) == 2:
            finish(waiting, second_before, bias_before, backward, gain, shift, emit)
            waiting = []
        if ready is None and step % 2 == 0 and step + 2 < steps:
            made = made + prepare(step + 2, backward, tokens, gain, shift, columns)
        dual = gelu(mixed[MINI : 2 * MINI] + bias_one)
        dual_high = dual.astype(bf16)
        dual_low = (dual - dual_high.astype(f32)).astype(bf16)
        waiting.append((places[step], dual_high, dual_low, act_high, weighted.astype(bf16)))
        act, slope = gelu_and_slope(mixed[:MINI] + bias_one)
        act_high = act.astype(bf16)
        weight_one = weight_one + mixed[2 * MINI : 3 * MINI]
        bias_one = bias_one + mixed[3 * MINI : 3 * MINI + 1]
    if not keep_last:
        finish(waiting, second_turned, bias_two, backward, gain, shift, emit)
    return (weight_one, bias_one, second_turned, bias_two), waiting


def run_chunks(total, backward, qk_ref, v_ref, r_ref, state_refs, gain, shift, emit):
    assert total % CHUNK == 0

    def body(index, carry):
        tokens = tokens_of(index * CHUNK, CHUNK, total, backward, qk_ref, v_ref, r_ref)
        state, _ = run_chunk(backward, tokens, tuple(ref[...] for ref in state_refs), gain, shift, emit)
        for ref, part in zip(state_refs, state):
            ref[...] = part
        return carry

    lax.fori_loop(0, total // CHUNK, body, 0)
    return tuple(ref[...] for ref in state_refs)


def centre_start(w1_ref, c1_ref, w2t_ref, c2_ref):
    second_turned = w2t_ref[...]
    second_turned = second_turned - jnp.mean(second_turned, axis=0, keepdims=True)
    bias_two = c2_ref[...] - row_mean(c2_ref[...])
    return w1_ref[...], c1_ref[...], second_turned, bias_two


def first_phase(total, dir_ref, qk_ref, v_ref, r_ref, w1_ref, c1_ref, w2t_ref, c2_ref, gain_ref, shift_ref, y_ref,
                delta_ref, *refs):
    backward = dir_ref[0]
    gain, shift = gain_ref[...], shift_ref[...]
    start = centre_start(w1_ref, c1_ref, w2t_ref, c2_ref)

    def emit(spot, rows):
        y_ref[pl.ds(pl.multiple_of(spot * MINI, MINI), MINI), :] = rows

    if total <= CHUNK:
        *kept_refs, second_ref, bias_ref = refs
        tokens = tokens_of(0, total, total, backward, qk_ref, v_ref, r_ref)
        end, waiting = run_chunk(backward, tokens, start, gain, shift, emit, keep_last=True)
        for at, one in enumerate(waiting):
            spots = slice(at * MINI, (at + 1) * MINI)
            for ref, part in zip(kept_refs, one[1:]):
                ref[spots, :] = part
        second_ref[...] = end[2]
        bias_ref[...] = end[3]
    else:
        for ref, part in zip(refs, start):
            ref[...] = part
        end = run_chunks(total, backward, qk_ref, v_ref, r_ref, refs, gain, shift, emit)
    start = centre_start(w1_ref, c1_ref, w2t_ref, c2_ref)
    ends = [part - first for part, first in zip(end, start)]
    delta_ref[0:D_HEAD, :] = ends[0].astype(bf16)
    delta_ref[D_HEAD : 2 * D_HEAD, :] = ends[2].astype(bf16)
    wide = jnp.concatenate([ends[3], jnp.zeros((1, INNER - D_HEAD), f32)], axis=1)
    delta_ref[2 * D_HEAD : 2 * D_HEAD + 16, :] = jnp.concatenate(
        [jnp.broadcast_to(ends[1], (8, INNER)), jnp.broadcast_to(wide, (8, INNER))], axis=0
    ).astype(bf16)


def between_phases(total, dir_ref, qk_ref, v_ref, r_ref, gain_ref, shift_ref, dual_ref, low_ref, act_ref, weighted_ref,
                   second_ref, bias_ref, tail_ref, plain_ref, mixer_ref, pull_ref, turned_ref, row_ref):
    gain, shift = gain_ref[...], shift_ref[...]
    backward = 1 - dir_ref[0]
    tokens = tokens_of(0, total, total, backward, qk_ref, v_ref, r_ref)
    columns = columns_of(gain, shift)
    for one in range(0, total, 2):
        for at, made in enumerate(prepare(one, backward, tokens, gain, shift, columns)):
            for ref, part in zip((plain_ref, mixer_ref, pull_ref, turned_ref, row_ref), made):
                ref[one + at] = part
    waiting = []
    for at in range(2):
        spots = slice(at * MINI, (at + 1) * MINI)
        kept = (ref[spots, :] for ref in (dual_ref, low_ref, act_ref, weighted_ref))
        waiting.append((at, *kept))

    def emit(at, rows):
        tail_ref[at * MINI : (at + 1) * MINI, :] = rows

    finish(waiting, second_ref[...], bias_ref[...], dir_ref[0], gain, shift, emit)


def second_phase(total, fold, dir_ref, qk_ref, v_ref, r_ref, w1_ref, c1_ref, w2t_ref, c2_ref, gain_ref, shift_ref, y_ref,
                 delta_ref, *refs):
    backward = 1 - dir_ref[0]
    gain, shift = gain_ref[...], shift_ref[...]
    biases = delta_ref[2 * D_HEAD : 2 * D_HEAD + 16, :].astype(f32)
    deltas = (
        delta_ref[0:D_HEAD, :].astype(f32),
        biases[0:1],
        delta_ref[D_HEAD : 2 * D_HEAD, :].astype(f32),
        biases[8:9, :D_HEAD],
    )
    start = centre_start(w1_ref, c1_ref, w2t_ref, c2_ref)
    state = tuple(part + delta for part, delta in zip(start, deltas))
    if total <= CHUNK:
        tail_ref, *ready_refs, out_ref = refs
        tokens = tokens_of(0, total, total, backward, qk_ref, None, r_ref)
        done = []

        def emit(spot, rows):
            spots = pl.ds(pl.multiple_of(spot * MINI, MINI), MINI)
            step = len(done)
            done.append(step)
            if step < 2:
                first = tail_ref[(1 - step) * MINI : (2 - step) * MINI, :]
            else:
                first = y_ref[spots, :]
            summed = (first + rows).astype(bf16)
            if fold is None:
                out_ref[spots, :] = summed
                return
            for block in range(MINI // (2 * fold)):
                at = block * 2 * fold
                folded = jnp.concatenate([summed[at : at + fold], summed[at + fold : at + 2 * fold]], axis=1)
                out_ref[spot * (MINI // (2 * fold)) + block] = folded

        def ready(step):
            return tuple(ref[step] for ref in ready_refs)

        run_chunk(backward, tokens, state, gain, shift, emit, ready)
    else:
        out_ref, *state_refs = refs
        for ref, part in zip(state_refs, state):
            ref[...] = part

        def emit(spot, rows):
            spots = pl.ds(pl.multiple_of(spot * MINI, MINI), MINI)
            out_ref[spots, :] = (y_ref[spots, :] + rows).astype(bf16)

        run_chunks(total, backward, qk_ref, v_ref, r_ref, state_refs, gain, shift, emit)


def pack_kernel(head_size, heads_local, query_hbm, key_hbm, value_hbm, rate_hbm, out_hbm, query_ref, key_ref,
                value_ref, rate_ref, block_ref, arrived, left):
    copies = [
        pltpu.make_async_copy(source, target, arrived.at[at])
        for at, (source, target) in enumerate(
            [(query_hbm, query_ref), (key_hbm, key_ref), (value_hbm, value_ref), (rate_hbm, rate_ref)]
        )
    ]
    for copy in copies:
        copy.start()
    leaving = []

    def leave(s):
        blocks = pl.ds(s * head_size, head_size)
        leaving.append(pltpu.make_async_copy(block_ref.at[blocks], out_hbm.at[blocks], left.at[s]))
        leaving[-1].start()

    for s in range(heads_local, out_hbm.shape[0] // head_size):
        for h in range(head_size):
            block_ref[s * head_size + h] = jnp.zeros(out_hbm.shape[1:], bf16)
        leave(s)
    for copy in copies:
        copy.wait()
    fold = query_ref.shape[0] // 2
    row_at = lax.broadcasted_iota(jnp.int32, (8, rate_ref.shape[1]), 0)
    for s in range(heads_local):
        rate = rate_ref[s : s + 1, :]
        high = rate.astype(bf16).astype(f32)
        middle = (rate - high).astype(bf16).astype(f32)
        low = rate - high - middle
        rate_rows = jnp.where(row_at == 0, high, jnp.where(row_at == 1, middle, jnp.where(row_at == 2, low, 0.0)))
        for h in range(head_size):
            at = (h * heads_local + s) * D_HEAD
            value = value_ref[:, at : at + D_HEAD]
            pair = jnp.concatenate([query_ref[:, at : at + D_HEAD], key_ref[:, at : at + D_HEAD]], axis=1)
            folded = jnp.concatenate([value[:fold], value[fold:]], axis=1)
            block_ref[s * head_size + h] = jnp.concatenate([pair, folded, rate_rows.astype(bf16)], axis=0)
        leave(s)
    for copy in leaving:
        copy.wait()


def join_kernel(head_size, heads_local, back_ref, gate_ref, out_ref):
    fold = back_ref.shape[1]
    for pair_at in range(head_size * heads_local // 2):
        blocks = []
        for head in (2 * pair_at, 2 * pair_at + 1):
            blocks.append(back_ref[(head % heads_local) * head_size + head // heads_local])
        columns = slice(pair_at * 2 * D_HEAD, (pair_at + 1) * 2 * D_HEAD)
        for part in range(2):
            lanes = slice(part * D_HEAD, (part + 1) * D_HEAD)
            ttt = jnp.concatenate([blocks[0][:, lanes], blocks[1][:, lanes]], axis=1)
            spots = slice(part * fold, (part + 1) * fold)
            gated = gate_ref[spots, columns].astype(f32) * ttt.astype(f32)
            out_ref[spots, columns] = gated.astype(bf16)


def call_phase(kernel, outs, keeps_state, *operands):
    in_vmem = pl.BlockSpec(memory_space=pltpu.VMEM)
    state = [(D_HEAD, INNER), (1, INNER), (D_HEAD, INNER), (1, D_HEAD)] if keeps_state else []
    return pl.pallas_call(
        kernel,
        out_shape=outs,
        in_specs=[pl.BlockSpec(memory_space=pltpu.SMEM)] + [in_vmem] * (len(operands) - 1),
        out_specs=[in_vmem] * len(outs),
        scratch_shapes=[pltpu.VMEM(shape, f32) for shape in state],
        compiler_params=pltpu.CompilerParams(vmem_limit_bytes=24 * 2**20),
        cost_estimate=pl.CostEstimate(flops=10**8, bytes_accessed=10**6, transcendentals=10**5),
    )(*operands)


def pack_plain(head_size, half_seq, query_rows, key_rows, value_rows, step_rates):
    rows_here = query_rows.shape[0]
    token_block, heads_local = step_rates.shape

    def by_slot(rows):
        return rows.reshape(rows_here, head_size, heads_local, D_HEAD).transpose(2, 1, 0, 3)

    query, key, value = by_slot(query_rows), by_slot(key_rows), by_slot(value_rows)
    pairs = jnp.concatenate([query, key], axis=3)
    folded = jnp.concatenate([value[:, :, : rows_here // 2], value[:, :, rows_here // 2 :]], axis=3)
    rates = step_rates.T
    high = rates.astype(bf16)
    rest = rates - high.astype(f32)
    middle = rest.astype(bf16)
    low = (rest - middle.astype(f32)).astype(bf16)
    rate_rows = jnp.stack([high, middle, low], axis=1)
    rate_rows = jnp.concatenate([rate_rows, jnp.zeros((heads_local, 5, token_block), bf16)], axis=1)
    rate_rows = jnp.broadcast_to(rate_rows[:, None], (heads_local, head_size, 8, token_block))
    blocks = jnp.concatenate([pairs, folded, rate_rows], axis=2)
    spare = jnp.zeros((half_seq - heads_local,) + blocks.shape[1:], bf16)
    blocks = jnp.concatenate([blocks, spare], axis=0)
    return blocks.reshape((half_seq * head_size,) + blocks.shape[2:])


def local(head_size, seq_size, query_rows, key_rows, value_rows, gate_rows, step_rates, first_weight,
          first_bias, second_weight, second_bias, norm_gain, norm_shift):
    rows_here = query_rows.shape[0]
    heads_local = step_rates.shape[1]
    token_block = step_rates.shape[0]
    half_seq = seq_size // 2
    group = half_seq * head_size
    half_tokens = group * rows_here
    total = half_tokens // MINI
    seq_at = lax.axis_index("seq")
    half = seq_at // half_seq
    slot = jnp.minimum(seq_at % half_seq, heads_local - 1)
    group_at = lax.axis_index("head")
    halves = [
        [s * head_size + h for s in range(k * half_seq, (k + 1) * half_seq) for h in range(head_size)]
        for k in range(2)
    ]

    def exchange(blocks):
        return lax.all_to_all(blocks, ("seq", "head"), 0, 0, axis_index_groups=halves)

    block_rows = rows_here + rows_here // 2 + 8
    kernels_fit = rows_here % 32 == 0 and token_block == 2 * D_HEAD and head_size * heads_local % 2 == 0
    if kernels_fit:
        blocks = pl.pallas_call(
            functools.partial(pack_kernel, head_size, heads_local),
            out_shape=jax.ShapeDtypeStruct((group, block_rows, 2 * D_HEAD), bf16),
            in_specs=[pl.BlockSpec(memory_space=pltpu.HBM)] * 4,
            out_specs=pl.BlockSpec(memory_space=pltpu.HBM),
            scratch_shapes=[
                pltpu.VMEM(query_rows.shape, bf16),
                pltpu.VMEM(key_rows.shape, bf16),
                pltpu.VMEM(value_rows.shape, bf16),
                pltpu.VMEM((heads_local, token_block), f32),
                pltpu.VMEM((group, block_rows, 2 * D_HEAD), bf16),
                pltpu.SemaphoreType.DMA((4,)),
                pltpu.SemaphoreType.DMA((half_seq,)),
            ],
            compiler_params=pltpu.CompilerParams(vmem_limit_bytes=60 * 2**20),
        )(query_rows, key_rows, value_rows, step_rates.T)
    else:
        blocks = pack_plain(head_size, half_seq, query_rows, key_rows, value_rows, step_rates)
    got = exchange(blocks)

    qk_all = got[:, :rows_here].reshape(half_tokens, 2 * D_HEAD)
    got_value = got[:, rows_here : rows_here + rows_here // 2]
    short = total <= CHUNK
    fold = rows_here // 2 if kernels_fit and short else None
    v_all = got_value
    if fold is None:
        v_all = jnp.stack([got_value[..., :D_HEAD], got_value[..., D_HEAD:]], axis=1).reshape(half_tokens, D_HEAD)
    got_rate = got[:, rows_here + rows_here // 2 :].reshape(half_seq, head_size, 8, token_block)
    got_rate = lax.dynamic_index_in_dim(got_rate, group_at, 1, keepdims=False).astype(f32)
    r_all = (got_rate[:, 0] + got_rate[:, 1] + got_rate[:, 2]).reshape(half_seq, 1, 2 * MINI)

    def pick(array_in):
        return lax.dynamic_index_in_dim(array_in, slot, 0, keepdims=False)

    params = (
        pick(first_weight),
        pick(first_bias)[None],
        pick(second_weight).T,
        pick(second_bias)[None],
        pick(norm_gain)[None],
        pick(norm_shift)[None],
    )
    ahead = half.astype(jnp.int32).reshape(1)
    shape = jax.ShapeDtypeStruct
    outs = [shape((half_tokens, D_HEAD), f32), shape((2 * D_HEAD + 16, INNER), bf16)]
    if short:
        outs += [
            shape((2 * MINI, INNER), bf16),
            shape((2 * MINI, INNER), bf16),
            shape((2 * MINI, INNER), bf16),
            shape((2 * MINI, D_HEAD), bf16),
            shape((D_HEAD, INNER), f32),
            shape((1, D_HEAD), f32),
        ]
    tokens = (ahead, qk_all, v_all, r_all)
    y_first, delta, *left = call_phase(functools.partial(first_phase, total), outs, not short, *tokens, *params)
    route = [(s, (s + half_seq) % seq_size) for s in range(seq_size)]
    delta = lax.ppermute(delta, "seq", route)
    extra = []
    if short:
        outs = [
            shape((2 * MINI, D_HEAD), f32),
            shape((total, 3 * MINI + 16, 2 * D_HEAD), bf16),
            shape((total, 3 * MINI + 16, D_HEAD), bf16),
            shape((total, MINI, D_HEAD), f32),
            shape((total, MINI, D_HEAD), f32),
            shape((total, 1, MINI), f32),
        ]
        extra = call_phase(functools.partial(between_phases, total), outs, False, *tokens, *params[4:], *left)
    (summed,) = call_phase(
        functools.partial(second_phase, total, fold),
        [shape((half_tokens, D_HEAD) if fold is None else (group, fold, 2 * D_HEAD), bf16)],
        not short, *tokens, *params, y_first, delta, *extra,
    )
    if fold is None:
        summed = summed.reshape(group, 2, rows_here // 2, D_HEAD)
        summed = jnp.concatenate([summed[:, 0], summed[:, 1]], axis=2)
    back = exchange(summed)
    if kernels_fit:
        return pl.pallas_call(
            functools.partial(join_kernel, head_size, heads_local),
            out_shape=jax.ShapeDtypeStruct(gate_rows.shape, bf16),
            compiler_params=pltpu.CompilerParams(vmem_limit_bytes=8 * 2**20),
        )(back, gate_rows)
    back = back.reshape(half_seq, head_size, rows_here // 2, 2, D_HEAD)[:heads_local]
    back = back.transpose(3, 2, 1, 0, 4).reshape(rows_here, head_size * heads_local * D_HEAD)
    return (gate_rows.astype(f32) * back.astype(f32)).astype(bf16)


def solution(mesh):
    tokens = P(("seq", "head"), None)
    in_specs = (
        tokens,
        tokens,
        tokens,
        tokens,
        P("seq", "head"),
        P("head", None, None),
        P("head", None),
        P("head", None, None),
        P("head", None),
        P("head", None),
        P("head", None),
    )
    body = functools.partial(local, mesh.shape["head"], mesh.shape["seq"])
    return jax.shard_map(body, mesh=mesh, in_specs=in_specs, out_specs=tokens, check_vma=False)
```

```python
import functools

import jax
import jax.numpy as jnp
from jax import lax
from jax.experimental import pallas as pl
from jax.experimental.pallas import tpu as pltpu
from jax.sharding import PartitionSpec as P

D_HEAD = 64
INNER = 256
MINI = 64
CHUNK = 8

eps_norm = 1e-06
root_factor = 0.7978845608028654
cube_factor = 0.044715
f32 = jnp.float32
bf16 = jnp.bfloat16


def mm(left, right):
    return lax.dot_general(left, right, (((1,), (0,)), ((), ())), preferred_element_type=f32)


def mm_turned(left, right):
    return lax.dot_general(left, right, (((1,), (1,)), ((), ())), preferred_element_type=f32)


def gelu_and_slope(values):
    square = values * values
    tanh_term = jnp.tanh(values * (root_factor + root_factor * cube_factor * square))
    half = 0.5 + 0.5 * tanh_term
    act = values * half
    inner = root_factor + 3.0 * root_factor * cube_factor * square
    return act, half + act * (1.0 - tanh_term) * inner


def gelu(values):
    tanh_term = jnp.tanh(values * (root_factor + root_factor * cube_factor * (values * values)))
    return values * (0.5 + 0.5 * tanh_term)


def row_mean(values):
    return jnp.mean(values, axis=1, keepdims=True)


def tokens_of(first_step, steps, total, backward, qk_ref, v_ref, r_ref):
    lower = lax.broadcasted_iota(jnp.int32, (MINI, 2 * D_HEAD), 1) < D_HEAD
    places, pairs, queries, keys, values, rates = [], [], [], [], [], []
    for step in range(first_step, first_step + steps) if isinstance(first_step, int) else range(steps):
        at = step if isinstance(first_step, int) else first_step + step
        spot = jnp.where(backward == 0, at, total - 1 - at)
        spots = pl.ds(pl.multiple_of(spot * MINI, MINI), MINI)
        pair = qk_ref[spots, :]
        turned = jnp.concatenate([pair[:, D_HEAD:], pair[:, :D_HEAD]], axis=1)
        places.append(spot)
        pairs.append(pair)
        queries.append(jnp.where(lower, pair, turned))
        keys.append(jnp.where(lower, turned, pair))
        rate = r_ref[lax.div(spot, 2)]
        rate_turned = jnp.concatenate([rate[:, MINI:], rate[:, :MINI]], axis=1)
        rates.append(jnp.where(lax.rem(spot, 2) == 0, rate, rate_turned)[:, :MINI])
        if v_ref is None:
            continue
        if len(v_ref.shape) == 2:
            value = v_ref[spots, :]
            values.append(jnp.concatenate([value, value], axis=1))
            continue
        halves = []
        for block in range(MINI // (2 * v_ref.shape[1])):
            folded = v_ref[spot * (MINI // (2 * v_ref.shape[1])) + block]
            halves += [folded, jnp.concatenate([folded[:, D_HEAD:], folded[:, :D_HEAD]], axis=1)]
        values.append(jnp.concatenate(halves, axis=0))
    return places, pairs, queries, keys, values, rates


def columns_of(gain, shift):
    both = jnp.concatenate([jnp.broadcast_to(gain, (MINI, D_HEAD)), jnp.broadcast_to(shift, (MINI, D_HEAD))], axis=1).T
    return both[:D_HEAD], both[D_HEAD:]


def order_of(backward, shape):
    ahead = lax.broadcasted_iota(jnp.int32, shape, 0) - lax.broadcasted_iota(jnp.int32, shape, 1)
    return jnp.where(backward == 0, ahead, -ahead)


def prepare(one, backward, tokens, gain, shift, columns):
    _, _, queries, keys, values, rates = tokens
    gain_column, shift_column = columns
    steps = len(keys)
    two = min(one + 1, steps - 1)
    lower = lax.broadcasted_iota(jnp.int32, (MINI, 2 * D_HEAD), 1) < D_HEAD
    none = jnp.zeros((MINI, 2 * D_HEAD), bf16)
    seen = order_of(backward, (MINI, MINI)) >= 0
    nexts = [keys[min(step + 1, steps - 1)] for step in (one, two)]
    probes = jnp.concatenate(
        [jnp.where(lower, nexts[0], nexts[1]), jnp.where(lower, queries[one], queries[two])], axis=0
    )
    met = jnp.concatenate([jnp.where(lower, keys[one], none), none, jnp.where(lower, none, keys[two]), none], axis=0)
    attend = mm_turned(probes, met) + 1.0
    made = []
    for at, step in enumerate((one, two)):
        rate = rates[step]
        here = attend[:, 2 * at * MINI : (2 * at + 1) * MINI] * rate
        value, key = values[step].astype(f32), keys[step].astype(f32)
        both = jnp.where(lower, value, key).T
        value_turned, key_turned = both[:D_HEAD], both[D_HEAD:]
        mixer = jnp.concatenate(
            [
                (-here[:MINI]).astype(bf16),
                jnp.where(seen, -here[MINI:], 0.0).astype(bf16),
                (key_turned * -rate).astype(bf16),
                jnp.broadcast_to(-rate, (16, MINI)).astype(bf16),
            ],
            axis=0,
        )
        plain = jnp.concatenate([nexts[at], queries[step], none, none[:16]], axis=0)
        pull = gain * (shift - value[:, :D_HEAD] + key[:, :D_HEAD])
        pull_turned = gain_column * (shift_column - value_turned + key_turned)
        pull_row = jnp.mean(pull_turned, axis=0, keepdims=True)
        made.append((plain, mixer, pull, pull_turned, pull_row))
    return made


def finish(waiting, second_turned, bias_two, backward, gain, shift, emit):
    count = len(waiting)
    shape = (count * MINI, count * MINI)
    rows, columns = (lax.broadcasted_iota(jnp.int32, shape, dim) // MINI for dim in range(2))
    later = jnp.logical_and(rows == columns, order_of(backward, shape) < 0)
    unseen = jnp.logical_or(rows < columns, later)
    dual, dual_low, acts, weighted = (jnp.concatenate([one[at] for one in waiting], axis=0) for at in (1, 2, 3, 4))
    second_high = second_turned.astype(bf16)
    hidden = mm(jnp.where(unseen, mm_turned(dual, acts) + 1.0, 0.0).astype(bf16), weighted)
    plain = mm_turned(jnp.concatenate([dual, dual_low], axis=0), second_high)
    dual_two = plain[: count * MINI] + plain[count * MINI :] + bias_two + hidden
    second_low = (second_turned - second_high.astype(f32)).astype(bf16)
    dual_two = dual_two + mm_turned(dual, second_low)
    spread = lax.rsqrt(row_mean(dual_two * dual_two) + eps_norm)
    found = gain * (dual_two * spread) + shift
    for at, one in enumerate(waiting):
        emit(one[0], found[at * MINI : (at + 1) * MINI])


def run_chunk(backward, tokens, state, gain, shift, emit, ready=None, keep_last=False):
    weight_one, bias_one, second_turned, bias_two = state
    places, pairs, queries, keys, values, rates = tokens
    steps = len(places)
    gain_square = gain * gain
    columns = columns_of(gain, shift)
    square_column = columns[0] * columns[0]
    blank = jnp.zeros((D_HEAD, INNER), bf16)
    first_high = weight_one.astype(bf16)
    first_low = (weight_one - first_high.astype(f32)).astype(bf16)
    act, slope = gelu_and_slope(
        mm(
            jnp.concatenate([pairs[0], pairs[0]], axis=1),
            jnp.concatenate([blank, first_high, blank, first_low], axis=0),
        )
        + bias_one
    )
    act_high = act.astype(bf16)
    bias_column = jnp.broadcast_to(bias_two, (MINI, D_HEAD)).T
    made = [] if ready is not None else prepare(0, backward, tokens, gain, shift, columns)
    waiting = []
    for step in range(steps):
        plain, mixer, pull, pull_turned, pull_row = made[step] if ready is None else ready(step)
        rate = rates[step]
        second_high = second_turned.astype(bf16)
        second_low = (second_turned - second_high.astype(f32)).astype(bf16)
        centred = mm_turned(act_high, second_high) + bias_two
        turned = mm_turned(jnp.concatenate([second_high, second_low], axis=0), act_high)
        turned = turned[:D_HEAD] + turned[D_HEAD:] + bias_column
        second_before, bias_before = second_turned, bias_two
        scaled = gain_square * centred
        both = [part.astype(bf16) for part in (centred, scaled)]
        woven = [part[at : at + 16] for at in range(0, MINI, 16) for part in both]
        back = mm(jnp.concatenate([pull.astype(bf16)] + woven, axis=0), second_high)
        back_plain = jnp.concatenate([back[MINI + at : MINI + at + 16] for at in range(0, 2 * MINI, 32)], axis=0)
        back_scaled = jnp.concatenate([back[MINI + at : MINI + at + 16] for at in range(16, 2 * MINI, 32)], axis=0)
        first_high = weight_one.astype(bf16)
        first_low = (weight_one - first_high.astype(f32)).astype(bf16)
        inverse = lax.rsqrt(row_mean(centred * centred) + eps_norm)
        mean_an = inverse * (inverse * row_mean(scaled * centred) + row_mean(pull * centred))
        front = inverse * slope
        grad_one = (front * inverse) * (back_scaled - mean_an * back_plain) + front * back[:MINI]
        grad_one = grad_one.astype(bf16)
        scaled_turned = square_column * turned
        inverse_row = lax.rsqrt(jnp.mean(turned * turned, axis=0, keepdims=True) + eps_norm)
        mean_a_row = inverse_row * jnp.mean(scaled_turned, axis=0, keepdims=True) + pull_row
        mean_an_row = inverse_row * (
            inverse_row * jnp.mean(scaled_turned * turned, axis=0, keepdims=True)
            + jnp.mean(pull_turned * turned, axis=0, keepdims=True)
        )
        weighted_turned = (rate * inverse_row) * (
            (square_column - mean_an_row) * (inverse_row * turned) + (pull_turned - mean_a_row)
        )
        weighted_high = weighted_turned.astype(bf16)
        weighted_low = (weighted_turned - weighted_high.astype(f32)).astype(bf16)
        change = mm(jnp.concatenate([weighted_high, weighted_low], axis=0), act_high)
        second_turned = second_turned - (change[:D_HEAD] + change[D_HEAD:])
        mixed = mm(
            jnp.concatenate([plain, mixer], axis=1), jnp.concatenate([first_high, first_low, grad_one], axis=0)
        )
        weighted = weighted_turned.T
        bias_column = bias_column - jnp.sum(weighted_turned, axis=1, keepdims=True)
        bias_two = bias_two - jnp.sum(weighted, axis=0, keepdims=True)
        if len(waiting) == 2:
            finish(waiting, second_before, bias_before, backward, gain, shift, emit)
            waiting = []
        if ready is None and step % 2 == 0 and step + 2 < steps:
            made = made + prepare(step + 2, backward, tokens, gain, shift, columns)
        dual = gelu(mixed[MINI : 2 * MINI] + bias_one)
        dual_high = dual.astype(bf16)
        dual_low = (dual - dual_high.astype(f32)).astype(bf16)
        waiting.append((places[step], dual_high, dual_low, act_high, weighted.astype(bf16)))
        act, slope = gelu_and_slope(mixed[:MINI] + bias_one)
        act_high = act.astype(bf16)
        weight_one = weight_one + mixed[2 * MINI : 3 * MINI]
        bias_one = bias_one + mixed[3 * MINI : 3 * MINI + 1]
    if not keep_last:
        finish(waiting, second_turned, bias_two, backward, gain, shift, emit)
    return (weight_one, bias_one, second_turned, bias_two), waiting


def run_chunks(total, backward, qk_ref, v_ref, r_ref, state_refs, gain, shift, emit):
    assert total % CHUNK == 0

    def body(index, carry):
        tokens = tokens_of(index * CHUNK, CHUNK, total, backward, qk_ref, v_ref, r_ref)
        state, _ = run_chunk(backward, tokens, tuple(ref[...] for ref in state_refs), gain, shift, emit)
        for ref, part in zip(state_refs, state):
            ref[...] = part
        return carry

    lax.fori_loop(0, total // CHUNK, body, 0)
    return tuple(ref[...] for ref in state_refs)


def centre_start(w1_ref, c1_ref, w2t_ref, c2_ref):
    second_turned = w2t_ref[...]
    second_turned = second_turned - jnp.mean(second_turned, axis=0, keepdims=True)
    bias_two = c2_ref[...] - row_mean(c2_ref[...])
    return w1_ref[...], c1_ref[...], second_turned, bias_two


def first_phase(total, dir_ref, qk_ref, v_ref, r_ref, w1_ref, c1_ref, w2t_ref, c2_ref, gain_ref, shift_ref, y_ref,
                delta_ref, *refs):
    backward = dir_ref[0]
    gain, shift = gain_ref[...], shift_ref[...]
    start = centre_start(w1_ref, c1_ref, w2t_ref, c2_ref)

    def emit(spot, rows):
        y_ref[pl.ds(pl.multiple_of(spot * MINI, MINI), MINI), :] = rows

    if total <= CHUNK:
        *kept_refs, second_ref, bias_ref = refs
        tokens = tokens_of(0, total, total, backward, qk_ref, v_ref, r_ref)
        end, waiting = run_chunk(backward, tokens, start, gain, shift, emit, keep_last=True)
        for at, one in enumerate(waiting):
            spots = slice(at * MINI, (at + 1) * MINI)
            for ref, part in zip(kept_refs, one[1:]):
                ref[spots, :] = part
        second_ref[...] = end[2]
        bias_ref[...] = end[3]
    else:
        for ref, part in zip(refs, start):
            ref[...] = part
        end = run_chunks(total, backward, qk_ref, v_ref, r_ref, refs, gain, shift, emit)
    start = centre_start(w1_ref, c1_ref, w2t_ref, c2_ref)
    ends = [part - first for part, first in zip(end, start)]
    wide = jnp.concatenate([ends[3], jnp.zeros((1, INNER - D_HEAD), f32)], axis=1)
    at = lax.broadcasted_iota(jnp.int32, (8, INNER), 0)
    biases = jnp.where(at == 0, ends[1], jnp.where(at == 1, wide, 0.0))
    delta_ref[...] = jnp.concatenate([ends[0], ends[2], biases], axis=0).astype(bf16)


def between_phases(total, dir_ref, qk_ref, v_ref, r_ref, gain_ref, shift_ref, dual_ref, low_ref, act_ref, weighted_ref,
                   second_ref, bias_ref, tail_ref, plain_ref, mixer_ref, pull_ref, turned_ref, row_ref):
    gain, shift = gain_ref[...], shift_ref[...]
    backward = 1 - dir_ref[0]
    tokens = tokens_of(0, total, total, backward, qk_ref, v_ref, r_ref)
    columns = columns_of(gain, shift)
    for one in range(0, total, 2):
        for at, made in enumerate(prepare(one, backward, tokens, gain, shift, columns)):
            for ref, part in zip((plain_ref, mixer_ref, pull_ref, turned_ref, row_ref), made):
                ref[one + at] = part
    waiting = []
    for at in range(2):
        spots = slice(at * MINI, (at + 1) * MINI)
        kept = (ref[spots, :] for ref in (dual_ref, low_ref, act_ref, weighted_ref))
        waiting.append((at, *kept))

    def emit(at, rows):
        tail_ref[at * MINI : (at + 1) * MINI, :] = rows

    finish(waiting, second_ref[...], bias_ref[...], dir_ref[0], gain, shift, emit)


def second_phase(total, fold, dir_ref, qk_ref, v_ref, r_ref, w1_ref, c1_ref, w2t_ref, c2_ref, gain_ref, shift_ref, y_ref,
                 delta_ref, *refs):
    backward = 1 - dir_ref[0]
    gain, shift = gain_ref[...], shift_ref[...]
    delta = delta_ref[...].astype(f32)
    deltas = (
        delta[:D_HEAD],
        delta[2 * D_HEAD : 2 * D_HEAD + 1],
        delta[D_HEAD : 2 * D_HEAD],
        delta[2 * D_HEAD + 1 : 2 * D_HEAD + 2, :D_HEAD],
    )
    start = centre_start(w1_ref, c1_ref, w2t_ref, c2_ref)
    state = tuple(part + delta for part, delta in zip(start, deltas))
    if total <= CHUNK:
        tail_ref, *ready_refs, out_ref = refs
        tokens = tokens_of(0, total, total, backward, qk_ref, None, r_ref)
        done = []

        def emit(spot, rows):
            spots = pl.ds(pl.multiple_of(spot * MINI, MINI), MINI)
            step = len(done)
            done.append(step)
            if step < 2:
                first = tail_ref[(1 - step) * MINI : (2 - step) * MINI, :]
            else:
                first = y_ref[spots, :]
            summed = (first + rows).astype(bf16)
            if fold is None:
                out_ref[spots, :] = summed
                return
            for block in range(MINI // (2 * fold)):
                at = block * 2 * fold
                folded = jnp.concatenate([summed[at : at + fold], summed[at + fold : at + 2 * fold]], axis=1)
                out_ref[spot * (MINI // (2 * fold)) + block] = folded

        def ready(step):
            return tuple(ref[step] for ref in ready_refs)

        run_chunk(backward, tokens, state, gain, shift, emit, ready)
    else:
        out_ref, *state_refs = refs
        for ref, part in zip(state_refs, state):
            ref[...] = part

        def emit(spot, rows):
            spots = pl.ds(pl.multiple_of(spot * MINI, MINI), MINI)
            out_ref[spots, :] = (y_ref[spots, :] + rows).astype(bf16)

        run_chunks(total, backward, qk_ref, v_ref, r_ref, state_refs, gain, shift, emit)


def pack_kernel(head_size, heads_local, query_hbm, key_hbm, value_hbm, rate_hbm, out_hbm, query_ref, key_ref,
                value_ref, rate_ref, block_ref, arrived, left):
    copies = [
        pltpu.make_async_copy(source, target, arrived.at[at])
        for at, (source, target) in enumerate(
            [(query_hbm, query_ref), (key_hbm, key_ref), (value_hbm, value_ref), (rate_hbm, rate_ref)]
        )
    ]
    for copy in copies:
        copy.start()
    leaving = []

    def leave(s):
        blocks = pl.ds(s * head_size, head_size)
        leaving.append(pltpu.make_async_copy(block_ref.at[blocks], out_hbm.at[blocks], left.at[s]))
        leaving[-1].start()

    for s in range(heads_local, out_hbm.shape[0] // head_size):
        for h in range(head_size):
            block_ref[s * head_size + h] = jnp.zeros(out_hbm.shape[1:], bf16)
        leave(s)
    for copy in copies:
        copy.wait()
    fold = query_ref.shape[0] // 2
    row_at = lax.broadcasted_iota(jnp.int32, (8, rate_ref.shape[1]), 0)
    for s in range(heads_local):
        rate = rate_ref[s : s + 1, :]
        high = rate.astype(bf16).astype(f32)
        middle = (rate - high).astype(bf16).astype(f32)
        low = rate - high - middle
        rate_rows = jnp.where(row_at == 0, high, jnp.where(row_at == 1, middle, jnp.where(row_at == 2, low, 0.0)))
        for h in range(head_size):
            at = (h * heads_local + s) * D_HEAD
            value = value_ref[:, at : at + D_HEAD]
            pair = jnp.concatenate([query_ref[:, at : at + D_HEAD], key_ref[:, at : at + D_HEAD]], axis=1)
            folded = jnp.concatenate([value[:fold], value[fold:]], axis=1)
            block_ref[s * head_size + h] = jnp.concatenate([pair, folded, rate_rows.astype(bf16)], axis=0)
        leave(s)
    for copy in leaving:
        copy.wait()


def join_kernel(head_size, heads_local, back_ref, gate_ref, out_ref):
    fold = back_ref.shape[1]
    for pair_at in range(head_size * heads_local // 2):
        blocks = []
        for head in (2 * pair_at, 2 * pair_at + 1):
            blocks.append(back_ref[(head % heads_local) * head_size + head // heads_local])
        columns = slice(pair_at * 2 * D_HEAD, (pair_at + 1) * 2 * D_HEAD)
        for part in range(2):
            lanes = slice(part * D_HEAD, (part + 1) * D_HEAD)
            ttt = jnp.concatenate([blocks[0][:, lanes], blocks[1][:, lanes]], axis=1)
            spots = slice(part * fold, (part + 1) * fold)
            gated = gate_ref[spots, columns].astype(f32) * ttt.astype(f32)
            out_ref[spots, columns] = gated.astype(bf16)


def call_phase(kernel, outs, keeps_state, *operands):
    in_vmem = pl.BlockSpec(memory_space=pltpu.VMEM)
    state = [(D_HEAD, INNER), (1, INNER), (D_HEAD, INNER), (1, D_HEAD)] if keeps_state else []
    return pl.pallas_call(
        kernel,
        out_shape=outs,
        in_specs=[pl.BlockSpec(memory_space=pltpu.SMEM)] + [in_vmem] * (len(operands) - 1),
        out_specs=[in_vmem] * len(outs),
        scratch_shapes=[pltpu.VMEM(shape, f32) for shape in state],
        compiler_params=pltpu.CompilerParams(vmem_limit_bytes=24 * 2**20),
        cost_estimate=pl.CostEstimate(flops=10**8, bytes_accessed=10**6, transcendentals=10**5),
    )(*operands)


def pack_plain(head_size, half_seq, query_rows, key_rows, value_rows, step_rates):
    rows_here = query_rows.shape[0]
    token_block, heads_local = step_rates.shape

    def by_slot(rows):
        return rows.reshape(rows_here, head_size, heads_local, D_HEAD).transpose(2, 1, 0, 3)

    query, key, value = by_slot(query_rows), by_slot(key_rows), by_slot(value_rows)
    pairs = jnp.concatenate([query, key], axis=3)
    folded = jnp.concatenate([value[:, :, : rows_here // 2], value[:, :, rows_here // 2 :]], axis=3)
    rates = step_rates.T
    high = rates.astype(bf16)
    rest = rates - high.astype(f32)
    middle = rest.astype(bf16)
    low = (rest - middle.astype(f32)).astype(bf16)
    rate_rows = jnp.stack([high, middle, low], axis=1)
    rate_rows = jnp.concatenate([rate_rows, jnp.zeros((heads_local, 5, token_block), bf16)], axis=1)
    rate_rows = jnp.broadcast_to(rate_rows[:, None], (heads_local, head_size, 8, token_block))
    blocks = jnp.concatenate([pairs, folded, rate_rows], axis=2)
    spare = jnp.zeros((half_seq - heads_local,) + blocks.shape[1:], bf16)
    blocks = jnp.concatenate([blocks, spare], axis=0)
    return blocks.reshape((half_seq * head_size,) + blocks.shape[2:])


def local(head_size, seq_size, query_rows, key_rows, value_rows, gate_rows, step_rates, first_weight,
          first_bias, second_weight, second_bias, norm_gain, norm_shift):
    rows_here = query_rows.shape[0]
    heads_local = step_rates.shape[1]
    token_block = step_rates.shape[0]
    half_seq = seq_size // 2
    group = half_seq * head_size
    half_tokens = group * rows_here
    total = half_tokens // MINI
    seq_at = lax.axis_index("seq")
    half = seq_at // half_seq
    slot = jnp.minimum(seq_at % half_seq, heads_local - 1)
    group_at = lax.axis_index("head")
    halves = [
        [s * head_size + h for s in range(k * half_seq, (k + 1) * half_seq) for h in range(head_size)]
        for k in range(2)
    ]

    def exchange(blocks):
        return lax.all_to_all(blocks, ("seq", "head"), 0, 0, axis_index_groups=halves)

    block_rows = rows_here + rows_here // 2 + 8
    kernels_fit = rows_here % 32 == 0 and token_block == 2 * D_HEAD and head_size * heads_local % 2 == 0
    if kernels_fit:
        blocks = pl.pallas_call(
            functools.partial(pack_kernel, head_size, heads_local),
            out_shape=jax.ShapeDtypeStruct((group, block_rows, 2 * D_HEAD), bf16),
            in_specs=[pl.BlockSpec(memory_space=pltpu.HBM)] * 4,
            out_specs=pl.BlockSpec(memory_space=pltpu.HBM),
            scratch_shapes=[
                pltpu.VMEM(query_rows.shape, bf16),
                pltpu.VMEM(key_rows.shape, bf16),
                pltpu.VMEM(value_rows.shape, bf16),
                pltpu.VMEM((heads_local, token_block), f32),
                pltpu.VMEM((group, block_rows, 2 * D_HEAD), bf16),
                pltpu.SemaphoreType.DMA((4,)),
                pltpu.SemaphoreType.DMA((half_seq,)),
            ],
            compiler_params=pltpu.CompilerParams(vmem_limit_bytes=60 * 2**20),
        )(query_rows, key_rows, value_rows, step_rates.T)
    else:
        blocks = pack_plain(head_size, half_seq, query_rows, key_rows, value_rows, step_rates)
    got = exchange(blocks)

    qk_all = got[:, :rows_here].reshape(half_tokens, 2 * D_HEAD)
    got_value = got[:, rows_here : rows_here + rows_here // 2]
    short = total <= CHUNK
    fold = rows_here // 2 if kernels_fit and short else None
    v_all = got_value
    if fold is None:
        v_all = jnp.stack([got_value[..., :D_HEAD], got_value[..., D_HEAD:]], axis=1).reshape(half_tokens, D_HEAD)
    got_rate = got[:, rows_here + rows_here // 2 :].reshape(half_seq, head_size, 8, token_block)
    got_rate = lax.dynamic_index_in_dim(got_rate, group_at, 1, keepdims=False).astype(f32)
    r_all = (got_rate[:, 0] + got_rate[:, 1] + got_rate[:, 2]).reshape(half_seq, 1, 2 * MINI)

    def pick(array_in):
        return lax.dynamic_index_in_dim(array_in, slot, 0, keepdims=False)

    params = (
        pick(first_weight),
        pick(first_bias)[None],
        pick(second_weight).T,
        pick(second_bias)[None],
        pick(norm_gain)[None],
        pick(norm_shift)[None],
    )
    ahead = half.astype(jnp.int32).reshape(1)
    shape = jax.ShapeDtypeStruct
    outs = [shape((half_tokens, D_HEAD), f32), shape((2 * D_HEAD + 8, INNER), bf16)]
    if short:
        outs += [
            shape((2 * MINI, INNER), bf16),
            shape((2 * MINI, INNER), bf16),
            shape((2 * MINI, INNER), bf16),
            shape((2 * MINI, D_HEAD), bf16),
            shape((D_HEAD, INNER), f32),
            shape((1, D_HEAD), f32),
        ]
    tokens = (ahead, qk_all, v_all, r_all)
    y_first, delta, *left = call_phase(functools.partial(first_phase, total), outs, not short, *tokens, *params)
    route = [(s, (s + half_seq) % seq_size) for s in range(seq_size)]
    delta = lax.ppermute(delta, "seq", route)
    extra = []
    if short:
        outs = [
            shape((2 * MINI, D_HEAD), f32),
            shape((total, 3 * MINI + 16, 2 * D_HEAD), bf16),
            shape((total, 3 * MINI + 16, D_HEAD), bf16),
            shape((total, MINI, D_HEAD), f32),
            shape((total, MINI, D_HEAD), f32),
            shape((total, 1, MINI), f32),
        ]
        extra = call_phase(functools.partial(between_phases, total), outs, False, *tokens, *params[4:], *left)
    (summed,) = call_phase(
        functools.partial(second_phase, total, fold),
        [shape((half_tokens, D_HEAD) if fold is None else (group, fold, 2 * D_HEAD), bf16)],
        not short, *tokens, *params, y_first, delta, *extra,
    )
    if fold is None:
        summed = summed.reshape(group, 2, rows_here // 2, D_HEAD)
        summed = jnp.concatenate([summed[:, 0], summed[:, 1]], axis=2)
    back = exchange(summed)
    if kernels_fit:
        return pl.pallas_call(
            functools.partial(join_kernel, head_size, heads_local),
            out_shape=jax.ShapeDtypeStruct(gate_rows.shape, bf16),
            compiler_params=pltpu.CompilerParams(vmem_limit_bytes=8 * 2**20),
        )(back, gate_rows)
    back = back.reshape(half_seq, head_size, rows_here // 2, 2, D_HEAD)[:heads_local]
    back = back.transpose(3, 2, 1, 0, 4).reshape(rows_here, head_size * heads_local * D_HEAD)
    return (gate_rows.astype(f32) * back.astype(f32)).astype(bf16)


def solution(mesh):
    tokens = P(("seq", "head"), None)
    in_specs = (
        tokens,
        tokens,
        tokens,
        tokens,
        P("seq", "head"),
        P("head", None, None),
        P("head", None),
        P("head", None, None),
        P("head", None),
        P("head", None),
        P("head", None),
    )
    body = functools.partial(local, mesh.shape["head"], mesh.shape["seq"])
    return jax.shard_map(body, mesh=mesh, in_specs=in_specs, out_specs=tokens, check_vma=False)
```

```python
import functools

import jax
import jax.numpy as jnp
from jax import lax
from jax.experimental import pallas as pl
from jax.experimental.pallas import tpu as pltpu
from jax.sharding import PartitionSpec as P

D_HEAD = 64
INNER = 256
MINI = 64
CHUNK = 8

eps_norm = 1e-06
root_factor = 0.7978845608028654
cube_factor = 0.044715
f32 = jnp.float32
bf16 = jnp.bfloat16


def mm(left, right):
    return lax.dot_general(left, right, (((1,), (0,)), ((), ())), preferred_element_type=f32)


def mm_turned(left, right):
    return lax.dot_general(left, right, (((1,), (1,)), ((), ())), preferred_element_type=f32)


def gelu_and_slope(values):
    square = values * values
    tanh_term = jnp.tanh(values * (root_factor + root_factor * cube_factor * square))
    half = 0.5 + 0.5 * tanh_term
    act = values * half
    inner = root_factor + 3.0 * root_factor * cube_factor * square
    return act, half + act * (1.0 - tanh_term) * inner


def gelu(values):
    tanh_term = jnp.tanh(values * (root_factor + root_factor * cube_factor * (values * values)))
    return values * (0.5 + 0.5 * tanh_term)


def row_mean(values):
    return jnp.mean(values, axis=1, keepdims=True)


def tokens_of(first_step, steps, total, backward, qk_ref, v_ref, r_ref):
    lower = lax.broadcasted_iota(jnp.int32, (MINI, 2 * D_HEAD), 1) < D_HEAD
    places, pairs, queries, keys, values, rates = [], [], [], [], [], []
    for step in range(first_step, first_step + steps) if isinstance(first_step, int) else range(steps):
        at = step if isinstance(first_step, int) else first_step + step
        spot = jnp.where(backward == 0, at, total - 1 - at)
        spots = pl.ds(pl.multiple_of(spot * MINI, MINI), MINI)
        pair = qk_ref[spots, :]
        turned = jnp.concatenate([pair[:, D_HEAD:], pair[:, :D_HEAD]], axis=1)
        places.append(spot)
        pairs.append(pair)
        queries.append(jnp.where(lower, pair, turned))
        keys.append(jnp.where(lower, turned, pair))
        rate = r_ref[lax.div(spot, 2)]
        rate_turned = jnp.concatenate([rate[:, MINI:], rate[:, :MINI]], axis=1)
        rates.append(jnp.where(lax.rem(spot, 2) == 0, rate, rate_turned)[:, :MINI])
        if v_ref is None:
            continue
        if len(v_ref.shape) == 2:
            value = v_ref[spots, :]
            values.append(jnp.concatenate([value, value], axis=1))
            continue
        halves = []
        for block in range(MINI // (2 * v_ref.shape[1])):
            folded = v_ref[spot * (MINI // (2 * v_ref.shape[1])) + block]
            halves += [folded, jnp.concatenate([folded[:, D_HEAD:], folded[:, :D_HEAD]], axis=1)]
        values.append(jnp.concatenate(halves, axis=0))
    return places, pairs, queries, keys, values, rates


def columns_of(gain, shift):
    both = jnp.concatenate([jnp.broadcast_to(gain, (MINI, D_HEAD)), jnp.broadcast_to(shift, (MINI, D_HEAD))], axis=1).T
    return both[:D_HEAD], both[D_HEAD:]


def order_of(backward, shape):
    ahead = lax.broadcasted_iota(jnp.int32, shape, 0) - lax.broadcasted_iota(jnp.int32, shape, 1)
    return jnp.where(backward == 0, ahead, -ahead)


def prepare(one, backward, tokens, gain, shift, columns):
    _, _, queries, keys, values, rates = tokens
    gain_column, shift_column = columns
    steps = len(keys)
    two = min(one + 1, steps - 1)
    lower = lax.broadcasted_iota(jnp.int32, (MINI, 2 * D_HEAD), 1) < D_HEAD
    none = jnp.zeros((MINI, 2 * D_HEAD), bf16)
    seen = order_of(backward, (MINI, MINI)) >= 0
    nexts = [keys[min(step + 1, steps - 1)] for step in (one, two)]
    probes = jnp.concatenate(
        [jnp.where(lower, nexts[0], nexts[1]), jnp.where(lower, queries[one], queries[two])], axis=0
    )
    met = jnp.concatenate([jnp.where(lower, keys[one], none), none, jnp.where(lower, none, keys[two]), none], axis=0)
    attend = mm_turned(probes, met) + 1.0
    made = []
    for at, step in enumerate((one, two)):
        rate = rates[step]
        here = attend[:, 2 * at * MINI : (2 * at + 1) * MINI] * rate
        value, key = values[step].astype(f32), keys[step].astype(f32)
        both = jnp.where(lower, value, key).T
        value_turned, key_turned = both[:D_HEAD], both[D_HEAD:]
        mixer = jnp.concatenate(
            [
                (-here[:MINI]).astype(bf16),
                jnp.where(seen, -here[MINI:], 0.0).astype(bf16),
                (key_turned * -rate).astype(bf16),
                jnp.broadcast_to(-rate, (16, MINI)).astype(bf16),
            ],
            axis=0,
        )
        plain = jnp.concatenate([nexts[at], queries[step], none, none[:16]], axis=0)
        pull = gain * (shift - value[:, :D_HEAD] + key[:, :D_HEAD])
        pull_turned = gain_column * (shift_column - value_turned + key_turned)
        pull_row = jnp.mean(pull_turned, axis=0, keepdims=True)
        made.append((plain, mixer, pull, pull_turned, pull_row))
    return made


def finish(waiting, second_turned, bias_two, backward, gain, shift, emit):
    count = len(waiting)
    shape = (count * MINI, count * MINI)
    rows, columns = (lax.broadcasted_iota(jnp.int32, shape, dim) // MINI for dim in range(2))
    later = jnp.logical_and(rows == columns, order_of(backward, shape) < 0)
    unseen = jnp.logical_or(rows < columns, later)
    dual, dual_low, acts, weighted = (jnp.concatenate([one[at] for one in waiting], axis=0) for at in (1, 2, 3, 4))
    second_high = second_turned.astype(bf16)
    hidden = mm(jnp.where(unseen, mm_turned(dual, acts) + 1.0, 0.0).astype(bf16), weighted)
    plain = mm_turned(jnp.concatenate([dual, dual_low], axis=0), second_high)
    dual_two = plain[: count * MINI] + plain[count * MINI :] + bias_two + hidden
    second_low = (second_turned - second_high.astype(f32)).astype(bf16)
    dual_two = dual_two + mm_turned(dual, second_low)
    spread = lax.rsqrt(row_mean(dual_two * dual_two) + eps_norm)
    found = gain * (dual_two * spread) + shift
    for at, one in enumerate(waiting):
        emit(one[0], found[at * MINI : (at + 1) * MINI])


def run_chunk(backward, tokens, state, gain, shift, emit, ready=None, keep_last=False, ends=False):
    weight_one, bias_one, second_turned, bias_two = state
    places, pairs, queries, keys, values, rates = tokens
    steps = len(places)
    gain_square = gain * gain
    columns = columns_of(gain, shift)
    square_column = columns[0] * columns[0]
    blank = jnp.zeros((D_HEAD, INNER), bf16)
    first_high = weight_one.astype(bf16)
    first_low = (weight_one - first_high.astype(f32)).astype(bf16)
    act, slope = gelu_and_slope(
        mm(
            jnp.concatenate([pairs[0], pairs[0]], axis=1),
            jnp.concatenate([blank, first_high, blank, first_low], axis=0),
        )
        + bias_one
    )
    act_high = act.astype(bf16)
    bias_column = jnp.broadcast_to(bias_two, (MINI, D_HEAD)).T
    made = [] if ready is not None else prepare(0, backward, tokens, gain, shift, columns)
    waiting = []
    for step in range(steps):
        plain, mixer, pull, pull_turned, pull_row = made[step] if ready is None else ready(step)
        rate = rates[step]
        second_high = second_turned.astype(bf16)
        second_low = (second_turned - second_high.astype(f32)).astype(bf16)
        centred = mm_turned(act_high, second_high) + bias_two
        turned = mm_turned(jnp.concatenate([second_high, second_low], axis=0), act_high)
        turned = turned[:D_HEAD] + turned[D_HEAD:] + bias_column
        second_before, bias_before = second_turned, bias_two
        scaled = gain_square * centred
        both = [part.astype(bf16) for part in (centred, scaled)]
        woven = [part[at : at + 16] for at in range(0, MINI, 16) for part in both]
        back = mm(jnp.concatenate([pull.astype(bf16)] + woven, axis=0), second_high)
        back_plain = jnp.concatenate([back[MINI + at : MINI + at + 16] for at in range(0, 2 * MINI, 32)], axis=0)
        back_scaled = jnp.concatenate([back[MINI + at : MINI + at + 16] for at in range(16, 2 * MINI, 32)], axis=0)
        first_high = weight_one.astype(bf16)
        first_low = (weight_one - first_high.astype(f32)).astype(bf16)
        inverse = lax.rsqrt(row_mean(centred * centred) + eps_norm)
        mean_an = inverse * (inverse * row_mean(scaled * centred) + row_mean(pull * centred))
        front = inverse * slope
        grad_one = (front * inverse) * (back_scaled - mean_an * back_plain) + front * back[:MINI]
        grad_one = grad_one.astype(bf16)
        scaled_turned = square_column * turned
        inverse_row = lax.rsqrt(jnp.mean(turned * turned, axis=0, keepdims=True) + eps_norm)
        mean_a_row = inverse_row * jnp.mean(scaled_turned, axis=0, keepdims=True) + pull_row
        mean_an_row = inverse_row * (
            inverse_row * jnp.mean(scaled_turned * turned, axis=0, keepdims=True)
            + jnp.mean(pull_turned * turned, axis=0, keepdims=True)
        )
        weighted_turned = (rate * inverse_row) * (
            (square_column - mean_an_row) * (inverse_row * turned) + (pull_turned - mean_a_row)
        )
        weighted_high = weighted_turned.astype(bf16)
        weighted_low = (weighted_turned - weighted_high.astype(f32)).astype(bf16)
        change = mm(jnp.concatenate([weighted_high, weighted_low], axis=0), act_high)
        second_turned = second_turned - (change[:D_HEAD] + change[D_HEAD:])
        last = step + 1 == steps
        first = MINI if last else 0
        rows = slice(first, 2 * MINI if last and ends else None)
        mixed = mm(
            jnp.concatenate([plain[rows], mixer[rows]], axis=1),
            jnp.concatenate([first_high, first_low, grad_one], axis=0),
        )
        mixed_query = mixed[MINI - first : 2 * MINI - first]
        weighted = weighted_turned.T
        bias_column = bias_column - jnp.sum(weighted_turned, axis=1, keepdims=True)
        bias_two = bias_two - jnp.sum(weighted, axis=0, keepdims=True)
        if len(waiting) == 2:
            finish(waiting, second_before, bias_before, backward, gain, shift, emit)
            waiting = []
        if ready is None and step % 2 == 0 and step + 2 < steps:
            made = made + prepare(step + 2, backward, tokens, gain, shift, columns)
        dual = gelu(mixed_query + bias_one)
        dual_high = dual.astype(bf16)
        dual_low = (dual - dual_high.astype(f32)).astype(bf16)
        waiting.append((places[step], dual_high, dual_low, act_high, weighted.astype(bf16)))
        if not last:
            act, slope = gelu_and_slope(mixed[:MINI] + bias_one)
            act_high = act.astype(bf16)
        if last and ends:
            continue
        weight_one = weight_one + mixed[2 * MINI - first : 3 * MINI - first]
        bias_one = bias_one + mixed[3 * MINI - first : 3 * MINI - first + 1]
    if not keep_last:
        finish(waiting, second_turned, bias_two, backward, gain, shift, emit)
    return (weight_one, bias_one, second_turned, bias_two), waiting


def run_chunks(total, backward, qk_ref, v_ref, r_ref, state_refs, gain, shift, emit):
    assert total % CHUNK == 0

    def body(index, carry):
        tokens = tokens_of(index * CHUNK, CHUNK, total, backward, qk_ref, v_ref, r_ref)
        state, _ = run_chunk(backward, tokens, tuple(ref[...] for ref in state_refs), gain, shift, emit)
        for ref, part in zip(state_refs, state):
            ref[...] = part
        return carry

    lax.fori_loop(0, total // CHUNK, body, 0)
    return tuple(ref[...] for ref in state_refs)


def centre_start(w1_ref, c1_ref, w2t_ref, c2_ref):
    second_turned = w2t_ref[...]
    second_turned = second_turned - jnp.mean(second_turned, axis=0, keepdims=True)
    bias_two = c2_ref[...] - row_mean(c2_ref[...])
    return w1_ref[...], c1_ref[...], second_turned, bias_two


def first_phase(total, dir_ref, qk_ref, v_ref, r_ref, w1_ref, c1_ref, w2t_ref, c2_ref, gain_ref, shift_ref, y_ref,
                delta_ref, *refs):
    backward = dir_ref[0]
    gain, shift = gain_ref[...], shift_ref[...]
    start = centre_start(w1_ref, c1_ref, w2t_ref, c2_ref)

    def emit(spot, rows):
        y_ref[pl.ds(pl.multiple_of(spot * MINI, MINI), MINI), :] = rows

    if total <= CHUNK:
        *kept_refs, second_ref, bias_ref = refs
        tokens = tokens_of(0, total, total, backward, qk_ref, v_ref, r_ref)
        end, waiting = run_chunk(backward, tokens, start, gain, shift, emit, keep_last=True)
        for at, one in enumerate(waiting):
            spots = slice(at * MINI, (at + 1) * MINI)
            for ref, part in zip(kept_refs, one[1:]):
                ref[spots, :] = part
        second_ref[...] = end[2]
        bias_ref[...] = end[3]
    else:
        for ref, part in zip(refs, start):
            ref[...] = part
        end = run_chunks(total, backward, qk_ref, v_ref, r_ref, refs, gain, shift, emit)
    start = centre_start(w1_ref, c1_ref, w2t_ref, c2_ref)
    ends = [part - first for part, first in zip(end, start)]
    wide = jnp.concatenate([ends[3], jnp.zeros((1, INNER - D_HEAD), f32)], axis=1)
    at = lax.broadcasted_iota(jnp.int32, (8, INNER), 0)
    biases = jnp.where(at == 0, ends[1], jnp.where(at == 1, wide, 0.0))
    delta_ref[...] = jnp.concatenate([ends[0], ends[2], biases], axis=0).astype(bf16)


def between_phases(total, dir_ref, qk_ref, v_ref, r_ref, gain_ref, shift_ref, dual_ref, low_ref, act_ref, weighted_ref,
                   second_ref, bias_ref, tail_ref, plain_ref, mixer_ref, pull_ref, turned_ref, row_ref):
    gain, shift = gain_ref[...], shift_ref[...]
    backward = 1 - dir_ref[0]
    tokens = tokens_of(0, total, total, backward, qk_ref, v_ref, r_ref)
    columns = columns_of(gain, shift)
    for one in range(0, total, 2):
        for at, made in enumerate(prepare(one, backward, tokens, gain, shift, columns)):
            for ref, part in zip((plain_ref, mixer_ref, pull_ref, turned_ref, row_ref), made):
                ref[one + at] = part
    waiting = []
    for at in range(2):
        spots = slice(at * MINI, (at + 1) * MINI)
        kept = (ref[spots, :] for ref in (dual_ref, low_ref, act_ref, weighted_ref))
        waiting.append((at, *kept))

    def emit(at, rows):
        tail_ref[at * MINI : (at + 1) * MINI, :] = rows

    finish(waiting, second_ref[...], bias_ref[...], dir_ref[0], gain, shift, emit)


def second_phase(total, fold, dir_ref, qk_ref, v_ref, r_ref, w1_ref, c1_ref, w2t_ref, c2_ref, gain_ref, shift_ref, y_ref,
                 delta_ref, *refs):
    backward = 1 - dir_ref[0]
    gain, shift = gain_ref[...], shift_ref[...]
    delta = delta_ref[...].astype(f32)
    deltas = (
        delta[:D_HEAD],
        delta[2 * D_HEAD : 2 * D_HEAD + 1],
        delta[D_HEAD : 2 * D_HEAD],
        delta[2 * D_HEAD + 1 : 2 * D_HEAD + 2, :D_HEAD],
    )
    start = centre_start(w1_ref, c1_ref, w2t_ref, c2_ref)
    state = tuple(part + delta for part, delta in zip(start, deltas))
    if total <= CHUNK:
        tail_ref, *ready_refs, out_ref = refs
        tokens = tokens_of(0, total, total, backward, qk_ref, None, r_ref)
        done = []

        def emit(spot, rows):
            spots = pl.ds(pl.multiple_of(spot * MINI, MINI), MINI)
            step = len(done)
            done.append(step)
            if step < 2:
                first = tail_ref[(1 - step) * MINI : (2 - step) * MINI, :]
            else:
                first = y_ref[spots, :]
            summed = (first + rows).astype(bf16)
            if fold is None:
                out_ref[spots, :] = summed
                return
            for block in range(MINI // (2 * fold)):
                at = block * 2 * fold
                folded = jnp.concatenate([summed[at : at + fold], summed[at + fold : at + 2 * fold]], axis=1)
                out_ref[spot * (MINI // (2 * fold)) + block] = folded

        def ready(step):
            return tuple(ref[step] for ref in ready_refs)

        run_chunk(backward, tokens, state, gain, shift, emit, ready, ends=True)
    else:
        out_ref, *state_refs = refs
        for ref, part in zip(state_refs, state):
            ref[...] = part

        def emit(spot, rows):
            spots = pl.ds(pl.multiple_of(spot * MINI, MINI), MINI)
            out_ref[spots, :] = (y_ref[spots, :] + rows).astype(bf16)

        run_chunks(total, backward, qk_ref, v_ref, r_ref, state_refs, gain, shift, emit)


def pack_kernel(head_size, heads_local, query_hbm, key_hbm, value_hbm, rate_hbm, out_hbm, query_ref, key_ref,
                value_ref, rate_ref, block_ref, arrived, left):
    copies = [
        pltpu.make_async_copy(source, target, arrived.at[at])
        for at, (source, target) in enumerate(
            [(query_hbm, query_ref), (key_hbm, key_ref), (value_hbm, value_ref), (rate_hbm, rate_ref)]
        )
    ]
    for copy in copies:
        copy.start()
    leaving = []

    def leave(s):
        blocks = pl.ds(s * head_size, head_size)
        leaving.append(pltpu.make_async_copy(block_ref.at[blocks], out_hbm.at[blocks], left.at[s]))
        leaving[-1].start()

    for s in range(heads_local, out_hbm.shape[0] // head_size):
        for h in range(head_size):
            block_ref[s * head_size + h] = jnp.zeros(out_hbm.shape[1:], bf16)
        leave(s)
    for copy in copies:
        copy.wait()
    fold = query_ref.shape[0] // 2
    row_at = lax.broadcasted_iota(jnp.int32, (8, rate_ref.shape[1]), 0)
    for s in range(heads_local):
        rate = rate_ref[s : s + 1, :]
        high = rate.astype(bf16).astype(f32)
        middle = (rate - high).astype(bf16).astype(f32)
        low = rate - high - middle
        rate_rows = jnp.where(row_at == 0, high, jnp.where(row_at == 1, middle, jnp.where(row_at == 2, low, 0.0)))
        for h in range(head_size):
            at = (h * heads_local + s) * D_HEAD
            value = value_ref[:, at : at + D_HEAD]
            pair = jnp.concatenate([query_ref[:, at : at + D_HEAD], key_ref[:, at : at + D_HEAD]], axis=1)
            folded = jnp.concatenate([value[:fold], value[fold:]], axis=1)
            block_ref[s * head_size + h] = jnp.concatenate([pair, folded, rate_rows.astype(bf16)], axis=0)
        leave(s)
    for copy in leaving:
        copy.wait()


def join_kernel(head_size, heads_local, back_ref, gate_ref, out_ref):
    fold = back_ref.shape[1]
    for pair_at in range(head_size * heads_local // 2):
        blocks = []
        for head in (2 * pair_at, 2 * pair_at + 1):
            blocks.append(back_ref[(head % heads_local) * head_size + head // heads_local])
        columns = slice(pair_at * 2 * D_HEAD, (pair_at + 1) * 2 * D_HEAD)
        for part in range(2):
            lanes = slice(part * D_HEAD, (part + 1) * D_HEAD)
            ttt = jnp.concatenate([blocks[0][:, lanes], blocks[1][:, lanes]], axis=1)
            spots = slice(part * fold, (part + 1) * fold)
            gated = gate_ref[spots, columns].astype(f32) * ttt.astype(f32)
            out_ref[spots, columns] = gated.astype(bf16)


def call_phase(kernel, outs, keeps_state, *operands):
    in_vmem = pl.BlockSpec(memory_space=pltpu.VMEM)
    state = [(D_HEAD, INNER), (1, INNER), (D_HEAD, INNER), (1, D_HEAD)] if keeps_state else []
    return pl.pallas_call(
        kernel,
        out_shape=outs,
        in_specs=[pl.BlockSpec(memory_space=pltpu.SMEM)] + [in_vmem] * (len(operands) - 1),
        out_specs=[in_vmem] * len(outs),
        scratch_shapes=[pltpu.VMEM(shape, f32) for shape in state],
        compiler_params=pltpu.CompilerParams(vmem_limit_bytes=24 * 2**20),
        cost_estimate=pl.CostEstimate(flops=10**8, bytes_accessed=10**6, transcendentals=10**5),
    )(*operands)


def pack_plain(head_size, half_seq, query_rows, key_rows, value_rows, step_rates):
    rows_here = query_rows.shape[0]
    token_block, heads_local = step_rates.shape

    def by_slot(rows):
        return rows.reshape(rows_here, head_size, heads_local, D_HEAD).transpose(2, 1, 0, 3)

    query, key, value = by_slot(query_rows), by_slot(key_rows), by_slot(value_rows)
    pairs = jnp.concatenate([query, key], axis=3)
    folded = jnp.concatenate([value[:, :, : rows_here // 2], value[:, :, rows_here // 2 :]], axis=3)
    rates = step_rates.T
    high = rates.astype(bf16)
    rest = rates - high.astype(f32)
    middle = rest.astype(bf16)
    low = (rest - middle.astype(f32)).astype(bf16)
    rate_rows = jnp.stack([high, middle, low], axis=1)
    rate_rows = jnp.concatenate([rate_rows, jnp.zeros((heads_local, 5, token_block), bf16)], axis=1)
    rate_rows = jnp.broadcast_to(rate_rows[:, None], (heads_local, head_size, 8, token_block))
    blocks = jnp.concatenate([pairs, folded, rate_rows], axis=2)
    spare = jnp.zeros((half_seq - heads_local,) + blocks.shape[1:], bf16)
    blocks = jnp.concatenate([blocks, spare], axis=0)
    return blocks.reshape((half_seq * head_size,) + blocks.shape[2:])


def local(head_size, seq_size, query_rows, key_rows, value_rows, gate_rows, step_rates, first_weight,
          first_bias, second_weight, second_bias, norm_gain, norm_shift):
    rows_here = query_rows.shape[0]
    heads_local = step_rates.shape[1]
    token_block = step_rates.shape[0]
    half_seq = seq_size // 2
    group = half_seq * head_size
    half_tokens = group * rows_here
    total = half_tokens // MINI
    seq_at = lax.axis_index("seq")
    half = seq_at // half_seq
    slot = jnp.minimum(seq_at % half_seq, heads_local - 1)
    group_at = lax.axis_index("head")
    halves = [
        [s * head_size + h for s in range(k * half_seq, (k + 1) * half_seq) for h in range(head_size)]
        for k in range(2)
    ]

    def exchange(blocks):
        return lax.all_to_all(blocks, ("seq", "head"), 0, 0, axis_index_groups=halves)

    block_rows = rows_here + rows_here // 2 + 8
    kernels_fit = rows_here % 32 == 0 and token_block == 2 * D_HEAD and head_size * heads_local % 2 == 0
    if kernels_fit:
        blocks = pl.pallas_call(
            functools.partial(pack_kernel, head_size, heads_local),
            out_shape=jax.ShapeDtypeStruct((group, block_rows, 2 * D_HEAD), bf16),
            in_specs=[pl.BlockSpec(memory_space=pltpu.HBM)] * 4,
            out_specs=pl.BlockSpec(memory_space=pltpu.HBM),
            scratch_shapes=[
                pltpu.VMEM(query_rows.shape, bf16),
                pltpu.VMEM(key_rows.shape, bf16),
                pltpu.VMEM(value_rows.shape, bf16),
                pltpu.VMEM((heads_local, token_block), f32),
                pltpu.VMEM((group, block_rows, 2 * D_HEAD), bf16),
                pltpu.SemaphoreType.DMA((4,)),
                pltpu.SemaphoreType.DMA((half_seq,)),
            ],
            compiler_params=pltpu.CompilerParams(vmem_limit_bytes=60 * 2**20),
        )(query_rows, key_rows, value_rows, step_rates.T)
    else:
        blocks = pack_plain(head_size, half_seq, query_rows, key_rows, value_rows, step_rates)
    got = exchange(blocks)

    qk_all = got[:, :rows_here].reshape(half_tokens, 2 * D_HEAD)
    got_value = got[:, rows_here : rows_here + rows_here // 2]
    short = total <= CHUNK
    fold = rows_here // 2 if kernels_fit and short else None
    v_all = got_value
    if fold is None:
        v_all = jnp.stack([got_value[..., :D_HEAD], got_value[..., D_HEAD:]], axis=1).reshape(half_tokens, D_HEAD)
    got_rate = got[:, rows_here + rows_here // 2 :].reshape(half_seq, head_size, 8, token_block)
    got_rate = lax.dynamic_index_in_dim(got_rate, group_at, 1, keepdims=False).astype(f32)
    r_all = (got_rate[:, 0] + got_rate[:, 1] + got_rate[:, 2]).reshape(half_seq, 1, 2 * MINI)

    def pick(array_in):
        return lax.dynamic_index_in_dim(array_in, slot, 0, keepdims=False)

    params = (
        pick(first_weight),
        pick(first_bias)[None],
        pick(second_weight).T,
        pick(second_bias)[None],
        pick(norm_gain)[None],
        pick(norm_shift)[None],
    )
    ahead = half.astype(jnp.int32).reshape(1)
    shape = jax.ShapeDtypeStruct
    outs = [shape((half_tokens, D_HEAD), f32), shape((2 * D_HEAD + 8, INNER), bf16)]
    if short:
        outs += [
            shape((2 * MINI, INNER), bf16),
            shape((2 * MINI, INNER), bf16),
            shape((2 * MINI, INNER), bf16),
            shape((2 * MINI, D_HEAD), bf16),
            shape((D_HEAD, INNER), f32),
            shape((1, D_HEAD), f32),
        ]
    tokens = (ahead, qk_all, v_all, r_all)
    y_first, delta, *left = call_phase(functools.partial(first_phase, total), outs, not short, *tokens, *params)
    route = [(s, (s + half_seq) % seq_size) for s in range(seq_size)]
    delta = lax.ppermute(delta, "seq", route)
    extra = []
    if short:
        outs = [
            shape((2 * MINI, D_HEAD), f32),
            shape((total, 3 * MINI + 16, 2 * D_HEAD), bf16),
            shape((total, 3 * MINI + 16, D_HEAD), bf16),
            shape((total, MINI, D_HEAD), f32),
            shape((total, MINI, D_HEAD), f32),
            shape((total, 1, MINI), f32),
        ]
        extra = call_phase(functools.partial(between_phases, total), outs, False, *tokens, *params[4:], *left)
    (summed,) = call_phase(
        functools.partial(second_phase, total, fold),
        [shape((half_tokens, D_HEAD) if fold is None else (group, fold, 2 * D_HEAD), bf16)],
        not short, *tokens, *params, y_first, delta, *extra,
    )
    if fold is None:
        summed = summed.reshape(group, 2, rows_here // 2, D_HEAD)
        summed = jnp.concatenate([summed[:, 0], summed[:, 1]], axis=2)
    back = exchange(summed)
    if kernels_fit:
        return pl.pallas_call(
            functools.partial(join_kernel, head_size, heads_local),
            out_shape=jax.ShapeDtypeStruct(gate_rows.shape, bf16),
            compiler_params=pltpu.CompilerParams(vmem_limit_bytes=8 * 2**20),
        )(back, gate_rows)
    back = back.reshape(half_seq, head_size, rows_here // 2, 2, D_HEAD)[:heads_local]
    back = back.transpose(3, 2, 1, 0, 4).reshape(rows_here, head_size * heads_local * D_HEAD)
    return (gate_rows.astype(f32) * back.astype(f32)).astype(bf16)


def solution(mesh):
    tokens = P(("seq", "head"), None)
    in_specs = (
        tokens,
        tokens,
        tokens,
        tokens,
        P("seq", "head"),
        P("head", None, None),
        P("head", None),
        P("head", None, None),
        P("head", None),
        P("head", None),
        P("head", None),
    )
    body = functools.partial(local, mesh.shape["head"], mesh.shape["seq"])
    return jax.shard_map(body, mesh=mesh, in_specs=in_specs, out_specs=tokens, check_vma=False)
```

```python
import functools

import jax
import jax.numpy as jnp
from jax import lax
from jax.experimental import pallas as pl
from jax.experimental.pallas import tpu as pltpu
from jax.sharding import PartitionSpec as P

D_HEAD = 64
INNER = 256
MINI = 64
CHUNK = 8

eps_norm = 1e-06
root_factor = 0.7978845608028654
cube_factor = 0.044715
f32 = jnp.float32
bf16 = jnp.bfloat16


def mm(left, right):
    return lax.dot_general(left, right, (((1,), (0,)), ((), ())), preferred_element_type=f32)


def mm_turned(left, right):
    return lax.dot_general(left, right, (((1,), (1,)), ((), ())), preferred_element_type=f32)


def gelu_and_slope(values):
    square = values * values
    tanh_term = jnp.tanh(values * (root_factor + root_factor * cube_factor * square))
    half = 0.5 + 0.5 * tanh_term
    act = values * half
    inner = root_factor + 3.0 * root_factor * cube_factor * square
    return act, half + act * (1.0 - tanh_term) * inner


def gelu(values):
    tanh_term = jnp.tanh(values * (root_factor + root_factor * cube_factor * (values * values)))
    return values * (0.5 + 0.5 * tanh_term)


def row_mean(values):
    return jnp.mean(values, axis=1, keepdims=True)


def tokens_of(first_step, steps, total, backward, qk_ref, v_ref, r_ref):
    lower = lax.broadcasted_iota(jnp.int32, (MINI, 2 * D_HEAD), 1) < D_HEAD
    places, pairs, queries, keys, values, rates = [], [], [], [], [], []
    for step in range(first_step, first_step + steps) if isinstance(first_step, int) else range(steps):
        at = step if isinstance(first_step, int) else first_step + step
        spot = jnp.where(backward == 0, at, total - 1 - at)
        spots = pl.ds(pl.multiple_of(spot * MINI, MINI), MINI)
        pair = qk_ref[spots, :]
        turned = jnp.concatenate([pair[:, D_HEAD:], pair[:, :D_HEAD]], axis=1)
        places.append(spot)
        pairs.append(pair)
        queries.append(jnp.where(lower, pair, turned))
        keys.append(jnp.where(lower, turned, pair))
        rate = r_ref[lax.div(spot, 2)]
        rate_turned = jnp.concatenate([rate[:, MINI:], rate[:, :MINI]], axis=1)
        rates.append(jnp.where(lax.rem(spot, 2) == 0, rate, rate_turned)[:, :MINI])
        if v_ref is None:
            continue
        if len(v_ref.shape) == 2:
            value = v_ref[spots, :]
            values.append(jnp.concatenate([value, value], axis=1))
            continue
        halves = []
        for block in range(MINI // (2 * v_ref.shape[1])):
            folded = v_ref[spot * (MINI // (2 * v_ref.shape[1])) + block]
            halves += [folded, jnp.concatenate([folded[:, D_HEAD:], folded[:, :D_HEAD]], axis=1)]
        values.append(jnp.concatenate(halves, axis=0))
    return places, pairs, queries, keys, values, rates


def columns_of(gain, shift):
    both = jnp.concatenate([jnp.broadcast_to(gain, (MINI, D_HEAD)), jnp.broadcast_to(shift, (MINI, D_HEAD))], axis=1).T
    return both[:D_HEAD], both[D_HEAD:]


def order_of(backward, shape):
    ahead = lax.broadcasted_iota(jnp.int32, shape, 0) - lax.broadcasted_iota(jnp.int32, shape, 1)
    return jnp.where(backward == 0, ahead, -ahead)


def prepare(one, backward, tokens, gain, shift, columns):
    _, _, queries, keys, values, rates = tokens
    gain_column, shift_column = columns
    steps = len(keys)
    two = min(one + 1, steps - 1)
    lower = lax.broadcasted_iota(jnp.int32, (MINI, 2 * D_HEAD), 1) < D_HEAD
    none = jnp.zeros((MINI, 2 * D_HEAD), bf16)
    seen = order_of(backward, (MINI, MINI)) >= 0
    nexts = [keys[min(step + 1, steps - 1)] for step in (one, two)]
    probes = jnp.concatenate(
        [jnp.where(lower, nexts[0], nexts[1]), jnp.where(lower, queries[one], queries[two])], axis=0
    )
    met = jnp.concatenate([jnp.where(lower, keys[one], none), none, jnp.where(lower, none, keys[two]), none], axis=0)
    attend = mm_turned(probes, met) + 1.0
    made = []
    for at, step in enumerate((one, two)):
        rate = rates[step]
        here = attend[:, 2 * at * MINI : (2 * at + 1) * MINI] * rate
        value, key = values[step].astype(f32), keys[step].astype(f32)
        both = jnp.where(lower, value, key).T
        value_turned, key_turned = both[:D_HEAD], both[D_HEAD:]
        mixer = jnp.concatenate(
            [
                (-here[:MINI]).astype(bf16),
                jnp.where(seen, -here[MINI:], 0.0).astype(bf16),
                (key_turned * -rate).astype(bf16),
                jnp.broadcast_to(-rate, (16, MINI)).astype(bf16),
            ],
            axis=0,
        )
        plain = jnp.concatenate([nexts[at], queries[step], none, none[:16]], axis=0)
        pull = gain * (shift - value[:, :D_HEAD] + key[:, :D_HEAD])
        pull_turned = gain_column * (shift_column - value_turned + key_turned)
        pull_row = jnp.mean(pull_turned, axis=0, keepdims=True)
        made.append((plain, mixer, pull, pull_turned, pull_row))
    return made


def finish(waiting, second_turned, bias_two, backward, gain, shift, emit):
    count = len(waiting)
    shape = (count * MINI, count * MINI)
    rows, columns = (lax.broadcasted_iota(jnp.int32, shape, dim) // MINI for dim in range(2))
    later = jnp.logical_and(rows == columns, order_of(backward, shape) < 0)
    unseen = jnp.logical_or(rows < columns, later)
    dual, dual_low, acts, weighted = (jnp.concatenate([one[at] for one in waiting], axis=0) for at in (1, 2, 3, 4))
    second_high = second_turned.astype(bf16)
    hidden = mm(jnp.where(unseen, mm_turned(dual, acts) + 1.0, 0.0).astype(bf16), weighted)
    plain = mm_turned(jnp.concatenate([dual, dual_low], axis=0), second_high)
    dual_two = plain[: count * MINI] + plain[count * MINI :] + bias_two + hidden
    second_low = (second_turned - second_high.astype(f32)).astype(bf16)
    dual_two = dual_two + mm_turned(dual, second_low)
    spread = lax.rsqrt(row_mean(dual_two * dual_two) + eps_norm)
    found = gain * (dual_two * spread) + shift
    for at, one in enumerate(waiting):
        emit(one[0], found[at * MINI : (at + 1) * MINI])


def first_product(pair, weight_one):
    blank = jnp.zeros((D_HEAD, INNER), bf16)
    first_high = weight_one.astype(bf16)
    first_low = (weight_one - first_high.astype(f32)).astype(bf16)
    return mm(
        jnp.concatenate([pair, pair], axis=1), jnp.concatenate([blank, first_high, blank, first_low], axis=0)
    )


def run_chunk(backward, tokens, state, gain, shift, emit, ready=None, keep_last=False, ends=False, pre_one=None):
    weight_one, bias_one, second_turned, bias_two = state
    places, pairs, queries, keys, values, rates = tokens
    steps = len(places)
    gain_square = gain * gain
    columns = columns_of(gain, shift)
    square_column = columns[0] * columns[0]
    if pre_one is None:
        pre_one = first_product(pairs[0], weight_one) + bias_one
    act, slope = gelu_and_slope(pre_one)
    act_high = act.astype(bf16)
    bias_column = jnp.broadcast_to(bias_two, (MINI, D_HEAD)).T
    made = [] if ready is not None else prepare(0, backward, tokens, gain, shift, columns)
    waiting = []
    for step in range(steps):
        plain, mixer, pull, pull_turned, pull_row = made[step] if ready is None else ready(step)
        rate = rates[step]
        second_high = second_turned.astype(bf16)
        second_low = (second_turned - second_high.astype(f32)).astype(bf16)
        centred = mm_turned(act_high, second_high) + bias_two
        turned = mm_turned(jnp.concatenate([second_high, second_low], axis=0), act_high)
        turned = turned[:D_HEAD] + turned[D_HEAD:] + bias_column
        second_before, bias_before = second_turned, bias_two
        scaled = gain_square * centred
        both = [part.astype(bf16) for part in (centred, scaled)]
        woven = [part[at : at + 16] for at in range(0, MINI, 16) for part in both]
        back = mm(jnp.concatenate([pull.astype(bf16)] + woven, axis=0), second_high)
        back_plain = jnp.concatenate([back[MINI + at : MINI + at + 16] for at in range(0, 2 * MINI, 32)], axis=0)
        back_scaled = jnp.concatenate([back[MINI + at : MINI + at + 16] for at in range(16, 2 * MINI, 32)], axis=0)
        first_high = weight_one.astype(bf16)
        first_low = (weight_one - first_high.astype(f32)).astype(bf16)
        inverse = lax.rsqrt(row_mean(centred * centred) + eps_norm)
        mean_an = inverse * (inverse * row_mean(scaled * centred) + row_mean(pull * centred))
        front = inverse * slope
        grad_one = (front * inverse) * (back_scaled - mean_an * back_plain) + front * back[:MINI]
        grad_one = grad_one.astype(bf16)
        scaled_turned = square_column * turned
        inverse_row = lax.rsqrt(jnp.mean(turned * turned, axis=0, keepdims=True) + eps_norm)
        mean_a_row = inverse_row * jnp.mean(scaled_turned, axis=0, keepdims=True) + pull_row
        mean_an_row = inverse_row * (
            inverse_row * jnp.mean(scaled_turned * turned, axis=0, keepdims=True)
            + jnp.mean(pull_turned * turned, axis=0, keepdims=True)
        )
        weighted_turned = (rate * inverse_row) * (
            (square_column - mean_an_row) * (inverse_row * turned) + (pull_turned - mean_a_row)
        )
        weighted_high = weighted_turned.astype(bf16)
        weighted_low = (weighted_turned - weighted_high.astype(f32)).astype(bf16)
        change = mm(jnp.concatenate([weighted_high, weighted_low], axis=0), act_high)
        second_turned = second_turned - (change[:D_HEAD] + change[D_HEAD:])
        last = step + 1 == steps
        first = MINI if last else 0
        rows = slice(first, 2 * MINI if last and ends else None)
        mixed = mm(
            jnp.concatenate([plain[rows], mixer[rows]], axis=1),
            jnp.concatenate([first_high, first_low, grad_one], axis=0),
        )
        mixed_query = mixed[MINI - first : 2 * MINI - first]
        weighted = weighted_turned.T
        bias_column = bias_column - jnp.sum(weighted_turned, axis=1, keepdims=True)
        bias_two = bias_two - jnp.sum(weighted, axis=0, keepdims=True)
        if len(waiting) == 2:
            finish(waiting, second_before, bias_before, backward, gain, shift, emit)
            waiting = []
        if ready is None and step % 2 == 0 and step + 2 < steps:
            made = made + prepare(step + 2, backward, tokens, gain, shift, columns)
        dual = gelu(mixed_query + bias_one)
        dual_high = dual.astype(bf16)
        dual_low = (dual - dual_high.astype(f32)).astype(bf16)
        waiting.append((places[step], dual_high, dual_low, act_high, weighted.astype(bf16)))
        if not last:
            act, slope = gelu_and_slope(mixed[:MINI] + bias_one)
            act_high = act.astype(bf16)
        if last and ends:
            continue
        weight_one = weight_one + mixed[2 * MINI - first : 3 * MINI - first]
        bias_one = bias_one + mixed[3 * MINI - first : 3 * MINI - first + 1]
    if not keep_last:
        finish(waiting, second_turned, bias_two, backward, gain, shift, emit)
    return (weight_one, bias_one, second_turned, bias_two), waiting


def run_chunks(total, backward, qk_ref, v_ref, r_ref, state_refs, gain, shift, emit):
    assert total % CHUNK == 0

    def body(index, carry):
        tokens = tokens_of(index * CHUNK, CHUNK, total, backward, qk_ref, v_ref, r_ref)
        state, _ = run_chunk(backward, tokens, tuple(ref[...] for ref in state_refs), gain, shift, emit)
        for ref, part in zip(state_refs, state):
            ref[...] = part
        return carry

    lax.fori_loop(0, total // CHUNK, body, 0)
    return tuple(ref[...] for ref in state_refs)


def centre_start(w1_ref, c1_ref, w2t_ref, c2_ref):
    second_turned = w2t_ref[...]
    second_turned = second_turned - jnp.mean(second_turned, axis=0, keepdims=True)
    bias_two = c2_ref[...] - row_mean(c2_ref[...])
    return w1_ref[...], c1_ref[...], second_turned, bias_two


def first_phase(total, dir_ref, qk_ref, v_ref, r_ref, w1_ref, c1_ref, w2t_ref, c2_ref, gain_ref, shift_ref, y_ref,
                delta_ref, *refs):
    backward = dir_ref[0]
    gain, shift = gain_ref[...], shift_ref[...]
    start = centre_start(w1_ref, c1_ref, w2t_ref, c2_ref)

    def emit(spot, rows):
        y_ref[pl.ds(pl.multiple_of(spot * MINI, MINI), MINI), :] = rows

    if total <= CHUNK:
        *kept_refs, second_ref, bias_ref = refs
        tokens = tokens_of(0, total, total, backward, qk_ref, v_ref, r_ref)
        end, waiting = run_chunk(backward, tokens, start, gain, shift, emit, keep_last=True)
        for at, one in enumerate(waiting):
            spots = slice(at * MINI, (at + 1) * MINI)
            for ref, part in zip(kept_refs, one[1:]):
                ref[spots, :] = part
        second_ref[...] = end[2]
        bias_ref[...] = end[3]
    else:
        for ref, part in zip(refs, start):
            ref[...] = part
        end = run_chunks(total, backward, qk_ref, v_ref, r_ref, refs, gain, shift, emit)
    start = centre_start(w1_ref, c1_ref, w2t_ref, c2_ref)
    ends = [part - first for part, first in zip(end, start)]
    wide = jnp.concatenate([ends[3], jnp.zeros((1, INNER - D_HEAD), f32)], axis=1)
    at = lax.broadcasted_iota(jnp.int32, (8, INNER), 0)
    biases = jnp.where(at == 0, ends[1], jnp.where(at == 1, wide, 0.0))
    delta_ref[...] = jnp.concatenate([ends[0], ends[2], biases], axis=0).astype(bf16)


def between_phases(total, dir_ref, qk_ref, v_ref, r_ref, w1_ref, c1_ref, gain_ref, shift_ref, dual_ref, low_ref, act_ref, weighted_ref,
                   second_ref, bias_ref, tail_ref, pre_ref, plain_ref, mixer_ref, pull_ref, turned_ref, row_ref):
    gain, shift = gain_ref[...], shift_ref[...]
    backward = 1 - dir_ref[0]
    tokens = tokens_of(0, total, total, backward, qk_ref, v_ref, r_ref)
    pre_ref[...] = first_product(tokens[1][0], w1_ref[...]) + c1_ref[...]
    columns = columns_of(gain, shift)
    for one in range(0, total, 2):
        for at, made in enumerate(prepare(one, backward, tokens, gain, shift, columns)):
            for ref, part in zip((plain_ref, mixer_ref, pull_ref, turned_ref, row_ref), made):
                ref[one + at] = part
    waiting = []
    for at in range(2):
        spots = slice(at * MINI, (at + 1) * MINI)
        kept = (ref[spots, :] for ref in (dual_ref, low_ref, act_ref, weighted_ref))
        waiting.append((at, *kept))

    def emit(at, rows):
        tail_ref[at * MINI : (at + 1) * MINI, :] = rows

    finish(waiting, second_ref[...], bias_ref[...], dir_ref[0], gain, shift, emit)


def second_phase(total, fold, dir_ref, qk_ref, v_ref, r_ref, w1_ref, c1_ref, w2t_ref, c2_ref, gain_ref, shift_ref, y_ref,
                 delta_ref, *refs):
    backward = 1 - dir_ref[0]
    gain, shift = gain_ref[...], shift_ref[...]
    delta = delta_ref[...].astype(f32)
    deltas = (
        delta[:D_HEAD],
        delta[2 * D_HEAD : 2 * D_HEAD + 1],
        delta[D_HEAD : 2 * D_HEAD],
        delta[2 * D_HEAD + 1 : 2 * D_HEAD + 2, :D_HEAD],
    )
    start = centre_start(w1_ref, c1_ref, w2t_ref, c2_ref)
    state = tuple(part + delta for part, delta in zip(start, deltas))
    if total <= CHUNK:
        tail_ref, pre_ref, *ready_refs, out_ref = refs
        tokens = tokens_of(0, total, total, backward, qk_ref, None, r_ref)
        done = []

        def emit(spot, rows):
            spots = pl.ds(pl.multiple_of(spot * MINI, MINI), MINI)
            step = len(done)
            done.append(step)
            if step < 2:
                first = tail_ref[(1 - step) * MINI : (2 - step) * MINI, :]
            else:
                first = y_ref[spots, :]
            summed = (first + rows).astype(bf16)
            if fold is None:
                out_ref[spots, :] = summed
                return
            for block in range(MINI // (2 * fold)):
                at = block * 2 * fold
                folded = jnp.concatenate([summed[at : at + fold], summed[at + fold : at + 2 * fold]], axis=1)
                out_ref[spot * (MINI // (2 * fold)) + block] = folded

        blank = jnp.zeros((D_HEAD, INNER), bf16)
        moved = jnp.concatenate([blank, delta_ref[0:D_HEAD, :]], axis=0)
        pre_one = pre_ref[...] + mm(tokens[1][0], moved) + deltas[1]

        def ready(step):
            return tuple(ref[step] for ref in ready_refs)

        run_chunk(backward, tokens, state, gain, shift, emit, ready, ends=True, pre_one=pre_one)
    else:
        out_ref, *state_refs = refs
        for ref, part in zip(state_refs, state):
            ref[...] = part

        def emit(spot, rows):
            spots = pl.ds(pl.multiple_of(spot * MINI, MINI), MINI)
            out_ref[spots, :] = (y_ref[spots, :] + rows).astype(bf16)

        run_chunks(total, backward, qk_ref, v_ref, r_ref, state_refs, gain, shift, emit)


def pack_kernel(head_size, heads_local, query_hbm, key_hbm, value_hbm, rate_hbm, out_hbm, query_ref, key_ref,
                value_ref, rate_ref, block_ref, arrived, left):
    copies = [
        pltpu.make_async_copy(source, target, arrived.at[at])
        for at, (source, target) in enumerate(
            [(query_hbm, query_ref), (key_hbm, key_ref), (value_hbm, value_ref), (rate_hbm, rate_ref)]
        )
    ]
    for copy in copies:
        copy.start()
    leaving = []

    def leave(s):
        blocks = pl.ds(s * head_size, head_size)
        leaving.append(pltpu.make_async_copy(block_ref.at[blocks], out_hbm.at[blocks], left.at[s]))
        leaving[-1].start()

    for s in range(heads_local, out_hbm.shape[0] // head_size):
        for h in range(head_size):
            block_ref[s * head_size + h] = jnp.zeros(out_hbm.shape[1:], bf16)
        leave(s)
    for copy in copies:
        copy.wait()
    fold = query_ref.shape[0] // 2
    row_at = lax.broadcasted_iota(jnp.int32, (8, rate_ref.shape[1]), 0)
    for s in range(heads_local):
        rate = rate_ref[s : s + 1, :]
        high = rate.astype(bf16).astype(f32)
        middle = (rate - high).astype(bf16).astype(f32)
        low = rate - high - middle
        rate_rows = jnp.where(row_at == 0, high, jnp.where(row_at == 1, middle, jnp.where(row_at == 2, low, 0.0)))
        for h in range(head_size):
            at = (h * heads_local + s) * D_HEAD
            value = value_ref[:, at : at + D_HEAD]
            pair = jnp.concatenate([query_ref[:, at : at + D_HEAD], key_ref[:, at : at + D_HEAD]], axis=1)
            folded = jnp.concatenate([value[:fold], value[fold:]], axis=1)
            block_ref[s * head_size + h] = jnp.concatenate([pair, folded, rate_rows.astype(bf16)], axis=0)
        leave(s)
    for copy in leaving:
        copy.wait()


def join_kernel(head_size, heads_local, back_ref, gate_ref, out_ref):
    fold = back_ref.shape[1]
    for pair_at in range(head_size * heads_local // 2):
        blocks = []
        for head in (2 * pair_at, 2 * pair_at + 1):
            blocks.append(back_ref[(head % heads_local) * head_size + head // heads_local])
        columns = slice(pair_at * 2 * D_HEAD, (pair_at + 1) * 2 * D_HEAD)
        for part in range(2):
            lanes = slice(part * D_HEAD, (part + 1) * D_HEAD)
            ttt = jnp.concatenate([blocks[0][:, lanes], blocks[1][:, lanes]], axis=1)
            spots = slice(part * fold, (part + 1) * fold)
            gated = gate_ref[spots, columns].astype(f32) * ttt.astype(f32)
            out_ref[spots, columns] = gated.astype(bf16)


def call_phase(kernel, outs, keeps_state, *operands):
    in_vmem = pl.BlockSpec(memory_space=pltpu.VMEM)
    state = [(D_HEAD, INNER), (1, INNER), (D_HEAD, INNER), (1, D_HEAD)] if keeps_state else []
    return pl.pallas_call(
        kernel,
        out_shape=outs,
        in_specs=[pl.BlockSpec(memory_space=pltpu.SMEM)] + [in_vmem] * (len(operands) - 1),
        out_specs=[in_vmem] * len(outs),
        scratch_shapes=[pltpu.VMEM(shape, f32) for shape in state],
        compiler_params=pltpu.CompilerParams(vmem_limit_bytes=24 * 2**20),
        cost_estimate=pl.CostEstimate(flops=10**8, bytes_accessed=10**6, transcendentals=10**5),
    )(*operands)


def pack_plain(head_size, half_seq, query_rows, key_rows, value_rows, step_rates):
    rows_here = query_rows.shape[0]
    token_block, heads_local = step_rates.shape

    def by_slot(rows):
        return rows.reshape(rows_here, head_size, heads_local, D_HEAD).transpose(2, 1, 0, 3)

    query, key, value = by_slot(query_rows), by_slot(key_rows), by_slot(value_rows)
    pairs = jnp.concatenate([query, key], axis=3)
    folded = jnp.concatenate([value[:, :, : rows_here // 2], value[:, :, rows_here // 2 :]], axis=3)
    rates = step_rates.T
    high = rates.astype(bf16)
    rest = rates - high.astype(f32)
    middle = rest.astype(bf16)
    low = (rest - middle.astype(f32)).astype(bf16)
    rate_rows = jnp.stack([high, middle, low], axis=1)
    rate_rows = jnp.concatenate([rate_rows, jnp.zeros((heads_local, 5, token_block), bf16)], axis=1)
    rate_rows = jnp.broadcast_to(rate_rows[:, None], (heads_local, head_size, 8, token_block))
    blocks = jnp.concatenate([pairs, folded, rate_rows], axis=2)
    spare = jnp.zeros((half_seq - heads_local,) + blocks.shape[1:], bf16)
    blocks = jnp.concatenate([blocks, spare], axis=0)
    return blocks.reshape((half_seq * head_size,) + blocks.shape[2:])


def local(head_size, seq_size, query_rows, key_rows, value_rows, gate_rows, step_rates, first_weight,
          first_bias, second_weight, second_bias, norm_gain, norm_shift):
    rows_here = query_rows.shape[0]
    heads_local = step_rates.shape[1]
    token_block = step_rates.shape[0]
    half_seq = seq_size // 2
    group = half_seq * head_size
    half_tokens = group * rows_here
    total = half_tokens // MINI
    seq_at = lax.axis_index("seq")
    half = seq_at // half_seq
    slot = jnp.minimum(seq_at % half_seq, heads_local - 1)
    group_at = lax.axis_index("head")
    halves = [
        [s * head_size + h for s in range(k * half_seq, (k + 1) * half_seq) for h in range(head_size)]
        for k in range(2)
    ]

    def exchange(blocks):
        return lax.all_to_all(blocks, ("seq", "head"), 0, 0, axis_index_groups=halves)

    block_rows = rows_here + rows_here // 2 + 8
    kernels_fit = rows_here % 32 == 0 and token_block == 2 * D_HEAD and head_size * heads_local % 2 == 0
    if kernels_fit:
        blocks = pl.pallas_call(
            functools.partial(pack_kernel, head_size, heads_local),
            out_shape=jax.ShapeDtypeStruct((group, block_rows, 2 * D_HEAD), bf16),
            in_specs=[pl.BlockSpec(memory_space=pltpu.HBM)] * 4,
            out_specs=pl.BlockSpec(memory_space=pltpu.HBM),
            scratch_shapes=[
                pltpu.VMEM(query_rows.shape, bf16),
                pltpu.VMEM(key_rows.shape, bf16),
                pltpu.VMEM(value_rows.shape, bf16),
                pltpu.VMEM((heads_local, token_block), f32),
                pltpu.VMEM((group, block_rows, 2 * D_HEAD), bf16),
                pltpu.SemaphoreType.DMA((4,)),
                pltpu.SemaphoreType.DMA((half_seq,)),
            ],
            compiler_params=pltpu.CompilerParams(vmem_limit_bytes=60 * 2**20),
        )(query_rows, key_rows, value_rows, step_rates.T)
    else:
        blocks = pack_plain(head_size, half_seq, query_rows, key_rows, value_rows, step_rates)
    got = exchange(blocks)

    qk_all = got[:, :rows_here].reshape(half_tokens, 2 * D_HEAD)
    got_value = got[:, rows_here : rows_here + rows_here // 2]
    short = total <= CHUNK
    fold = rows_here // 2 if kernels_fit and short else None
    v_all = got_value
    if fold is None:
        v_all = jnp.stack([got_value[..., :D_HEAD], got_value[..., D_HEAD:]], axis=1).reshape(half_tokens, D_HEAD)
    got_rate = got[:, rows_here + rows_here // 2 :].reshape(half_seq, head_size, 8, token_block)
    got_rate = lax.dynamic_index_in_dim(got_rate, group_at, 1, keepdims=False).astype(f32)
    r_all = (got_rate[:, 0] + got_rate[:, 1] + got_rate[:, 2]).reshape(half_seq, 1, 2 * MINI)

    def pick(array_in):
        return lax.dynamic_index_in_dim(array_in, slot, 0, keepdims=False)

    params = (
        pick(first_weight),
        pick(first_bias)[None],
        pick(second_weight).T,
        pick(second_bias)[None],
        pick(norm_gain)[None],
        pick(norm_shift)[None],
    )
    ahead = half.astype(jnp.int32).reshape(1)
    shape = jax.ShapeDtypeStruct
    outs = [shape((half_tokens, D_HEAD), f32), shape((2 * D_HEAD + 8, INNER), bf16)]
    if short:
        outs += [
            shape((2 * MINI, INNER), bf16),
            shape((2 * MINI, INNER), bf16),
            shape((2 * MINI, INNER), bf16),
            shape((2 * MINI, D_HEAD), bf16),
            shape((D_HEAD, INNER), f32),
            shape((1, D_HEAD), f32),
        ]
    tokens = (ahead, qk_all, v_all, r_all)
    y_first, delta, *left = call_phase(functools.partial(first_phase, total), outs, not short, *tokens, *params)
    route = [(s, (s + half_seq) % seq_size) for s in range(seq_size)]
    delta = lax.ppermute(delta, "seq", route)
    extra = []
    if short:
        outs = [
            shape((2 * MINI, D_HEAD), f32),
            shape((MINI, INNER), f32),
            shape((total, 3 * MINI + 16, 2 * D_HEAD), bf16),
            shape((total, 3 * MINI + 16, D_HEAD), bf16),
            shape((total, MINI, D_HEAD), f32),
            shape((total, MINI, D_HEAD), f32),
            shape((total, 1, MINI), f32),
        ]
        extra = call_phase(functools.partial(between_phases, total), outs, False, *tokens, *params[:2], *params[4:], *left)
    (summed,) = call_phase(
        functools.partial(second_phase, total, fold),
        [shape((half_tokens, D_HEAD) if fold is None else (group, fold, 2 * D_HEAD), bf16)],
        not short, *tokens, *params, y_first, delta, *extra,
    )
    if fold is None:
        summed = summed.reshape(group, 2, rows_here // 2, D_HEAD)
        summed = jnp.concatenate([summed[:, 0], summed[:, 1]], axis=2)
    back = exchange(summed)
    if kernels_fit:
        return pl.pallas_call(
            functools.partial(join_kernel, head_size, heads_local),
            out_shape=jax.ShapeDtypeStruct(gate_rows.shape, bf16),
            compiler_params=pltpu.CompilerParams(vmem_limit_bytes=8 * 2**20),
        )(back, gate_rows)
    back = back.reshape(half_seq, head_size, rows_here // 2, 2, D_HEAD)[:heads_local]
    back = back.transpose(3, 2, 1, 0, 4).reshape(rows_here, head_size * heads_local * D_HEAD)
    return (gate_rows.astype(f32) * back.astype(f32)).astype(bf16)


def solution(mesh):
    tokens = P(("seq", "head"), None)
    in_specs = (
        tokens,
        tokens,
        tokens,
        tokens,
        P("seq", "head"),
        P("head", None, None),
        P("head", None),
        P("head", None, None),
        P("head", None),
        P("head", None),
        P("head", None),
    )
    body = functools.partial(local, mesh.shape["head"], mesh.shape["seq"])
    return jax.shard_map(body, mesh=mesh, in_specs=in_specs, out_specs=tokens, check_vma=False)
```

```python
import functools

import jax
import jax.numpy as jnp
from jax import lax
from jax.experimental import pallas as pl
from jax.experimental.pallas import tpu as pltpu
from jax.sharding import PartitionSpec as P

D_HEAD = 64
INNER = 256
MINI = 64
CHUNK = 8

eps_norm = 1e-06
root_factor = 0.7978845608028654
cube_factor = 0.044715
f32 = jnp.float32
bf16 = jnp.bfloat16


def mm(left, right):
    return lax.dot_general(left, right, (((1,), (0,)), ((), ())), preferred_element_type=f32)


def mm_turned(left, right):
    return lax.dot_general(left, right, (((1,), (1,)), ((), ())), preferred_element_type=f32)


def gelu_and_slope(values):
    square = values * values
    tanh_term = jnp.tanh(values * (root_factor + root_factor * cube_factor * square))
    half = 0.5 + 0.5 * tanh_term
    act = values * half
    inner = root_factor + 3.0 * root_factor * cube_factor * square
    return act, half + act * (1.0 - tanh_term) * inner


def gelu(values):
    tanh_term = jnp.tanh(values * (root_factor + root_factor * cube_factor * (values * values)))
    return values * (0.5 + 0.5 * tanh_term)


def row_mean(values):
    return jnp.mean(values, axis=1, keepdims=True)


def tokens_of(first_step, steps, total, backward, qk_ref, v_ref, r_ref):
    lower = lax.broadcasted_iota(jnp.int32, (MINI, 2 * D_HEAD), 1) < D_HEAD
    places, pairs, queries, keys, values, rates = [], [], [], [], [], []
    for step in range(first_step, first_step + steps) if isinstance(first_step, int) else range(steps):
        at = step if isinstance(first_step, int) else first_step + step
        spot = jnp.where(backward == 0, at, total - 1 - at)
        spots = pl.ds(pl.multiple_of(spot * MINI, MINI), MINI)
        pair = qk_ref[spots, :]
        turned = jnp.concatenate([pair[:, D_HEAD:], pair[:, :D_HEAD]], axis=1)
        places.append(spot)
        pairs.append(pair)
        queries.append(jnp.where(lower, pair, turned))
        keys.append(jnp.where(lower, turned, pair))
        rate = r_ref[lax.div(spot, 2)]
        rate_turned = jnp.concatenate([rate[:, MINI:], rate[:, :MINI]], axis=1)
        rates.append(jnp.where(lax.rem(spot, 2) == 0, rate, rate_turned)[:, :MINI])
        if v_ref is None:
            continue
        if len(v_ref.shape) == 2:
            value = v_ref[spots, :]
            values.append(jnp.concatenate([value, value], axis=1))
            continue
        halves = []
        for block in range(MINI // (2 * v_ref.shape[1])):
            folded = v_ref[spot * (MINI // (2 * v_ref.shape[1])) + block]
            halves += [folded, jnp.concatenate([folded[:, D_HEAD:], folded[:, :D_HEAD]], axis=1)]
        values.append(jnp.concatenate(halves, axis=0))
    return places, pairs, queries, keys, values, rates


def columns_of(gain, shift):
    both = jnp.concatenate([jnp.broadcast_to(gain, (MINI, D_HEAD)), jnp.broadcast_to(shift, (MINI, D_HEAD))], axis=1).T
    return both[:D_HEAD], both[D_HEAD:]


def order_of(backward, shape):
    ahead = lax.broadcasted_iota(jnp.int32, shape, 0) - lax.broadcasted_iota(jnp.int32, shape, 1)
    return jnp.where(backward == 0, ahead, -ahead)


def prepare(one, backward, tokens, gain, shift, columns):
    _, _, queries, keys, values, rates = tokens
    gain_column, shift_column = columns
    steps = len(keys)
    two = min(one + 1, steps - 1)
    lower = lax.broadcasted_iota(jnp.int32, (MINI, 2 * D_HEAD), 1) < D_HEAD
    none = jnp.zeros((MINI, 2 * D_HEAD), bf16)
    seen = order_of(backward, (MINI, MINI)) >= 0
    nexts = [keys[min(step + 1, steps - 1)] for step in (one, two)]
    probes = jnp.concatenate(
        [jnp.where(lower, nexts[0], nexts[1]), jnp.where(lower, queries[one], queries[two])], axis=0
    )
    met = jnp.concatenate([jnp.where(lower, keys[one], none), none, jnp.where(lower, none, keys[two]), none], axis=0)
    attend = mm_turned(probes, met) + 1.0
    made = []
    for at, step in enumerate((one, two)):
        rate = rates[step]
        here = attend[:, 2 * at * MINI : (2 * at + 1) * MINI] * rate
        value, key = values[step].astype(f32), keys[step].astype(f32)
        both = jnp.where(lower, value, key).T
        value_turned, key_turned = both[:D_HEAD], both[D_HEAD:]
        mixer = jnp.concatenate(
            [
                (-here[:MINI]).astype(bf16),
                jnp.where(seen, -here[MINI:], 0.0).astype(bf16),
                (key_turned * -rate).astype(bf16),
                jnp.broadcast_to(-rate, (16, MINI)).astype(bf16),
            ],
            axis=0,
        )
        plain = jnp.concatenate([nexts[at], queries[step], none, none[:16]], axis=0)
        pull = gain * (shift - value[:, :D_HEAD] + key[:, :D_HEAD])
        pull_turned = gain_column * (shift_column - value_turned + key_turned)
        pull_row = jnp.mean(pull_turned, axis=0, keepdims=True)
        made.append((plain, mixer, pull, pull_turned, pull_row))
    return made


def finish(waiting, second_turned, bias_two, backward, gain, shift, emit):
    count = len(waiting)
    shape = (count * MINI, count * MINI)
    rows, columns = (lax.broadcasted_iota(jnp.int32, shape, dim) // MINI for dim in range(2))
    later = jnp.logical_and(rows == columns, order_of(backward, shape) < 0)
    unseen = jnp.logical_or(rows < columns, later)
    dual, dual_low, acts, weighted = (jnp.concatenate([one[at] for one in waiting], axis=0) for at in (1, 2, 3, 4))
    second_high = second_turned.astype(bf16)
    hidden = mm(jnp.where(unseen, mm_turned(dual, acts) + 1.0, 0.0).astype(bf16), weighted)
    plain = mm_turned(jnp.concatenate([dual, dual_low], axis=0), second_high)
    dual_two = plain[: count * MINI] + plain[count * MINI :] + bias_two + hidden
    second_low = (second_turned - second_high.astype(f32)).astype(bf16)
    dual_two = dual_two + mm_turned(dual, second_low)
    spread = lax.rsqrt(row_mean(dual_two * dual_two) + eps_norm)
    found = gain * (dual_two * spread) + shift
    for at, one in enumerate(waiting):
        emit(one[0], found[at * MINI : (at + 1) * MINI])


def run_chunk(backward, tokens, state, gain, shift, emit, ready=None, keep_last=False, ends=False):
    weight_one, bias_one, second_turned, bias_two = state
    places, pairs, queries, keys, values, rates = tokens
    steps = len(places)
    gain_square = gain * gain
    columns = columns_of(gain, shift)
    square_column = columns[0] * columns[0]
    blank = jnp.zeros((D_HEAD, INNER), bf16)
    first_high = weight_one.astype(bf16)
    first_low = (weight_one - first_high.astype(f32)).astype(bf16)
    act, slope = gelu_and_slope(
        mm(
            jnp.concatenate([pairs[0], pairs[0]], axis=1),
            jnp.concatenate([blank, first_high, blank, first_low], axis=0),
        )
        + bias_one
    )
    act_high = act.astype(bf16)
    bias_column = jnp.broadcast_to(bias_two, (MINI, D_HEAD)).T
    made = [] if ready is not None else prepare(0, backward, tokens, gain, shift, columns)
    waiting = []
    for step in range(steps):
        plain, mixer, pull, pull_turned, pull_row = made[step] if ready is None else ready(step)
        rate = rates[step]
        second_high = second_turned.astype(bf16)
        second_low = (second_turned - second_high.astype(f32)).astype(bf16)
        centred = mm_turned(act_high, second_high) + bias_two
        turned = mm_turned(jnp.concatenate([second_high, second_low], axis=0), act_high)
        turned = turned[:D_HEAD] + turned[D_HEAD:] + bias_column
        second_before, bias_before = second_turned, bias_two
        scaled = gain_square * centred
        both = [part.astype(bf16) for part in (centred, scaled)]
        woven = [part[at : at + 16] for at in range(0, MINI, 16) for part in both]
        back = mm(jnp.concatenate([pull.astype(bf16)] + woven, axis=0), second_high)
        back_plain = jnp.concatenate([back[MINI + at : MINI + at + 16] for at in range(0, 2 * MINI, 32)], axis=0)
        back_scaled = jnp.concatenate([back[MINI + at : MINI + at + 16] for at in range(16, 2 * MINI, 32)], axis=0)
        first_high = weight_one.astype(bf16)
        first_low = (weight_one - first_high.astype(f32)).astype(bf16)
        if ready is None and step % 2 == 0 and step + 2 < steps:
            made = made + prepare(step + 2, backward, tokens, gain, shift, columns)
        inverse = lax.rsqrt(row_mean(centred * centred) + eps_norm)
        mean_an = inverse * (inverse * row_mean(scaled * centred) + row_mean(pull * centred))
        front = inverse * slope
        grad_one = (front * inverse) * (back_scaled - mean_an * back_plain) + front * back[:MINI]
        grad_one = grad_one.astype(bf16)
        scaled_turned = square_column * turned
        inverse_row = lax.rsqrt(jnp.mean(turned * turned, axis=0, keepdims=True) + eps_norm)
        mean_a_row = inverse_row * jnp.mean(scaled_turned, axis=0, keepdims=True) + pull_row
        mean_an_row = inverse_row * (
            inverse_row * jnp.mean(scaled_turned * turned, axis=0, keepdims=True)
            + jnp.mean(pull_turned * turned, axis=0, keepdims=True)
        )
        weighted_turned = (rate * inverse_row) * (
            (square_column - mean_an_row) * (inverse_row * turned) + (pull_turned - mean_a_row)
        )
        weighted_high = weighted_turned.astype(bf16)
        weighted_low = (weighted_turned - weighted_high.astype(f32)).astype(bf16)
        change = mm(jnp.concatenate([weighted_high, weighted_low], axis=0), act_high)
        second_turned = second_turned - (change[:D_HEAD] + change[D_HEAD:])
        last = step + 1 == steps
        first = MINI if last else 0
        rows = slice(first, 2 * MINI if last and ends else None)
        mixed = mm(
            jnp.concatenate([plain[rows], mixer[rows]], axis=1),
            jnp.concatenate([first_high, first_low, grad_one], axis=0),
        )
        mixed_query = mixed[MINI - first : 2 * MINI - first]
        weighted = weighted_turned.T
        bias_column = bias_column - jnp.sum(weighted_turned, axis=1, keepdims=True)
        bias_two = bias_two - jnp.sum(weighted, axis=0, keepdims=True)
        if len(waiting) == (2 if ready is None else 3):
            finish(waiting, second_before, bias_before, backward, gain, shift, emit)
            waiting = []
        dual = gelu(mixed_query + bias_one)
        dual_high = dual.astype(bf16)
        dual_low = (dual - dual_high.astype(f32)).astype(bf16)
        waiting.append((places[step], dual_high, dual_low, act_high, weighted.astype(bf16)))
        if not last:
            act, slope = gelu_and_slope(mixed[:MINI] + bias_one)
            act_high = act.astype(bf16)
        if last and ends:
            continue
        weight_one = weight_one + mixed[2 * MINI - first : 3 * MINI - first]
        bias_one = bias_one + mixed[3 * MINI - first : 3 * MINI - first + 1]
    if not keep_last:
        finish(waiting, second_turned, bias_two, backward, gain, shift, emit)
    return (weight_one, bias_one, second_turned, bias_two), waiting


def run_chunks(total, backward, qk_ref, v_ref, r_ref, state_refs, gain, shift, emit):
    assert total % CHUNK == 0

    def body(index, carry):
        tokens = tokens_of(index * CHUNK, CHUNK, total, backward, qk_ref, v_ref, r_ref)
        state, _ = run_chunk(backward, tokens, tuple(ref[...] for ref in state_refs), gain, shift, emit)
        for ref, part in zip(state_refs, state):
            ref[...] = part
        return carry

    lax.fori_loop(0, total // CHUNK, body, 0)
    return tuple(ref[...] for ref in state_refs)


def centre_start(w1_ref, c1_ref, w2t_ref, c2_ref):
    second_turned = w2t_ref[...]
    second_turned = second_turned - jnp.mean(second_turned, axis=0, keepdims=True)
    bias_two = c2_ref[...] - row_mean(c2_ref[...])
    return w1_ref[...], c1_ref[...], second_turned, bias_two


def first_phase(total, dir_ref, qk_ref, v_ref, r_ref, w1_ref, c1_ref, w2t_ref, c2_ref, gain_ref, shift_ref, y_ref,
                delta_ref, *refs):
    backward = dir_ref[0]
    gain, shift = gain_ref[...], shift_ref[...]
    start = centre_start(w1_ref, c1_ref, w2t_ref, c2_ref)

    def emit(spot, rows):
        y_ref[pl.ds(pl.multiple_of(spot * MINI, MINI), MINI), :] = rows

    if total <= CHUNK:
        *kept_refs, second_ref, bias_ref = refs
        tokens = tokens_of(0, total, total, backward, qk_ref, v_ref, r_ref)
        end, waiting = run_chunk(backward, tokens, start, gain, shift, emit, keep_last=True)
        for at, one in enumerate(waiting):
            spots = slice(at * MINI, (at + 1) * MINI)
            for ref, part in zip(kept_refs, one[1:]):
                ref[spots, :] = part
        second_ref[...] = end[2]
        bias_ref[...] = end[3]
    else:
        for ref, part in zip(refs, start):
            ref[...] = part
        end = run_chunks(total, backward, qk_ref, v_ref, r_ref, refs, gain, shift, emit)
    start = centre_start(w1_ref, c1_ref, w2t_ref, c2_ref)
    ends = [part - first for part, first in zip(end, start)]
    wide = jnp.concatenate([ends[3], jnp.zeros((1, INNER - D_HEAD), f32)], axis=1)
    at = lax.broadcasted_iota(jnp.int32, (8, INNER), 0)
    biases = jnp.where(at == 0, ends[1], jnp.where(at == 1, wide, 0.0))
    delta_ref[...] = jnp.concatenate([ends[0], ends[2], biases], axis=0).astype(bf16)


def between_phases(total, dir_ref, qk_ref, v_ref, r_ref, gain_ref, shift_ref, dual_ref, low_ref, act_ref, weighted_ref,
                   second_ref, bias_ref, tail_ref, plain_ref, mixer_ref, pull_ref, turned_ref, row_ref):
    gain, shift = gain_ref[...], shift_ref[...]
    backward = 1 - dir_ref[0]
    tokens = tokens_of(0, total, total, backward, qk_ref, v_ref, r_ref)
    columns = columns_of(gain, shift)
    for one in range(0, total, 2):
        for at, made in enumerate(prepare(one, backward, tokens, gain, shift, columns)):
            for ref, part in zip((plain_ref, mixer_ref, pull_ref, turned_ref, row_ref), made):
                ref[one + at] = part
    waiting = []
    for at in range(2):
        spots = slice(at * MINI, (at + 1) * MINI)
        kept = (ref[spots, :] for ref in (dual_ref, low_ref, act_ref, weighted_ref))
        waiting.append((at, *kept))

    def emit(at, rows):
        tail_ref[at * MINI : (at + 1) * MINI, :] = rows

    finish(waiting, second_ref[...], bias_ref[...], dir_ref[0], gain, shift, emit)


def second_phase(total, fold, dir_ref, qk_ref, v_ref, r_ref, w1_ref, c1_ref, w2t_ref, c2_ref, gain_ref, shift_ref, y_ref,
                 delta_ref, *refs):
    backward = 1 - dir_ref[0]
    gain, shift = gain_ref[...], shift_ref[...]
    delta = delta_ref[...].astype(f32)
    deltas = (
        delta[:D_HEAD],
        delta[2 * D_HEAD : 2 * D_HEAD + 1],
        delta[D_HEAD : 2 * D_HEAD],
        delta[2 * D_HEAD + 1 : 2 * D_HEAD + 2, :D_HEAD],
    )
    start = centre_start(w1_ref, c1_ref, w2t_ref, c2_ref)
    state = tuple(part + delta for part, delta in zip(start, deltas))
    if total <= CHUNK:
        tail_ref, *ready_refs, out_ref = refs
        tokens = tokens_of(0, total, total, backward, qk_ref, None, r_ref)
        done = []

        def emit(spot, rows):
            spots = pl.ds(pl.multiple_of(spot * MINI, MINI), MINI)
            step = len(done)
            done.append(step)
            if step < 2:
                first = tail_ref[(1 - step) * MINI : (2 - step) * MINI, :]
            else:
                first = y_ref[spots, :]
            summed = (first + rows).astype(bf16)
            if fold is None:
                out_ref[spots, :] = summed
                return
            for block in range(MINI // (2 * fold)):
                at = block * 2 * fold
                folded = jnp.concatenate([summed[at : at + fold], summed[at + fold : at + 2 * fold]], axis=1)
                out_ref[spot * (MINI // (2 * fold)) + block] = folded

        def ready(step):
            return tuple(ref[step] for ref in ready_refs)

        run_chunk(backward, tokens, state, gain, shift, emit, ready, ends=True)
    else:
        out_ref, *state_refs = refs
        for ref, part in zip(state_refs, state):
            ref[...] = part

        def emit(spot, rows):
            spots = pl.ds(pl.multiple_of(spot * MINI, MINI), MINI)
            out_ref[spots, :] = (y_ref[spots, :] + rows).astype(bf16)

        run_chunks(total, backward, qk_ref, v_ref, r_ref, state_refs, gain, shift, emit)


def pack_kernel(head_size, heads_local, query_hbm, key_hbm, value_hbm, rate_hbm, out_hbm, query_ref, key_ref,
                value_ref, rate_ref, block_ref, arrived, left):
    copies = [
        pltpu.make_async_copy(source, target, arrived.at[at])
        for at, (source, target) in enumerate(
            [(query_hbm, query_ref), (key_hbm, key_ref), (value_hbm, value_ref), (rate_hbm, rate_ref)]
        )
    ]
    for copy in copies:
        copy.start()
    leaving = []

    def leave(s):
        blocks = pl.ds(s * head_size, head_size)
        leaving.append(pltpu.make_async_copy(block_ref.at[blocks], out_hbm.at[blocks], left.at[s]))
        leaving[-1].start()

    for s in range(heads_local, out_hbm.shape[0] // head_size):
        for h in range(head_size):
            block_ref[s * head_size + h] = jnp.zeros(out_hbm.shape[1:], bf16)
        leave(s)
    for copy in copies:
        copy.wait()
    fold = query_ref.shape[0] // 2
    row_at = lax.broadcasted_iota(jnp.int32, (8, rate_ref.shape[1]), 0)
    for s in range(heads_local):
        rate = rate_ref[s : s + 1, :]
        high = rate.astype(bf16).astype(f32)
        middle = (rate - high).astype(bf16).astype(f32)
        low = rate - high - middle
        rate_rows = jnp.where(row_at == 0, high, jnp.where(row_at == 1, middle, jnp.where(row_at == 2, low, 0.0)))
        for h in range(head_size):
            at = (h * heads_local + s) * D_HEAD
            value = value_ref[:, at : at + D_HEAD]
            pair = jnp.concatenate([query_ref[:, at : at + D_HEAD], key_ref[:, at : at + D_HEAD]], axis=1)
            folded = jnp.concatenate([value[:fold], value[fold:]], axis=1)
            block_ref[s * head_size + h] = jnp.concatenate([pair, folded, rate_rows.astype(bf16)], axis=0)
        leave(s)
    for copy in leaving:
        copy.wait()


def join_kernel(head_size, heads_local, back_ref, gate_ref, out_ref):
    fold = back_ref.shape[1]
    for pair_at in range(head_size * heads_local // 2):
        blocks = []
        for head in (2 * pair_at, 2 * pair_at + 1):
            blocks.append(back_ref[(head % heads_local) * head_size + head // heads_local])
        columns = slice(pair_at * 2 * D_HEAD, (pair_at + 1) * 2 * D_HEAD)
        for part in range(2):
            lanes = slice(part * D_HEAD, (part + 1) * D_HEAD)
            ttt = jnp.concatenate([blocks[0][:, lanes], blocks[1][:, lanes]], axis=1)
            spots = slice(part * fold, (part + 1) * fold)
            gated = gate_ref[spots, columns].astype(f32) * ttt.astype(f32)
            out_ref[spots, columns] = gated.astype(bf16)


def call_phase(kernel, outs, keeps_state, *operands):
    in_vmem = pl.BlockSpec(memory_space=pltpu.VMEM)
    state = [(D_HEAD, INNER), (1, INNER), (D_HEAD, INNER), (1, D_HEAD)] if keeps_state else []
    return pl.pallas_call(
        kernel,
        out_shape=outs,
        in_specs=[pl.BlockSpec(memory_space=pltpu.SMEM)] + [in_vmem] * (len(operands) - 1),
        out_specs=[in_vmem] * len(outs),
        scratch_shapes=[pltpu.VMEM(shape, f32) for shape in state],
        compiler_params=pltpu.CompilerParams(vmem_limit_bytes=24 * 2**20),
        cost_estimate=pl.CostEstimate(flops=10**8, bytes_accessed=10**6, transcendentals=10**5),
    )(*operands)


def pack_plain(head_size, half_seq, query_rows, key_rows, value_rows, step_rates):
    rows_here = query_rows.shape[0]
    token_block, heads_local = step_rates.shape

    def by_slot(rows):
        return rows.reshape(rows_here, head_size, heads_local, D_HEAD).transpose(2, 1, 0, 3)

    query, key, value = by_slot(query_rows), by_slot(key_rows), by_slot(value_rows)
    pairs = jnp.concatenate([query, key], axis=3)
    folded = jnp.concatenate([value[:, :, : rows_here // 2], value[:, :, rows_here // 2 :]], axis=3)
    rates = step_rates.T
    high = rates.astype(bf16)
    rest = rates - high.astype(f32)
    middle = rest.astype(bf16)
    low = (rest - middle.astype(f32)).astype(bf16)
    rate_rows = jnp.stack([high, middle, low], axis=1)
    rate_rows = jnp.concatenate([rate_rows, jnp.zeros((heads_local, 5, token_block), bf16)], axis=1)
    rate_rows = jnp.broadcast_to(rate_rows[:, None], (heads_local, head_size, 8, token_block))
    blocks = jnp.concatenate([pairs, folded, rate_rows], axis=2)
    spare = jnp.zeros((half_seq - heads_local,) + blocks.shape[1:], bf16)
    blocks = jnp.concatenate([blocks, spare], axis=0)
    return blocks.reshape((half_seq * head_size,) + blocks.shape[2:])


def local(head_size, seq_size, query_rows, key_rows, value_rows, gate_rows, step_rates, first_weight,
          first_bias, second_weight, second_bias, norm_gain, norm_shift):
    rows_here = query_rows.shape[0]
    heads_local = step_rates.shape[1]
    token_block = step_rates.shape[0]
    half_seq = seq_size // 2
    group = half_seq * head_size
    half_tokens = group * rows_here
    total = half_tokens // MINI
    seq_at = lax.axis_index("seq")
    half = seq_at // half_seq
    slot = jnp.minimum(seq_at % half_seq, heads_local - 1)
    group_at = lax.axis_index("head")
    halves = [
        [s * head_size + h for s in range(k * half_seq, (k + 1) * half_seq) for h in range(head_size)]
        for k in range(2)
    ]

    def exchange(blocks):
        return lax.all_to_all(blocks, ("seq", "head"), 0, 0, axis_index_groups=halves)

    block_rows = rows_here + rows_here // 2 + 8
    kernels_fit = rows_here % 32 == 0 and token_block == 2 * D_HEAD and head_size * heads_local % 2 == 0
    if kernels_fit:
        blocks = pl.pallas_call(
            functools.partial(pack_kernel, head_size, heads_local),
            out_shape=jax.ShapeDtypeStruct((group, block_rows, 2 * D_HEAD), bf16),
            in_specs=[pl.BlockSpec(memory_space=pltpu.HBM)] * 4,
            out_specs=pl.BlockSpec(memory_space=pltpu.HBM),
            scratch_shapes=[
                pltpu.VMEM(query_rows.shape, bf16),
                pltpu.VMEM(key_rows.shape, bf16),
                pltpu.VMEM(value_rows.shape, bf16),
                pltpu.VMEM((heads_local, token_block), f32),
                pltpu.VMEM((group, block_rows, 2 * D_HEAD), bf16),
                pltpu.SemaphoreType.DMA((4,)),
                pltpu.SemaphoreType.DMA((half_seq,)),
            ],
            compiler_params=pltpu.CompilerParams(vmem_limit_bytes=60 * 2**20),
        )(query_rows, key_rows, value_rows, step_rates.T)
    else:
        blocks = pack_plain(head_size, half_seq, query_rows, key_rows, value_rows, step_rates)
    got = exchange(blocks)

    qk_all = got[:, :rows_here].reshape(half_tokens, 2 * D_HEAD)
    got_value = got[:, rows_here : rows_here + rows_here // 2]
    short = total <= CHUNK
    fold = rows_here // 2 if kernels_fit and short else None
    v_all = got_value
    if fold is None:
        v_all = jnp.stack([got_value[..., :D_HEAD], got_value[..., D_HEAD:]], axis=1).reshape(half_tokens, D_HEAD)
    got_rate = got[:, rows_here + rows_here // 2 :].reshape(half_seq, head_size, 8, token_block)
    got_rate = lax.dynamic_index_in_dim(got_rate, group_at, 1, keepdims=False).astype(f32)
    r_all = (got_rate[:, 0] + got_rate[:, 1] + got_rate[:, 2]).reshape(half_seq, 1, 2 * MINI)

    def pick(array_in):
        return lax.dynamic_index_in_dim(array_in, slot, 0, keepdims=False)

    params = (
        pick(first_weight),
        pick(first_bias)[None],
        pick(second_weight).T,
        pick(second_bias)[None],
        pick(norm_gain)[None],
        pick(norm_shift)[None],
    )
    ahead = half.astype(jnp.int32).reshape(1)
    shape = jax.ShapeDtypeStruct
    outs = [shape((half_tokens, D_HEAD), f32), shape((2 * D_HEAD + 8, INNER), bf16)]
    if short:
        outs += [
            shape((2 * MINI, INNER), bf16),
            shape((2 * MINI, INNER), bf16),
            shape((2 * MINI, INNER), bf16),
            shape((2 * MINI, D_HEAD), bf16),
            shape((D_HEAD, INNER), f32),
            shape((1, D_HEAD), f32),
        ]
    tokens = (ahead, qk_all, v_all, r_all)
    y_first, delta, *left = call_phase(functools.partial(first_phase, total), outs, not short, *tokens, *params)
    route = [(s, (s + half_seq) % seq_size) for s in range(seq_size)]
    delta = lax.ppermute(delta, "seq", route)
    extra = []
    if short:
        outs = [
            shape((2 * MINI, D_HEAD), f32),
            shape((total, 3 * MINI + 16, 2 * D_HEAD), bf16),
            shape((total, 3 * MINI + 16, D_HEAD), bf16),
            shape((total, MINI, D_HEAD), f32),
            shape((total, MINI, D_HEAD), f32),
            shape((total, 1, MINI), f32),
        ]
        extra = call_phase(functools.partial(between_phases, total), outs, False, *tokens, *params[4:], *left)
    (summed,) = call_phase(
        functools.partial(second_phase, total, fold),
        [shape((half_tokens, D_HEAD) if fold is None else (group, fold, 2 * D_HEAD), bf16)],
        not short, *tokens, *params, y_first, delta, *extra,
    )
    if fold is None:
        summed = summed.reshape(group, 2, rows_here // 2, D_HEAD)
        summed = jnp.concatenate([summed[:, 0], summed[:, 1]], axis=2)
    back = exchange(summed)
    if kernels_fit:
        return pl.pallas_call(
            functools.partial(join_kernel, head_size, heads_local),
            out_shape=jax.ShapeDtypeStruct(gate_rows.shape, bf16),
            compiler_params=pltpu.CompilerParams(vmem_limit_bytes=8 * 2**20),
        )(back, gate_rows)
    back = back.reshape(half_seq, head_size, rows_here // 2, 2, D_HEAD)[:heads_local]
    back = back.transpose(3, 2, 1, 0, 4).reshape(rows_here, head_size * heads_local * D_HEAD)
    return (gate_rows.astype(f32) * back.astype(f32)).astype(bf16)


def solution(mesh):
    tokens = P(("seq", "head"), None)
    in_specs = (
        tokens,
        tokens,
        tokens,
        tokens,
        P("seq", "head"),
        P("head", None, None),
        P("head", None),
        P("head", None, None),
        P("head", None),
        P("head", None),
        P("head", None),
    )
    body = functools.partial(local, mesh.shape["head"], mesh.shape["seq"])
    return jax.shard_map(body, mesh=mesh, in_specs=in_specs, out_specs=tokens, check_vma=False)
```
